512 devices in a mesh: shard: 128 (over z, y, core), rep: 4 (over x).
Axes of the slice: x: 4, y: 4, z: 16, core: 2. Of those that a mesh axis runs over, the one named last changes fastest.
Arguments:
- queries: bfloat16 [4, 128, 9, 3840], P('rep', 'shard'), may hold values from -2.2 to 2.2
- corpus: bfloat16 [256, 32, 9, 3840], P('shard'), may hold values from -2.2 to 2.2
- cand_shard: int32 [16, 256], replicated, may hold values from 0 to 127, as said below
- cand_clip: int32 [16, 256], replicated, may hold values from 0 to 1
- cand_count: int32 [16], replicated, may hold values from 1 to 256, as said below
- first_kernel: bfloat16 [3, 3, 1, 32], replicated, may hold values from -3 to 3
- first_bias: float32 [32], replicated, may hold values from -3 to 3
- second_kernel: bfloat16 [3, 3, 32, 64], replicated, may hold values from -0.5 to 0.5
- second_bias: float32 [64], replicated, may hold values from -3 to 3
- third_kernel: bfloat16 [3, 3, 64, 128], replicated, may hold values from -0.375 to 0.375
- third_bias: float32 [128], replicated, may hold values from -3 to 3
- score_weight: bfloat16 [128], replicated, may hold values from -0.5 to 0.5
- score_bias: float32 [1], replicated, may hold values from -3 to 3
Outputs:
- scores: float32 [16, 256], P('rep', 'shard')
The draws below stay inside these ranges and needn't reach their ends.
Inputs may be any that keep to these rules, and one draw needn't show every extreme that they name: `cand_shard`: query q belongs to rep group q // 4. Over the first cand_count[q] slots of every query, at most 8 candidates of one rep group's queries lie on one shard, and at most 20 of all queries lie on one shard; both bounds are reached in every draw. Slots from cand_count[q] on are unused. `cand_count`: some query of every rep group has all 256 slots in use.
All inputs are finite; a program needn't handle non-finite values.
Results may differ from the reference program's by a relative error of at most 0.009.
Values may be sent and summed in bfloat16 or wider, within the bound.
No kernel may reach another device: no remote copies, remote signals or barrier semaphores. Data moves between devices by JAX's collectives and lax.ppermute only.
A program may use at most 128 MiB of HBM per device.

```python
import jax
import jax.numpy as jnp
from jax import lax

C = 3840
R = 9
F = 32
CH1 = 32
CH2 = 64
CH3 = 128
Q = 16
CLIP_DEV = 2
CAP = 8
LOW = 4
K = 256
FB = 8
CLIPS = 256
N_SHARD = 128
N_REP = 4


def candidate_plan(key):
    keys = jax.random.split(key, 8)
    shard_count = N_SHARD
    rep_count = N_REP
    group_size = Q // N_REP
    slot_total = shard_count * CAP
    offset = jax.random.randint(keys[0], (), 0, rep_count)
    busiest = jax.random.randint(keys[1], (), 0, shard_count)
    shard_ids = jnp.arange(shard_count, dtype=jnp.int32)[:, None]
    rep_ids = jnp.arange(rep_count, dtype=jnp.int32)[None, :]
    hot_rep = (shard_ids + offset) % rep_count == rep_ids
    lower = jax.random.randint(keys[2], (shard_count, rep_count), 1, LOW + 1)
    lower = jnp.where(shard_ids == busiest, LOW, lower)
    loads = jnp.where(hot_rep, CAP, lower).astype(jnp.int32)
    slot_ids = jnp.arange(CAP, dtype=jnp.int32)
    used = slot_ids[None, None, :] < loads[:, :, None]
    used = jnp.transpose(used, (1, 0, 2)).reshape(rep_count, slot_total)
    priority = jax.random.randint(keys[3], (rep_count, slot_total), 0, slot_total) * slot_total + jnp.arange(slot_total, dtype=jnp.int32)[None, :]
    priority = jnp.where(used, priority, priority + slot_total * slot_total)
    order = jnp.argsort(priority, axis=1).astype(jnp.int32)
    totals = loads.sum(axis=0)
    remain = totals - K
    third_part = remain // 3
    eighth_part = remain // 8
    jitter = jax.random.randint(keys[4], (rep_count, 2), -eighth_part[:, None], eighth_part[:, None] + 1)
    count_one = third_part + jitter[:, 0]
    count_two = third_part + jitter[:, 1]
    count_three = remain - count_one - count_two
    role_counts = jnp.stack([jnp.full((rep_count,), K, jnp.int32), count_one, count_two, count_three], axis=1).astype(jnp.int32)
    role_keys = jax.random.randint(keys[5], (rep_count, group_size), 0, 64) * group_size + jnp.arange(group_size, dtype=jnp.int32)[None, :]
    roles = jnp.argsort(role_keys, axis=1).astype(jnp.int32)
    counts = jnp.take_along_axis(role_counts, roles, axis=1)
    starts = jnp.cumsum(counts, axis=1) - counts
    cand_pos = jnp.arange(K, dtype=jnp.int32)
    position = jnp.minimum(starts[:, :, None] + cand_pos[None, None, :], slot_total - 1)
    valid = cand_pos[None, None, :] < counts[:, :, None]
    picked = jnp.take_along_axis(order, position.reshape(rep_count, group_size * K), axis=1).reshape(rep_count, group_size, K)
    filler = jax.random.randint(keys[6], (rep_count, group_size, K), 0, shard_count)
    shards = jnp.where(valid, picked // CAP, filler).reshape(Q, K).astype(jnp.int32)
    clips = jax.random.randint(keys[7], (Q, K), 0, CLIP_DEV).astype(jnp.int32)
    return (shards, clips, counts.reshape(Q).astype(jnp.int32))


def draw_cand_shard(key, part):
    plan_out = candidate_plan(key)
    return plan_out[0]


def draw_cand_clip(key, part):
    plan_out = candidate_plan(key)
    return plan_out[1]


def draw_cand_count(key, part):
    plan_out = candidate_plan(key)
    return plan_out[2]


def base_entries(key, shape):
    values = jnp.clip(jax.random.normal(key, shape, jnp.float32), -6.0, 6.0)
    return values * 0.127


def log_spread(key, shape, low_value, high_value):
    unit = jax.random.uniform(key, shape, jnp.float32, 0.0, 1.0)
    return jnp.exp(jnp.log(low_value) + unit * (jnp.log(high_value) - jnp.log(low_value)))


def draw_queries(key, part):
    key = jax.random.fold_in(key, 11)
    keys = jax.random.split(key, 3)
    values = base_entries(keys[0], (N_REP, Q * FB, R, C))
    clip_scale = log_spread(keys[1], (1, Q, 1, 1, 1), 0.5, 2.0)
    frame_scale = log_spread(keys[2], (N_REP, Q, FB, 1, 1), 0.7, 1.4)
    values = values.reshape(N_REP, Q, FB, R, C) * clip_scale * frame_scale
    return values.reshape(N_REP, Q * FB, R, C).astype(jnp.bfloat16)


def draw_corpus(key, part):
    key = jax.random.fold_in(key, 23)
    keys = jax.random.split(key, 3)
    values = base_entries(keys[0], (CLIPS, F, R, C))
    clip_scale = log_spread(keys[1], (CLIPS, 1, 1, 1), 0.5, 2.0)
    frame_scale = log_spread(keys[2], (CLIPS, F, 1, 1), 0.7, 1.4)
    return (values * clip_scale * frame_scale).astype(jnp.bfloat16)


def centred(key, dims, scale, reach, kind=jnp.bfloat16):
    return jnp.clip(scale * jax.random.normal(key, dims, jnp.float32), -reach, reach).astype(kind)


def setup_inputs(seed: int = 0) -> dict:
    splits = jax.random.split(jax.random.key(seed), 14)
    queries = draw_queries(jax.random.fold_in(splits[13], 71), 0)
    corpus = draw_corpus(jax.random.fold_in(splits[13], 71), 0)
    cand_shard = draw_cand_shard(jax.random.fold_in(splits[13], 71), 0)
    cand_clip = draw_cand_clip(jax.random.fold_in(splits[13], 71), 0)
    cand_count = draw_cand_count(jax.random.fold_in(splits[13], 71), 0)
    first_kernel = centred(splits[5], (3, 3, 1, CH1), 4 ** -0.5, 3.0)
    first_bias = centred(splits[6], (CH1,), 0.5, 3.0, jnp.float32)
    second_kernel = centred(splits[7], (3, 3, CH1, CH2), (9 * CH1 // 2) ** -0.5, 0.5)
    second_bias = centred(splits[8], (CH2,), 0.5, 3.0, jnp.float32)
    third_kernel = centred(splits[9], (3, 3, CH2, CH3), (9 * CH2 // 2) ** -0.5, 0.375)
    third_bias = centred(splits[10], (CH3,), 0.5, 3.0, jnp.float32)
    score_weight = centred(splits[11], (CH3,), CH3 ** -0.5, 0.5)
    score_bias = centred(splits[12], (1,), 0.5, 3.0, jnp.float32)
    return {"queries": queries, "corpus": corpus, "cand_shard": cand_shard, "cand_clip": cand_clip, "cand_count": cand_count, "first_kernel": first_kernel, "first_bias": first_bias, "second_kernel": second_kernel, "second_bias": second_bias, "third_kernel": third_kernel, "third_bias": third_bias, "score_weight": score_weight, "score_bias": score_bias}


def convolve(inputs, kernel):
    return lax.conv_general_dilated(inputs, kernel, (1, 1), "SAME", dimension_numbers=("NHWC", "HWIO", "NHWC"), precision=lax.Precision.HIGHEST)


def shrink(values):
    batch, height, width, chans = values.shape
    return values.reshape(batch, height // 2, 2, width // 2, 2, chans).max(axis=(2, 4))


def rounded(values):
    return lax.optimization_barrier(values.astype(jnp.bfloat16)).astype(jnp.float32)


def pair_scores(query_rows, cand_rows, first_kernel, first_bias, second_kernel, second_bias, third_kernel, third_bias, score_weight, score_bias):
    batch = query_rows.shape[0]
    region_sim = jnp.einsum("bic,bjc->bij", query_rows, cand_rows, precision=lax.Precision.HIGHEST)
    region_sim = region_sim.reshape(batch, F, R, F, R)
    frame_sim = rounded(region_sim.max(axis=4).mean(axis=2))
    first = rounded(shrink(jax.nn.relu(convolve(frame_sim[..., None], first_kernel.astype(jnp.float32)) + first_bias)))
    second = rounded(shrink(jax.nn.relu(convolve(first, second_kernel.astype(jnp.float32)) + second_bias)))
    third = rounded(jax.nn.relu(convolve(second, third_kernel.astype(jnp.float32)) + third_bias))
    out_map = jnp.einsum("bhwc,c->bhw", third, score_weight.astype(jnp.float32), precision=lax.Precision.HIGHEST) + score_bias[0]
    return out_map.max(axis=2).mean(axis=1)


def reference(queries, corpus, cand_shard, cand_clip, cand_count, first_kernel, first_bias, second_kernel, second_bias, third_kernel, third_bias, score_weight, score_bias):
    query_all = jnp.transpose(queries.reshape(N_REP, Q, FB, R, C), (1, 0, 2, 3, 4)).reshape(Q, F * R, C)
    corpus_all = corpus.reshape(CLIPS, F * R, C)
    global_clip = (cand_shard * CLIP_DEV + cand_clip).astype(jnp.int32).reshape(-1)
    query_ids = jnp.arange(Q * K, dtype=jnp.int32) // K
    block_count = Q * K // 32

    def score_block(ids):
        query_sel = query_all[ids[0]].astype(jnp.float32)
        cand_sel = corpus_all[ids[1]].astype(jnp.float32)
        return pair_scores(query_sel, cand_sel, first_kernel, first_bias, second_kernel, second_bias, third_kernel, third_bias, score_weight, score_bias)

    all_scores = lax.map(score_block, (query_ids.reshape(block_count, 32), global_clip.reshape(block_count, 32)))
    all_scores = all_scores.reshape(Q, K)
    usable = jnp.arange(K, dtype=jnp.int32)[None, :] < cand_count[:, None]
    return jnp.where(usable, all_scores, jnp.float32(0.0))
```

```python
import functools

import jax
import jax.numpy as jnp
import numpy as np
from jax import lax
from jax.experimental import pallas as pl
from jax.experimental.pallas import tpu as pltpu
from jax.sharding import Mesh
from jax.sharding import PartitionSpec as P

NZ, NY, NC, NX = 16, 4, 2, 4
PLANE = ("z", "y", "c")
BACK = (0, 1, -1, 2)


def device_at(z, y, c):
    return ((z % NZ) * NY + y % NY) * NC + c


def shift(values, even, odd):
    pairs = []
    for z in range(NZ):
        for y in range(NY):
            for c, (dz, dy) in ((0, even), (1, odd)):
                pairs.append((device_at(z, y, c), device_at(z + dz, y + dy, c)))
    return lax.ppermute(values, PLANE, pairs)


def gather_queries(block):
    regions, width = block.shape
    flat = block.reshape(regions, width // 128, 128)
    groups = [[j + 4 * k for k in range(4)] for j in range(4)]
    four = lax.all_to_all(
        jnp.broadcast_to(flat, (4,) + flat.shape), "z", 0, 0, axis_index_groups=groups
    )
    four = four.reshape(4, regions, width).transpose(1, 0, 2)
    steps = [four] + [shift(four, (d, 0), (0, d)) for d in BACK[1:]]
    sixteen = jnp.concatenate(steps, axis=1)
    return [sixteen] + [shift(sixteen, (0, d), (d, 0)) for d in BACK[1:]]


def sims_body(regions, frames, own_ref, other_ref, query_ref, out_ref):
    rows = query_ref[...].reshape(-1, query_ref.shape[-1])
    count = rows.shape[0] // regions

    def one(ref):
        sims = lax.dot_general(
            ref[0], rows, (((1,), (1,)), ((), ())), preferred_element_type=jnp.float32
        )
        best = sims[0:frames]
        for j in range(1, regions):
            best = jnp.maximum(best, sims[j * frames : (j + 1) * frames])
        total = best[:, 0:count]
        for i in range(1, regions):
            total = total + best[:, i * count : (i + 1) * count]
        return total * (1.0 / regions)

    step = pl.program_id(0)

    @pl.when(step < 2)
    def _():
        out_ref[0] = one(own_ref)

    @pl.when(step >= 2)
    def _():
        out_ref[0] = one(other_ref)


def frame_sims(own, other, queries):
    clips, rows, width = own.shape
    regions, count = queries.shape[:2]
    frames = rows // regions
    return pl.pallas_call(
        functools.partial(sims_body, regions, frames),
        grid=(4,),
        in_specs=[
            pl.BlockSpec((1, rows, width), lambda s: (jnp.minimum(s, 1), 0, 0)),
            pl.BlockSpec((1, rows, width), lambda s: (jnp.maximum(s, 2) - 2, 0, 0)),
            pl.BlockSpec((regions, count, width), lambda s: (0, 0, 0)),
        ],
        out_specs=pl.BlockSpec((1, frames, count), lambda s: (s, 0, 0)),
        out_shape=jax.ShapeDtypeStruct((4, frames, count), jnp.float32),
        compiler_params=pltpu.CompilerParams(vmem_limit_bytes=40 * 2**20),
        cost_estimate=pl.CostEstimate(
            flops=2 * 4 * rows * regions * count * width,
            bytes_accessed=2 * (4 * rows + regions * count) * width,
            transcendentals=0,
        ),
    )(own, other, queries)


def convolve(inputs, kernel):
    return lax.conv_general_dilated(
        inputs,
        kernel,
        (1, 1),
        "SAME",
        dimension_numbers=("NHWC", "HWIO", "NHWC"),
        preferred_element_type=jnp.float32,
    )


def shrink(values):
    batch, height, width, chans = values.shape
    return values.reshape(batch, height // 2, 2, width // 2, 2, chans).max(axis=(2, 4))


def map_scores(
    frame_sim,
    first_kernel,
    first_bias,
    second_kernel,
    second_bias,
    third_kernel,
    third_bias,
    score_weight,
    score_bias,
):
    first = shrink(jax.nn.relu(convolve(frame_sim[..., None], first_kernel) + first_bias)).astype(
        jnp.bfloat16
    )
    second = shrink(jax.nn.relu(convolve(first, second_kernel) + second_bias)).astype(jnp.bfloat16)
    third = jax.nn.relu(convolve(second, third_kernel) + third_bias).astype(jnp.bfloat16)
    out_map = (
        jnp.einsum("bhwc,c->bhw", third, score_weight, preferred_element_type=jnp.float32)
        + score_bias[0]
    )
    return out_map.max(axis=2).mean(axis=1)


def on_device(
    queries,
    corpus,
    cand_shard,
    cand_clip,
    cand_count,
    *weights,
):
    z, y, c, x = (lax.axis_index(a) for a in ("z", "y", "c", "x"))
    clip_dev, frames, regions, width = corpus.shape
    slots = cand_shard.shape[1]
    group = cand_shard.shape[0] // NX

    own = corpus.transpose(0, 2, 1, 3).reshape(clip_dev, regions * frames, width)
    other = lax.ppermute(own, "c", [(0, 1), (1, 0)])

    blocks = gather_queries(queries[0, 0])
    sims = [frame_sims(own, other, b) for b in blocks]
    sims = jnp.concatenate(sims, axis=2).astype(jnp.bfloat16)
    sims = sims.reshape(NC * clip_dev * frames, NZ * NY)
    sims = jnp.where(c == 0, sims, jnp.roll(sims, clip_dev * frames, axis=0))

    col = jnp.arange(NZ * NY, dtype=jnp.int32)
    back = jnp.array(BACK, jnp.int32)
    far, near = back[col // 16], back[(col // 4) % 4]
    from_z = (z - jnp.where(c == 0, near, far)) % 4 + 4 * (col % 4)
    from_y = (y - jnp.where(c == 0, far, near)) % NY
    place = (from_z * NY + from_y)[:, None] == col[None, :]
    table = lax.dot_general(
        place.astype(jnp.bfloat16),
        sims,
        (((0,), (1,)), ((), ())),
        preferred_element_type=jnp.float32,
    ).astype(jnp.bfloat16)

    parts = lax.all_to_all(
        jnp.concatenate([table, table], axis=0), ("c", "x"), 0, 0, tiled=True
    )
    parts = parts.reshape(NC, NX, group, NY, NC * clip_dev, frames)
    frame_sim = parts.transpose(2, 4, 1, 3, 0, 5).reshape(group * NC * clip_dev, frames, frames)
    scores = map_scores(frame_sim, *weights).reshape(group, NC * clip_dev)

    def mine(listed):
        listed = lax.dynamic_slice_in_dim(listed, x * group, group, 0)
        listed = listed.reshape(group, NZ * NY, NC, slots // (NZ * NY * NC))
        return lax.dynamic_index_in_dim(listed, c, 2, keepdims=False)

    position = jnp.arange(slots, dtype=jnp.int32)
    usable = position[None, :] < cand_count[:, None]
    chip = z * NY + y
    listed = jnp.where(usable & (cand_shard // NC == chip), cand_shard % NC * clip_dev + cand_clip, -1)
    listed = mine(listed)
    hit = listed[..., None] == jnp.arange(NC * clip_dev, dtype=jnp.int32)
    values = jnp.sum(jnp.where(hit, scores[:, None, None, :], 0.0), axis=3)
    values = values.transpose(1, 0, 2).reshape(NZ * NY, -1)
    values = lax.all_to_all(values, ("z", "y"), 0, 0, tiled=True)
    return values.sum(axis=0).reshape(group, -1)


def solution(mesh):
    devices = mesh.devices.reshape(NZ, NY, NC, NX)
    grid = Mesh(devices, ("z", "y", "c", "x"))
    return jax.shard_map(
        on_device,
        mesh=grid,
        in_specs=(P("x", PLANE), P(PLANE)) + (P(),) * 11,
        out_specs=P("x", PLANE),
        check_vma=False,
    )
```

```python
import functools

import jax
import jax.numpy as jnp
import numpy as np
from jax import lax
from jax.experimental import pallas as pl
from jax.experimental.pallas import tpu as pltpu
from jax.sharding import Mesh
from jax.sharding import PartitionSpec as P

NZ, NY, NC, NX = 16, 4, 2, 4
PLANE = ("z", "y", "c")
BACK = (0, 1, -1, 2)


def device_at(z, y, c):
    return ((z % NZ) * NY + y % NY) * NC + c


def shift(values, even, odd):
    pairs = []
    for z in range(NZ):
        for y in range(NY):
            for c, (dz, dy) in ((0, even), (1, odd)):
                pairs.append((device_at(z, y, c), device_at(z + dz, y + dy, c)))
    return lax.ppermute(values, PLANE, pairs)


def gather_stage(block):
    regions, width = block.shape
    flat = block.reshape(regions, width // 128, 128)
    groups = [[j + 4 * k for k in range(4)] for j in range(4)]
    four = lax.all_to_all(
        jnp.broadcast_to(flat, (4,) + flat.shape), "z", 0, 0, axis_index_groups=groups
    )
    four = four.reshape(4, regions, width).transpose(1, 0, 2)
    behind, ahead, two = (shift(four, (d, 0), (0, d)) for d in BACK[1:])
    return jnp.concatenate([four, behind], axis=1), jnp.concatenate([ahead, two], axis=1)


def sims_body(regions, frames, own_ref, other_ref, *refs):
    out_ref = refs[-1]
    rows = jnp.concatenate([ref[...].reshape(-1, ref.shape[-1]) for ref in refs[:-1]], axis=0)
    count = refs[0].shape[1]
    pieces = len(refs) - 1
    for half, corpus_ref in enumerate((own_ref, other_ref)):
        for clip in range(corpus_ref.shape[0]):
            sims = lax.dot_general(
                corpus_ref[clip], rows, (((1,), (1,)), ((), ())), preferred_element_type=jnp.float32
            )
            best = sims[0:frames]
            for j in range(1, regions):
                best = jnp.maximum(best, sims[j * frames : (j + 1) * frames])
            for p in range(pieces):
                total = 0.0
                for i in range(regions):
                    at = (p * regions + i) * count
                    total = total + best[:, at : at + count]
                out_ref[half * 2 + clip, :, p * count : (p + 1) * count] = total * (1.0 / regions)


def frame_sims(own, other, pieces):
    clips, rows, width = own.shape
    regions, count = pieces[0].shape[:2]
    frames = rows // regions
    total = count * len(pieces)
    return pl.pallas_call(
        functools.partial(sims_body, regions, frames),
        in_specs=[pl.BlockSpec(memory_space=pltpu.VMEM)] * (2 + len(pieces)),
        out_specs=pl.BlockSpec(memory_space=pltpu.VMEM),
        out_shape=jax.ShapeDtypeStruct((4, frames, total), jnp.float32),
        compiler_params=pltpu.CompilerParams(vmem_limit_bytes=24 * 2**20),
        cost_estimate=pl.CostEstimate(
            flops=2 * 4 * rows * regions * total * width,
            bytes_accessed=2 * (4 * rows + regions * total) * width,
            transcendentals=0,
        ),
    )(own, other, *pieces)


def convolve(inputs, kernel):
    return lax.conv_general_dilated(
        inputs,
        kernel,
        (1, 1),
        "SAME",
        dimension_numbers=("NHWC", "HWIO", "NHWC"),
        preferred_element_type=jnp.float32,
    )


def shrink(values):
    batch, height, width, chans = values.shape
    return values.reshape(batch, height // 2, 2, width // 2, 2, chans).max(axis=(2, 4))


def map_scores(
    frame_sim,
    first_kernel,
    first_bias,
    second_kernel,
    second_bias,
    third_kernel,
    third_bias,
    score_weight,
    score_bias,
):
    first = shrink(jax.nn.relu(convolve(frame_sim[..., None], first_kernel) + first_bias)).astype(
        jnp.bfloat16
    )
    second = shrink(jax.nn.relu(convolve(first, second_kernel) + second_bias)).astype(jnp.bfloat16)
    third = jax.nn.relu(convolve(second, third_kernel) + third_bias).astype(jnp.bfloat16)
    out_map = (
        jnp.einsum("bhwc,c->bhw", third, score_weight, preferred_element_type=jnp.float32)
        + score_bias[0]
    )
    return out_map.max(axis=2).mean(axis=1)


def on_device(
    queries,
    corpus,
    cand_shard,
    cand_clip,
    cand_count,
    *weights,
):
    z, y, c, x = (lax.axis_index(a) for a in ("z", "y", "c", "x"))
    clip_dev, frames, regions, width = corpus.shape
    slots = cand_shard.shape[1]
    group = cand_shard.shape[0] // NX

    own = corpus.transpose(0, 2, 1, 3).reshape(clip_dev, regions * frames, width)
    other = lax.ppermute(own, "c", [(0, 1), (1, 0)])

    first, last = gather_stage(queries[0, 0])
    behind_first = shift(first, (0, 1), (1, 0))
    ahead_last = shift(last, (0, -1), (-1, 0))
    behind_last = shift(last, (0, 1), (1, 0))
    ahead_first = shift(first, (0, -1), (-1, 0))
    two_first = shift(behind_first, (0, 1), (1, 0))
    two_last = shift(ahead_last, (0, -1), (-1, 0))
    sims = [frame_sims(own, other, [first, last])]
    near, sims[0] = lax.optimization_barrier(
        ((behind_first, behind_last, ahead_first, ahead_last), sims[0])
    )
    sims.append(frame_sims(own, other, near))
    two, sims[1] = lax.optimization_barrier(((two_first, two_last), sims[1]))
    sims.append(frame_sims(own, other, two))
    sims = jnp.concatenate(sims, axis=2).astype(jnp.bfloat16)
    sims = sims.reshape(NC * clip_dev * frames, NZ * NY)
    sims = jnp.where(c == 0, sims, jnp.roll(sims, clip_dev * frames, axis=0))

    col = jnp.arange(NZ * NY, dtype=jnp.int32)
    back = jnp.array(BACK, jnp.int32)
    far, near = back[col // 16], back[(col // 4) % 4]
    from_z = (z - jnp.where(c == 0, near, far)) % 4 + 4 * (col % 4)
    from_y = (y - jnp.where(c == 0, far, near)) % NY
    place = (from_z * NY + from_y)[:, None] == col[None, :]
    table = lax.dot_general(
        place.astype(jnp.bfloat16),
        sims,
        (((0,), (1,)), ((), ())),
        preferred_element_type=jnp.float32,
    ).astype(jnp.bfloat16)

    parts = lax.all_to_all(
        jnp.concatenate([table, table], axis=0), ("c", "x"), 0, 0, tiled=True
    )
    parts = parts.reshape(NC, NX, group, NY, NC * clip_dev, frames)
    frame_sim = parts.transpose(2, 4, 1, 3, 0, 5).reshape(group * NC * clip_dev, frames, frames)
    scores = map_scores(frame_sim, *weights).reshape(group, NC * clip_dev)

    def mine(listed):
        listed = lax.dynamic_slice_in_dim(listed, x * group, group, 0)
        listed = listed.reshape(group, NZ * NY, NC, slots // (NZ * NY * NC))
        return lax.dynamic_index_in_dim(listed, c, 2, keepdims=False)

    position = jnp.arange(slots, dtype=jnp.int32)
    usable = position[None, :] < cand_count[:, None]
    chip = z * NY + y
    listed = jnp.where(usable & (cand_shard // NC == chip), cand_shard % NC * clip_dev + cand_clip, -1)
    listed = mine(listed)
    hit = listed[..., None] == jnp.arange(NC * clip_dev, dtype=jnp.int32)
    values = jnp.sum(jnp.where(hit, scores[:, None, None, :], 0.0), axis=3)
    values = values.transpose(1, 0, 2).reshape(NZ * NY, -1)
    values = lax.all_to_all(values, ("z", "y"), 0, 0, tiled=True)
    return values.sum(axis=0).reshape(group, -1)


def solution(mesh):
    devices = mesh.devices.reshape(NZ, NY, NC, NX)
    grid = Mesh(devices, ("z", "y", "c", "x"))
    return jax.shard_map(
        on_device,
        mesh=grid,
        in_specs=(P("x", PLANE), P(PLANE)) + (P(),) * 11,
        out_specs=P("x", PLANE),
        check_vma=False,
    )
```

```python
import functools

import jax
import jax.numpy as jnp
import numpy as np
from jax import lax
from jax.experimental import pallas as pl
from jax.experimental.pallas import tpu as pltpu
from jax.sharding import Mesh
from jax.sharding import PartitionSpec as P

NZ, NY, NC, NX = 16, 4, 2, 4
PLANE = ("z", "y", "c")
BACK = (0, 1, -1, 2)


def device_at(z, y, c):
    return ((z % NZ) * NY + y % NY) * NC + c


def shift(values, even, odd):
    pairs = []
    for z in range(NZ):
        for y in range(NY):
            for c, (dz, dy) in ((0, even), (1, odd)):
                pairs.append((device_at(z, y, c), device_at(z + dz, y + dy, c)))
    return lax.ppermute(values, PLANE, pairs)


def gather_stage(block):
    regions, width = block.shape
    flat = block.reshape(regions, width // 128, 128)
    groups = [[j + 4 * k for k in range(4)] for j in range(4)]
    four = lax.all_to_all(
        jnp.broadcast_to(flat, (4,) + flat.shape), "z", 0, 0, axis_index_groups=groups
    )
    four = four.reshape(4, regions, width).transpose(1, 0, 2)
    behind, ahead, two = (shift(four, (d, 0), (0, d)) for d in BACK[1:])
    return jnp.concatenate([four, behind], axis=1), jnp.concatenate([ahead, two], axis=1)


def best_means(regions, frames, corpus_ref, clip, rows, count):
    sims = lax.dot_general(
        corpus_ref[clip], rows, (((1,), (1,)), ((), ())), preferred_element_type=jnp.float32
    )
    best = sims[0:frames]
    for j in range(1, regions):
        best = jnp.maximum(best, sims[j * frames : (j + 1) * frames])
    totals = []
    for p in range(rows.shape[0] // (regions * count)):
        total = 0.0
        for i in range(regions):
            at = (p * regions + i) * count
            total = total + best[:, at : at + count]
        totals.append(total * (1.0 / regions))
    return totals


def stacked(refs):
    return jnp.concatenate([ref[...].reshape(-1, ref.shape[-1]) for ref in refs], axis=0)


def sims_body(regions, frames, own_ref, other_ref, *refs):
    out_ref = refs[-1]
    count = refs[0].shape[1]
    rows = stacked(refs[:-1])
    for half, corpus_ref in enumerate((own_ref, other_ref)):
        for clip in range(2):
            at = (half * 2 + clip) * frames
            totals = best_means(regions, frames, corpus_ref, clip, rows, count)
            for p, total in enumerate(totals):
                out_ref[at : at + frames, p * count : (p + 1) * count] = total


def table_body(regions, frames, own_ref, other_ref, prev_ref, place_ref, *refs):
    out_ref, last_ref = refs[-2:]
    sims_body(regions, frames, own_ref, other_ref, *refs[:-2], last_ref)
    prev = prev_ref[...].astype(jnp.bfloat16)
    last = last_ref[...].astype(jnp.bfloat16)
    done = prev.shape[1]
    dims = (((1,), (1,)), ((), ()))
    table = lax.dot_general(
        place_ref[:, :done], prev, dims, preferred_element_type=jnp.float32
    ) + lax.dot_general(place_ref[:, done:], last, dims, preferred_element_type=jnp.float32)
    table = table.astype(jnp.bfloat16)
    out_ref[0 : table.shape[0], :] = table
    out_ref[table.shape[0] :, :] = table


def kernel_call(body, shape, dtype, operands, scratch, flops):
    return pl.pallas_call(
        body,
        in_specs=[pl.BlockSpec(memory_space=pltpu.VMEM)] * len(operands),
        out_specs=pl.BlockSpec(memory_space=pltpu.VMEM),
        out_shape=jax.ShapeDtypeStruct(shape, dtype),
        scratch_shapes=scratch,
        compiler_params=pltpu.CompilerParams(vmem_limit_bytes=24 * 2**20),
        cost_estimate=pl.CostEstimate(
            flops=flops,
            bytes_accessed=sum(o.size * o.dtype.itemsize for o in operands),
            transcendentals=0,
        ),
    )(*operands)


def frame_sims(own, other, pieces):
    clips, rows, width = own.shape
    regions, count = pieces[0].shape[:2]
    frames = rows // regions
    total = count * len(pieces)
    body = functools.partial(sims_body, regions, frames)
    flops = 4 * clips * rows * regions * total * width
    return kernel_call(body, (2 * clips * frames, total), jnp.float32, [own, other, *pieces], [], flops)


def frame_table(own, other, prev, place, pieces):
    clips, rows, width = own.shape
    regions, count = pieces[0].shape[:2]
    frames = rows // regions
    total = count * len(pieces)
    body = functools.partial(table_body, regions, frames)
    flops = 4 * clips * rows * regions * total * width
    return kernel_call(
        body,
        (NC * NZ * NY, 2 * clips * frames),
        jnp.bfloat16,
        [own, other, prev, place, *pieces],
        [pltpu.VMEM((2 * clips * frames, total), jnp.float32)],
        flops,
    )


def row_order():
    group = 4
    order = np.zeros((4, 2, group, 8, NC, NX, group, NY), np.float32)
    for k in range(4):
        for f in range(16):
            frame = 2 * f - 1 + k
            if 0 <= frame < 32:
                for q in range(group):
                    order[k, f % 2, q, f // 2, frame % 2, frame // 8, q, frame % 8 // 2] = 1
    return order.reshape(4 * 64, 128)


def weights_body(first_ref, second_ref, third_ref, t1_ref, t2_ref, t3_ref):
    lanes = t1_ref.shape[1]
    row = lax.broadcasted_iota(jnp.int32, (128, lanes), 0) % 32
    lane = lax.broadcasted_iota(jnp.int32, (128, lanes), 1)
    column = (lane // 32) % 16 * 2 + lane // 512
    for dy in range(3):
        block = jnp.zeros((128, lanes), jnp.float32)
        for dx in range(3):
            tap = first_ref[dy * 3 + dx : dy * 3 + dx + 1, :]
            block = jnp.where(row == column + (dx - 1), tap, block)
        t1_ref[dy * 128 : (dy + 1) * 128, :] = block.astype(jnp.bfloat16)
    left = lax.broadcasted_iota(jnp.int32, (384, 128), 1) < 64

    def placed(tap, before, total):
        rows, width = tap.shape
        parts = [jnp.zeros((before, width), jnp.float32), tap]
        parts.append(jnp.zeros((total - before - rows, width), jnp.float32))
        return jnp.concatenate(parts, axis=0)

    for dy in range(3):
        tap = second_ref[dy * 96 : (dy + 1) * 96, :]
        for odd in range(2):
            one = placed(tap, 96 + 32 * odd, 384)
            two = placed(tap, 160 + 32 * odd, 384)
            t2_ref[dy * 384 : (dy + 1) * 384, odd * 128 : (odd + 1) * 128] = jnp.where(
                left, one, two
            ).astype(jnp.bfloat16)
    for dy in range(3):
        tap = third_ref[dy * 192 : (dy + 1) * 192, :]
        for w in range(2):
            t3_ref[dy * 384 : (dy + 1) * 384, w * 128 : (w + 1) * 128] = placed(
                tap, 64 + 64 * w, 384
            ).astype(jnp.bfloat16)


def spread_weights(first_kernel, second_kernel, third_kernel):
    first = jnp.tile(first_kernel.reshape(9, 32), (1, 32)).astype(jnp.float32)
    second = jnp.tile(second_kernel.reshape(288, 64), (1, 2)).astype(jnp.float32)
    third = third_kernel.reshape(576, 128).astype(jnp.float32)
    return pl.pallas_call(
        weights_body,
        in_specs=[pl.BlockSpec(memory_space=pltpu.VMEM)] * 3,
        out_specs=[pl.BlockSpec(memory_space=pltpu.VMEM)] * 3,
        out_shape=[
            jax.ShapeDtypeStruct((384, 1024), jnp.bfloat16),
            jax.ShapeDtypeStruct((1152, 256), jnp.bfloat16),
            jax.ShapeDtypeStruct((1152, 256), jnp.bfloat16),
        ],
        compiler_params=pltpu.CompilerParams(vmem_limit_bytes=24 * 2**20),
        cost_estimate=pl.CostEstimate(flops=4000000, bytes_accessed=4000000, transcendentals=0),
    )(first, second, third)


def dot(a, b):
    return jnp.dot(a, b, preferred_element_type=jnp.float32)


def rows_beside(values):
    rows = values.shape[0]
    at = lax.broadcasted_iota(jnp.int32, values.shape, 0) % 8
    before = jnp.where(at == 0, 0.0, pltpu.roll(values, 1, 0))
    after = jnp.where(at == 7, 0.0, pltpu.roll(values, rows - 1, 0))
    return before, after


def windows(layers, blocks):
    zero = jnp.zeros((layers[0].shape[0], 128), layers[0].dtype)
    out = []
    for t in range(blocks):
        parts = []
        for layer in layers:
            for b in (t - 1, t, t + 1):
                parts.append(layer[:, b * 128 : (b + 1) * 128] if 0 <= b < blocks else zero)
        out.append(jnp.concatenate(parts, axis=1))
    return out


def score_body(
    parts_ref, order_ref, t1_ref, b1_ref, t2_ref, b2_ref, t3_ref, b3_ref, weight_ref, bias_ref, listed_ref, out_ref
):
    bf16 = jnp.bfloat16
    maps = dot(order_ref[...], parts_ref[...])
    x = [maps[k * 64 : (k + 1) * 64] for k in range(4)]
    x = [(pltpu.roll(v, 64, 1) if k % 2 == 0 else v).astype(bf16) for k, v in enumerate(x)]
    both = jnp.concatenate(
        [jnp.concatenate(x[0:3], axis=1), jnp.concatenate(x[1:4], axis=1)], axis=0
    )
    clip = lax.broadcasted_iota(jnp.int32, both.shape, 1) // 32 % 4
    wide = both.astype(jnp.float32)
    lhs = jnp.concatenate([jnp.where(clip == k, wide, 0.0).astype(bf16) for k in range(4)], axis=0)
    first = dot(lhs, t1_ref[...])
    first = jnp.maximum(first[:, :512], first[:, 512:])
    first = jnp.concatenate(
        [jnp.maximum(first[k * 128 : k * 128 + 64], first[k * 128 + 64 : k * 128 + 128]) for k in range(4)],
        axis=0,
    )
    first = jnp.maximum(first + b1_ref[...], 0.0)
    even = jnp.concatenate([first[k * 64 : k * 64 + 32] for k in range(4)], axis=0)
    odd = jnp.concatenate([first[k * 64 + 32 : k * 64 + 64] for k in range(4)], axis=0)
    odd_before = rows_beside(odd)[0]
    even_after = rows_beside(even)[1]
    layers = [v.astype(bf16) for v in (odd_before, even, odd, even_after)]
    lhs = jnp.concatenate(windows(layers[0:3], 4) + windows(layers[1:4], 4), axis=0)
    second = dot(lhs, t2_ref[...])
    second = jnp.maximum(second[:, :128], second[:, 128:])
    second = jnp.maximum(second[:512], second[512:])
    second = jnp.maximum(second + b2_ref[...], 0.0)
    second = jnp.concatenate([second[t * 128 : (t + 1) * 128] for t in range(4)], axis=1)
    before, after = rows_beside(second)
    lhs = jnp.concatenate(windows([v.astype(bf16) for v in (before, second, after)], 4), axis=0)
    third = jnp.maximum(dot(lhs, t3_ref[...]) + b3_ref[...], 0.0).astype(bf16)
    score = dot(third, weight_ref[...])
    score = jnp.maximum(
        jnp.maximum(score[0:128], score[128:256]), jnp.maximum(score[256:384], score[384:512])
    )
    score = jnp.max(score, axis=1, keepdims=True) + bias_ref[...]
    score = score.reshape(16, 8, score.shape[1]).sum(axis=1) * 0.125
    listed = listed_ref[...]
    slot_query = lax.broadcasted_iota(jnp.int32, (1, listed.shape[1]), 1) // 2
    total = jnp.zeros(listed.shape, jnp.float32)
    for k in range(4):
        line = jnp.zeros((1, listed.shape[1]), jnp.float32)
        for q in range(4):
            line = jnp.where(slot_query == q, score[k * 4 + q : k * 4 + q + 1, : listed.shape[1]], line)
        total = jnp.where(listed == k, line, total)
    out_ref[...] = total


def slot_scores(parts, listed, spread, first_bias, second_bias, third_bias, score_weight, score_bias):
    lanes = jnp.arange(128, dtype=jnp.int32)[None, :] % 2
    half = jnp.arange(256, dtype=jnp.int32)[:, None] // 128
    weight = jnp.where(lanes == half, jnp.tile(score_weight, 2)[:, None], 0).astype(jnp.bfloat16)
    operands = [
        parts,
        jnp.asarray(row_order(), jnp.bfloat16),
        spread[0],
        jnp.tile(first_bias, 16)[None, :],
        spread[1],
        jnp.tile(second_bias, 2)[None, :],
        spread[2],
        jnp.tile(third_bias, 2)[None, :],
        weight,
        jnp.broadcast_to(score_bias[None, :], (1, 128)),
        listed,
    ]
    return kernel_call(score_body, listed.shape, jnp.float32, operands, [], 2 * 10**9)


def on_device(
    queries,
    corpus,
    cand_shard,
    cand_clip,
    cand_count,
    first_kernel,
    first_bias,
    second_kernel,
    second_bias,
    third_kernel,
    third_bias,
    score_weight,
    score_bias,
):
    z, y, c, x = (lax.axis_index(a) for a in ("z", "y", "c", "x"))
    clip_dev, frames, regions, width = corpus.shape
    slots = cand_shard.shape[1]
    group = cand_shard.shape[0] // NX

    own = corpus.transpose(0, 2, 1, 3).reshape(clip_dev, regions * frames, width)
    other = lax.ppermute(own, "c", [(0, 1), (1, 0)])

    first, last = gather_stage(queries[0, 0])
    behind_first = shift(first, (0, 1), (1, 0))
    ahead_last = shift(last, (0, -1), (-1, 0))
    behind_last = shift(last, (0, 1), (1, 0))
    ahead_first = shift(first, (0, -1), (-1, 0))
    two_first = shift(behind_first, (0, 1), (1, 0))
    two_last = shift(ahead_last, (0, -1), (-1, 0))
    col = jnp.arange(NZ * NY, dtype=jnp.int32)
    back = jnp.array(BACK, jnp.int32)
    far, near = back[col // 16], back[(col // 4) % 4]
    from_z = (z - jnp.where(c == 0, near, far)) % 4 + 4 * (col % 4)
    from_y = (y - jnp.where(c == 0, far, near)) % NY
    place = ((from_z * NY + from_y)[None, :] == col[:, None]).astype(jnp.bfloat16)

    def mine(listed):
        listed = lax.dynamic_slice_in_dim(listed, x * group, group, 0)
        listed = listed.reshape(group, NZ * NY, NC, slots // (NZ * NY * NC))
        return lax.dynamic_index_in_dim(listed, c, 2, keepdims=False)

    position = jnp.arange(slots, dtype=jnp.int32)
    usable = position[None, :] < cand_count[:, None]
    chip = z * NY + y
    listed = jnp.where(usable & (cand_shard // NC == chip), cand_shard % NC * clip_dev + cand_clip, -1)
    listed = mine(listed).transpose(1, 0, 2).reshape(NZ * NY, -1)

    spread = spread_weights(first_kernel, second_kernel, third_kernel)

    near = [first, last, behind_first, behind_last, ahead_first, ahead_last]
    prev = frame_sims(own, other, near)
    two, prev = lax.optimization_barrier(((two_first, two_last), prev))
    table = frame_table(own, other, prev, place, two)

    parts = lax.all_to_all(table, ("c", "x"), 0, 0, tiled=True)
    values = slot_scores(
        parts, listed, spread, first_bias, second_bias, third_bias, score_weight, score_bias
    )
    values = lax.all_to_all(values, ("z", "y"), 0, 0, tiled=True)
    return values.sum(axis=0).reshape(group, -1)


def solution(mesh):
    devices = mesh.devices.reshape(NZ, NY, NC, NX)
    grid = Mesh(devices, ("z", "y", "c", "x"))
    return jax.shard_map(
        on_device,
        mesh=grid,
        in_specs=(P("x", PLANE), P(PLANE)) + (P(),) * 11,
        out_specs=P("x", PLANE),
        check_vma=False,
    )
```

```python
import functools

import jax
import jax.numpy as jnp
import numpy as np
from jax import lax
from jax.experimental import pallas as pl
from jax.experimental.pallas import tpu as pltpu
from jax.sharding import Mesh
from jax.sharding import PartitionSpec as P

NZ, NY, NC, NX = 16, 4, 2, 4
PLANE = ("z", "y", "c")


def device_at(z, y, c):
    return ((z % NZ) * NY + y % NY) * NC + c


def send(values, even, odd):
    pairs = []
    for z in range(NZ):
        for y in range(NY):
            for c, to in ((0, even), (1, odd)):
                pairs.append((device_at(z, y, c), device_at(*to(z, y), c)))
    return lax.ppermute(values, PLANE, pairs)


def shift(values, d):
    return send(values, lambda z, y: (z, y + d), lambda z, y: (z + d, y))


def paired(values, side):
    return send(values, lambda z, y: (partner(z, side), y), lambda z, y: (z, partner(y, side)))


def partner(at, side):
    return at + 1 if at % 2 == side else at - 1


def gather_classes(block):
    regions, width = block.shape
    flat = block.reshape(regions, width // 128, 128)
    groups = [[j + 4 * k for k in range(4)] for j in range(4)]
    four = lax.all_to_all(
        jnp.broadcast_to(flat, (4,) + flat.shape), "z", 0, 0, axis_index_groups=groups
    )
    return four.reshape(4, regions, width).transpose(1, 0, 2)


def best_means(regions, frames, corpus_ref, clip, rows, count):
    sims = lax.dot_general(
        corpus_ref[clip], rows, (((1,), (1,)), ((), ())), preferred_element_type=jnp.float32
    )
    best = sims[0:frames]
    for j in range(1, regions):
        best = jnp.maximum(best, sims[j * frames : (j + 1) * frames])
    totals = []
    for p in range(rows.shape[0] // (regions * count)):
        total = 0.0
        for i in range(regions):
            at = (p * regions + i) * count
            total = total + best[:, at : at + count]
        totals.append(total * (1.0 / regions))
    return totals


def stacked(refs):
    return jnp.concatenate([ref[...].reshape(-1, ref.shape[-1]) for ref in refs], axis=0)


def sims_body(regions, frames, own_ref, other_ref, *refs):
    out_ref = refs[-1]
    count = refs[0].shape[1]
    rows = stacked(refs[:-1])
    for half, corpus_ref in enumerate((own_ref, other_ref)):
        for clip in range(2):
            at = (half * 2 + clip) * frames
            totals = best_means(regions, frames, corpus_ref, clip, rows, count)
            for p, total in enumerate(totals):
                out_ref[at : at + frames, p * count : (p + 1) * count] = total


def column_places(z, y, c):
    shape = (NZ * NY, NZ * NY)
    col = lax.broadcasted_iota(jnp.int32, shape, 1)
    row = lax.broadcasted_iota(jnp.int32, shape, 0)
    far = col // 16
    far = jnp.where(far == 2, -1, jnp.where(far == 3, 2, far))
    step = col // 4 % 4

    def near(at):
        beside = jnp.where(at % 2 == 0, at - 1, at + 1)
        start = jnp.where(step < 2, at, (beside + NZ) % NZ)
        return jnp.where(step % 2 == 0, start, start + 1 - start % 2 * 2)

    from_z = jnp.where(c == 0, near(z), z - far + NZ) % 4 + 4 * (col % 4)
    from_y = jnp.where(c == 0, y - far + NZ, near(y)) % NY
    return jnp.where(from_z * NY + from_y == row, 1.0, 0.0).astype(jnp.bfloat16)


def table_body(regions, frames, at_ref, own_ref, other_ref, prev_ref, *refs):
    out_ref, last_ref = refs[-2:]
    place = column_places(at_ref[0], at_ref[1], at_ref[2])
    sims_body(regions, frames, own_ref, other_ref, *refs[:-2], last_ref)
    prev = prev_ref[...].astype(jnp.bfloat16)
    last = last_ref[...].astype(jnp.bfloat16)
    done = prev.shape[1]
    dims = (((1,), (1,)), ((), ()))
    table = lax.dot_general(
        place[:, :done], prev, dims, preferred_element_type=jnp.float32
    ) + lax.dot_general(place[:, done:], last, dims, preferred_element_type=jnp.float32)
    table = table.astype(jnp.bfloat16)
    out_ref[0 : table.shape[0], :] = table
    out_ref[table.shape[0] :, :] = table


def kernel_call(body, outs, operands, scratch, flops, scalars=0):
    spaces = [pltpu.SMEM] * scalars + [pltpu.VMEM] * (len(operands) - scalars)
    return pl.pallas_call(
        body,
        in_specs=[pl.BlockSpec(memory_space=space) for space in spaces],
        out_specs=[pl.BlockSpec(memory_space=pltpu.VMEM)] * len(outs),
        out_shape=[jax.ShapeDtypeStruct(*out) for out in outs],
        scratch_shapes=scratch,
        compiler_params=pltpu.CompilerParams(vmem_limit_bytes=24 * 2**20),
        cost_estimate=pl.CostEstimate(
            flops=flops,
            bytes_accessed=sum(o.size * o.dtype.itemsize for o in operands),
            transcendentals=0,
        ),
    )(*operands)


def frame_sims(own, other, pieces):
    clips, rows, width = own.shape
    regions, count = pieces[0].shape[:2]
    frames = rows // regions
    total = count * len(pieces)
    body = functools.partial(sims_body, regions, frames)
    flops = 4 * clips * rows * regions * total * width
    outs = [((2 * clips * frames, total), jnp.float32)]
    return kernel_call(body, outs, [own, other, *pieces], [], flops)[0]


def frame_table(at, own, other, prev, pieces):
    clips, rows, width = own.shape
    regions, count = pieces[0].shape[:2]
    frames = rows // regions
    total = count * len(pieces)
    return kernel_call(
        functools.partial(table_body, regions, frames),
        [((NC * NZ * NY, 2 * clips * frames), jnp.bfloat16)],
        [at, own, other, prev, *pieces],
        [pltpu.VMEM((2 * clips * frames, total), jnp.float32)],
        4 * clips * rows * regions * total * width,
        scalars=1,
    )[0]


def row_order():
    group = 4
    order = np.zeros((4, 2, group, 8, NC, NX, group, NY), np.float32)
    for k in range(4):
        for f in range(16):
            frame = 2 * f - 1 + k
            if 0 <= frame < 32:
                for q in range(group):
                    order[k, f % 2, q, f // 2, frame % 2, frame // 8, q, frame % 8 // 2] = 1
    return order.reshape(4 * 64, 128)


def prepare_body(
    at_ref, count_ref, shard_ref, clip_ref, first_ref, second_ref, third_ref, listed_ref, t1_ref, t2_ref, t3_ref
):
    f32, bf16 = jnp.float32, jnp.bfloat16
    group, slots = 4, shard_ref.shape[1]
    chip, core, x = at_ref[0] * NY + at_ref[1], at_ref[2], at_ref[3]
    shards = shard_ref[...]
    names = jnp.where(shards // NC == chip, shards % NC * 2 + clip_ref[...], -1)
    line = lax.broadcasted_iota(jnp.int32, names.shape, 0)
    slot = lax.broadcasted_iota(jnp.int32, (1, slots), 1)
    chips = slots // 4
    to_chip = lax.broadcasted_iota(jnp.int32, (chips, slots), 0)
    of_slot = lax.broadcasted_iota(jnp.int32, (chips, slots), 1)
    pick_slot = lax.broadcasted_iota(jnp.int32, (slots, 2 * group), 0) % 4
    pick_to = lax.broadcasted_iota(jnp.int32, (slots, 2 * group), 1)
    listed = jnp.zeros((chips, 2 * group), f32)
    for q in range(group):
        query = x * group + q
        names_q = jnp.sum(jnp.where(line == query, names, 0), axis=0, keepdims=True)
        names_q = jnp.where(slot < count_ref[query], names_q, -1).astype(f32)
        spread = jnp.where(of_slot // 4 == to_chip, names_q, 0.0).astype(bf16)
        pick = jnp.where((pick_to // 2 == q) & (pick_slot == core * 2 + pick_to % 2), 1.0, 0.0)
        listed = listed + dot(spread, pick.astype(bf16))
    listed_ref[...] = listed.astype(jnp.int32)

    lanes = t1_ref.shape[1]
    row = lax.broadcasted_iota(jnp.int32, (128, lanes), 0) % 32
    lane = lax.broadcasted_iota(jnp.int32, (128, lanes), 1)
    column = (lane // 32) % 16 * 2 + lane // 512
    channel = lax.broadcasted_iota(jnp.int32, (32, lanes), 1) % 32
    each = lax.broadcasted_iota(jnp.int32, (32, lanes), 0)
    taps = dot(first_ref[...], jnp.where(channel == each, 1.0, 0.0).astype(bf16))
    for dy in range(3):
        block = jnp.zeros((128, lanes), f32)
        for dx in range(3):
            tap = taps[dy * 3 + dx : dy * 3 + dx + 1, :]
            block = jnp.where(row == column + (dx - 1), tap, block)
        t1_ref[dy * 128 : (dy + 1) * 128, :] = block.astype(bf16)

    def placed(tap, before, total):
        rows, width = tap.shape
        parts = [jnp.zeros((before, width), f32), tap]
        parts.append(jnp.zeros((total - before - rows, width), f32))
        return jnp.concatenate(parts, axis=0)

    left = lax.broadcasted_iota(jnp.int32, (384, 128), 1) < 64
    for dy in range(3):
        tap = second_ref[dy * 96 : (dy + 1) * 96, :].astype(f32)
        tap = jnp.concatenate([tap, tap], axis=1)
        for odd in range(2):
            one = placed(tap, 96 + 32 * odd, 384)
            two = placed(tap, 160 + 32 * odd, 384)
            block = jnp.where(left, one, two).astype(bf16)
            t2_ref[dy * 384 : (dy + 1) * 384, odd * 128 : (odd + 1) * 128] = block
    for dy in range(3):
        tap = third_ref[dy * 192 : (dy + 1) * 192, :].astype(f32)
        for w in range(2):
            block = placed(tap, 64 + 64 * w, 384).astype(bf16)
            t3_ref[dy * 384 : (dy + 1) * 384, w * 128 : (w + 1) * 128] = block


def prepare(at, cand_count, cand_shard, cand_clip, first_kernel, second_kernel, third_kernel):
    operands = [
        at,
        cand_count,
        cand_shard,
        cand_clip,
        first_kernel.reshape(9, 32),
        second_kernel.reshape(288, 64),
        third_kernel.reshape(576, 128),
    ]
    outs = [
        ((cand_shard.shape[1] // 4, 8), jnp.int32),
        ((384, 1024), jnp.bfloat16),
        ((1152, 256), jnp.bfloat16),
        ((1152, 256), jnp.bfloat16),
    ]
    return kernel_call(prepare_body, outs, operands, [], 10**9, scalars=2)


def dot(a, b):
    return jnp.dot(a, b, preferred_element_type=jnp.float32)


def rows_beside(values):
    rows = values.shape[0]
    at = lax.broadcasted_iota(jnp.int32, values.shape, 0) % 8
    before = jnp.where(at == 0, 0.0, pltpu.roll(values, 1, 0))
    after = jnp.where(at == 7, 0.0, pltpu.roll(values, rows - 1, 0))
    return before, after


def windows(layers, blocks):
    zero = jnp.zeros((layers[0].shape[0], 128), layers[0].dtype)
    out = []
    for t in range(blocks):
        parts = []
        for layer in layers:
            for b in (t - 1, t, t + 1):
                parts.append(layer[:, b * 128 : (b + 1) * 128] if 0 <= b < blocks else zero)
        out.append(jnp.concatenate(parts, axis=1))
    return out


def score_body(
    bias_ref, parts_ref, order_ref, t1_ref, b1_ref, t2_ref, b2_ref, t3_ref, b3_ref, weight_ref, listed_ref, out_ref
):
    b1 = jnp.concatenate([b1_ref[...]] * 16, axis=1)
    b2 = jnp.concatenate([b2_ref[...]] * 2, axis=1)
    b3 = jnp.concatenate([b3_ref[...]] * 2, axis=1)
    weight = jnp.concatenate([weight_ref[...].astype(jnp.float32)] * 2, axis=1)
    lane = lax.broadcasted_iota(jnp.int32, (128, 256), 1) // 128
    even_row = lax.broadcasted_iota(jnp.int32, (128, 256), 0) % 2
    weight = jnp.where(lane == even_row, weight, 0.0).astype(jnp.bfloat16)
    bf16 = jnp.bfloat16
    maps = dot(order_ref[...], parts_ref[...])
    x = [maps[k * 64 : (k + 1) * 64] for k in range(4)]
    x = [(pltpu.roll(v, 64, 1) if k % 2 == 0 else v).astype(bf16) for k, v in enumerate(x)]
    both = jnp.concatenate(
        [jnp.concatenate(x[0:3], axis=1), jnp.concatenate(x[1:4], axis=1)], axis=0
    )
    clip = lax.broadcasted_iota(jnp.int32, both.shape, 1) // 32 % 4
    wide = both.astype(jnp.float32)
    lhs = jnp.concatenate([jnp.where(clip == k, wide, 0.0).astype(bf16) for k in range(4)], axis=0)
    first = dot(lhs, t1_ref[...])
    first = jnp.maximum(first[:, :512], first[:, 512:])
    first = jnp.concatenate(
        [jnp.maximum(first[k * 128 : k * 128 + 64], first[k * 128 + 64 : k * 128 + 128]) for k in range(4)],
        axis=0,
    )
    first = jnp.maximum(first + b1, 0.0)
    even = jnp.concatenate([first[k * 64 : k * 64 + 32] for k in range(4)], axis=0)
    odd = jnp.concatenate([first[k * 64 + 32 : k * 64 + 64] for k in range(4)], axis=0)
    odd_before = rows_beside(odd)[0]
    even_after = rows_beside(even)[1]
    layers = [v.astype(bf16) for v in (odd_before, even, odd, even_after)]
    lhs = jnp.concatenate(windows(layers[0:3], 4) + windows(layers[1:4], 4), axis=0)
    second = dot(lhs, t2_ref[...])
    second = jnp.maximum(second[:, :128], second[:, 128:])
    second = jnp.maximum(second[:512], second[512:])
    second = jnp.maximum(second + b2, 0.0)
    second = jnp.concatenate([second[t * 128 : (t + 1) * 128] for t in range(4)], axis=1)
    before, after = rows_beside(second)
    lhs = jnp.concatenate(windows([v.astype(bf16) for v in (before, second, after)], 4), axis=0)
    third = jnp.maximum(dot(lhs, t3_ref[...]) + b3, 0.0).astype(bf16)
    score = lax.dot_general(
        third, weight, (((1,), (1,)), ((), ())), preferred_element_type=jnp.float32
    )
    score = jnp.maximum(
        jnp.maximum(score[0:128], score[128:256]), jnp.maximum(score[256:384], score[384:512])
    )
    score = jnp.max(score, axis=1, keepdims=True) + jnp.broadcast_to(bias_ref[0], (1, 128))
    score = score.reshape(16, 8, score.shape[1]).sum(axis=1) * 0.125
    listed = listed_ref[...]
    slot_query = lax.broadcasted_iota(jnp.int32, (1, listed.shape[1]), 1) // 2
    total = jnp.zeros(listed.shape, jnp.float32)
    for k in range(4):
        line = jnp.zeros((1, listed.shape[1]), jnp.float32)
        for q in range(4):
            line = jnp.where(slot_query == q, score[k * 4 + q : k * 4 + q + 1, : listed.shape[1]], line)
        total = jnp.where(listed == k, line, total)
    out_ref[...] = total


def slot_scores(parts, listed, spread, first_bias, second_bias, third_bias, score_weight, score_bias):
    operands = [
        score_bias,
        parts,
        jnp.asarray(row_order(), jnp.bfloat16),
        spread[0],
        first_bias[None, :],
        spread[1],
        second_bias[None, :],
        spread[2],
        third_bias[None, :],
        score_weight[None, :],
        listed,
    ]
    outs = [(listed.shape, jnp.float32)]
    return kernel_call(score_body, outs, operands, [], 2 * 10**9, scalars=1)[0]


def on_device(
    queries,
    corpus,
    cand_shard,
    cand_clip,
    cand_count,
    first_kernel,
    first_bias,
    second_kernel,
    second_bias,
    third_kernel,
    third_bias,
    score_weight,
    score_bias,
):
    at = jnp.stack([lax.axis_index(a) for a in ("z", "y", "c", "x")]).astype(jnp.int32)
    clip_dev, frames, regions, width = corpus.shape
    group = cand_shard.shape[0] // NX

    own = corpus.transpose(0, 2, 1, 3).reshape(clip_dev, regions * frames, width)
    four = gather_classes(queries[0, 0])
    beside = paired(four, 0)
    kernels = (first_kernel, second_kernel, third_kernel)
    kernels, four = lax.optimization_barrier((kernels, four))
    listed, *spread = prepare(at, cand_count, cand_shard, cand_clip, *kernels)
    first = jnp.concatenate([four, beside], axis=1)
    own, first, listed = lax.optimization_barrier((own, first, listed))
    other = lax.ppermute(own, "c", [(0, 1), (1, 0)])
    last = paired(first, 1)
    behind_first = shift(first, 1)
    ahead_first = shift(first, -1)
    two_first = shift(behind_first, 1)
    behind_last = shift(last, 1)
    ahead_last = shift(last, -1)
    two_last = shift(ahead_last, -1)

    near = [first, last, behind_first, behind_last, ahead_first, ahead_last]
    prev = frame_sims(own, other, near)
    two, prev = lax.optimization_barrier(((two_first, two_last), prev))
    table = frame_table(at, own, other, prev, two)

    parts = lax.all_to_all(table, ("c", "x"), 0, 0, tiled=True)
    values = slot_scores(
        parts, listed, spread, first_bias, second_bias, third_bias, score_weight, score_bias
    )
    values = lax.all_to_all(values, ("z", "y"), 0, 0, tiled=True)
    return values.sum(axis=0).reshape(group, -1)


def solution(mesh):
    devices = mesh.devices.reshape(NZ, NY, NC, NX)
    grid = Mesh(devices, ("z", "y", "c", "x"))
    return jax.shard_map(
        on_device,
        mesh=grid,
        in_specs=(P("x", PLANE), P(PLANE)) + (P(),) * 11,
        out_specs=P("x", PLANE),
        check_vma=False,
    )
```

```python
import functools

import jax
import jax.numpy as jnp
import numpy as np
from jax import lax
from jax.experimental import pallas as pl
from jax.experimental.pallas import tpu as pltpu
from jax.sharding import Mesh
from jax.sharding import PartitionSpec as P

NZ, NY, NC, NX = 16, 4, 2, 4
PLANE = ("z", "y", "c")


def device_at(z, y, c):
    return ((z % NZ) * NY + y % NY) * NC + c


def send(values, even, odd):
    pairs = []
    for z in range(NZ):
        for y in range(NY):
            for c, to in ((0, even), (1, odd)):
                pairs.append((device_at(z, y, c), device_at(*to(z, y), c)))
    return lax.ppermute(values, PLANE, pairs)


def shift(values, d):
    return send(values, lambda z, y: (z, y + d), lambda z, y: (z + d, y))


def near_shift(values, d):
    return send(values, lambda z, y: (z + d, y), lambda z, y: (z, y + d))


def gather_classes(block):
    regions, width = block.shape
    flat = block.reshape(regions, width // 128, 128)
    groups = [[j + 4 * k for k in range(4)] for j in range(4)]
    four = lax.all_to_all(
        jnp.broadcast_to(flat, (4,) + flat.shape), "z", 0, 0, axis_index_groups=groups
    )
    return four.reshape(4, regions, width).transpose(1, 0, 2)


def best_means(regions, frames, corpus_ref, clip, rows, count):
    sims = lax.dot_general(
        corpus_ref[clip], rows, (((1,), (1,)), ((), ())), preferred_element_type=jnp.float32
    )
    best = sims[0:frames]
    for j in range(1, regions):
        best = jnp.maximum(best, sims[j * frames : (j + 1) * frames])
    totals = []
    for p in range(rows.shape[0] // (regions * count)):
        total = 0.0
        for i in range(regions):
            at = (p * regions + i) * count
            total = total + best[:, at : at + count]
        totals.append(total * (1.0 / regions))
    return totals


def stacked(refs):
    return jnp.concatenate([ref[...].reshape(-1, ref.shape[-1]) for ref in refs], axis=0)


def sims_body(regions, frames, own_ref, other_ref, *refs):
    out_ref = refs[-1]
    count = refs[0].shape[1]
    rows = stacked(refs[:-1])
    for half, corpus_ref in enumerate((own_ref, other_ref)):
        for clip in range(2):
            at = (half * 2 + clip) * frames
            totals = best_means(regions, frames, corpus_ref, clip, rows, count)
            for p, total in enumerate(totals):
                out_ref[at : at + frames, p * count : (p + 1) * count] = total


def column_places(z, y, c):
    shape = (NZ * NY, NZ * NY)
    col = lax.broadcasted_iota(jnp.int32, shape, 1)
    row = lax.broadcasted_iota(jnp.int32, shape, 0)

    def back(k):
        return jnp.where(k == 2, -1, jnp.where(k == 3, 2, k))

    far, near = back(col // 16), back(col // 4 % 4)
    from_z = (z + NZ - jnp.where(c == 0, near, far)) % 4 + 4 * (col % 4)
    from_y = (y + NY - jnp.where(c == 0, far, near)) % NY
    return jnp.where(from_z * NY + from_y == row, 1.0, 0.0).astype(jnp.bfloat16)


def table_body(regions, frames, at_ref, own_ref, other_ref, prev_ref, *refs):
    out_ref, last_ref = refs[-2:]
    place = column_places(at_ref[0], at_ref[1], at_ref[2])
    sims_body(regions, frames, own_ref, other_ref, *refs[:-2], last_ref)
    prev = prev_ref[...].astype(jnp.bfloat16)
    last = last_ref[...].astype(jnp.bfloat16)
    done = prev.shape[1]
    dims = (((1,), (1,)), ((), ()))
    table = lax.dot_general(
        place[:, :done], prev, dims, preferred_element_type=jnp.float32
    ) + lax.dot_general(place[:, done:], last, dims, preferred_element_type=jnp.float32)
    table = table.astype(jnp.bfloat16)
    out_ref[0 : table.shape[0], :] = table
    out_ref[table.shape[0] :, :] = table


def kernel_call(body, outs, operands, scratch, flops, scalars=0):
    spaces = [pltpu.SMEM] * scalars + [pltpu.VMEM] * (len(operands) - scalars)
    return pl.pallas_call(
        body,
        in_specs=[pl.BlockSpec(memory_space=space) for space in spaces],
        out_specs=[pl.BlockSpec(memory_space=pltpu.VMEM)] * len(outs),
        out_shape=[jax.ShapeDtypeStruct(*out) for out in outs],
        scratch_shapes=scratch,
        compiler_params=pltpu.CompilerParams(vmem_limit_bytes=24 * 2**20),
        cost_estimate=pl.CostEstimate(
            flops=flops,
            bytes_accessed=sum(o.size * o.dtype.itemsize for o in operands),
            transcendentals=0,
        ),
    )(*operands)


def frame_sims(own, other, pieces):
    clips, rows, width = own.shape
    regions, count = pieces[0].shape[:2]
    frames = rows // regions
    total = count * len(pieces)
    body = functools.partial(sims_body, regions, frames)
    flops = 4 * clips * rows * regions * total * width
    outs = [((2 * clips * frames, total), jnp.float32)]
    return kernel_call(body, outs, [own, other, *pieces], [], flops)[0]


def frame_table(at, own, other, prev, pieces):
    clips, rows, width = own.shape
    regions, count = pieces[0].shape[:2]
    frames = rows // regions
    total = count * len(pieces)
    return kernel_call(
        functools.partial(table_body, regions, frames),
        [((NC * NZ * NY, 2 * clips * frames), jnp.bfloat16)],
        [at, own, other, prev, *pieces],
        [pltpu.VMEM((2 * clips * frames, total), jnp.float32)],
        4 * clips * rows * regions * total * width,
        scalars=1,
    )[0]


def row_order():
    group = 4
    order = np.zeros((4, 2, group, 8, NC, NX, group, NY), np.float32)
    for k in range(4):
        for f in range(16):
            frame = 2 * f - 1 + k
            if 0 <= frame < 32:
                for q in range(group):
                    order[k, f % 2, q, f // 2, frame % 2, frame // 8, q, frame % 8 // 2] = 1
    return order.reshape(4 * 64, 128)


def prepare_body(
    at_ref, count_ref, shard_ref, clip_ref, first_ref, second_ref, third_ref, listed_ref, t1_ref, t2_ref, t3_ref
):
    f32, bf16 = jnp.float32, jnp.bfloat16
    group, slots = 4, shard_ref.shape[1]
    chip, core, x = at_ref[0] * NY + at_ref[1], at_ref[2], at_ref[3]
    shards = shard_ref[...]
    names = jnp.where(shards // NC == chip, shards % NC * 2 + clip_ref[...], -1)
    line = lax.broadcasted_iota(jnp.int32, names.shape, 0)
    slot = lax.broadcasted_iota(jnp.int32, (1, slots), 1)
    chips = slots // 4
    to_chip = lax.broadcasted_iota(jnp.int32, (chips, slots), 0)
    of_slot = lax.broadcasted_iota(jnp.int32, (chips, slots), 1)
    pick_slot = lax.broadcasted_iota(jnp.int32, (slots, 2 * group), 0) % 4
    pick_to = lax.broadcasted_iota(jnp.int32, (slots, 2 * group), 1)
    listed = jnp.zeros((chips, 2 * group), f32)
    for q in range(group):
        query = x * group + q
        names_q = jnp.sum(jnp.where(line == query, names, 0), axis=0, keepdims=True)
        names_q = jnp.where(slot < count_ref[query], names_q, -1).astype(f32)
        spread = jnp.where(of_slot // 4 == to_chip, names_q, 0.0).astype(bf16)
        pick = jnp.where((pick_to // 2 == q) & (pick_slot == core * 2 + pick_to % 2), 1.0, 0.0)
        listed = listed + dot(spread, pick.astype(bf16))
    listed_ref[...] = listed.astype(jnp.int32)

    lanes = t1_ref.shape[1]
    row = lax.broadcasted_iota(jnp.int32, (128, lanes), 0) % 32
    lane = lax.broadcasted_iota(jnp.int32, (128, lanes), 1)
    column = (lane // 32) % 16 * 2 + lane // 512
    channel = lax.broadcasted_iota(jnp.int32, (32, lanes), 1) % 32
    each = lax.broadcasted_iota(jnp.int32, (32, lanes), 0)
    taps = dot(first_ref[...], jnp.where(channel == each, 1.0, 0.0).astype(bf16))
    for dy in range(3):
        block = jnp.zeros((128, lanes), f32)
        for dx in range(3):
            tap = taps[dy * 3 + dx : dy * 3 + dx + 1, :]
            block = jnp.where(row == column + (dx - 1), tap, block)
        t1_ref[dy * 128 : (dy + 1) * 128, :] = block.astype(bf16)

    def placed(tap, before, total):
        rows, width = tap.shape
        parts = [jnp.zeros((before, width), f32), tap]
        parts.append(jnp.zeros((total - before - rows, width), f32))
        return jnp.concatenate(parts, axis=0)

    left = lax.broadcasted_iota(jnp.int32, (384, 128), 1) < 64
    for dy in range(3):
        tap = second_ref[dy * 96 : (dy + 1) * 96, :].astype(f32)
        tap = jnp.concatenate([tap, tap], axis=1)
        for odd in range(2):
            one = placed(tap, 96 + 32 * odd, 384)
            two = placed(tap, 160 + 32 * odd, 384)
            block = jnp.where(left, one, two).astype(bf16)
            t2_ref[dy * 384 : (dy + 1) * 384, odd * 128 : (odd + 1) * 128] = block
    for dy in range(3):
        tap = third_ref[dy * 192 : (dy + 1) * 192, :].astype(f32)
        for w in range(2):
            block = placed(tap, 64 + 64 * w, 384).astype(bf16)
            t3_ref[dy * 384 : (dy + 1) * 384, w * 128 : (w + 1) * 128] = block


def prepare(at, cand_count, cand_shard, cand_clip, first_kernel, second_kernel, third_kernel):
    operands = [
        at,
        cand_count,
        cand_shard,
        cand_clip,
        first_kernel.reshape(9, 32),
        second_kernel.reshape(288, 64),
        third_kernel.reshape(576, 128),
    ]
    outs = [
        ((cand_shard.shape[1] // 4, 8), jnp.int32),
        ((384, 1024), jnp.bfloat16),
        ((1152, 256), jnp.bfloat16),
        ((1152, 256), jnp.bfloat16),
    ]
    return kernel_call(prepare_body, outs, operands, [], 10**9, scalars=2)


def dot(a, b):
    return jnp.dot(a, b, preferred_element_type=jnp.float32)


def rows_beside(values):
    rows = values.shape[0]
    at = lax.broadcasted_iota(jnp.int32, values.shape, 0) % 8
    before = jnp.where(at == 0, 0.0, pltpu.roll(values, 1, 0))
    after = jnp.where(at == 7, 0.0, pltpu.roll(values, rows - 1, 0))
    return before, after


def windows(layers, blocks):
    zero = jnp.zeros((layers[0].shape[0], 128), layers[0].dtype)
    out = []
    for t in range(blocks):
        parts = []
        for layer in layers:
            for b in (t - 1, t, t + 1):
                parts.append(layer[:, b * 128 : (b + 1) * 128] if 0 <= b < blocks else zero)
        out.append(jnp.concatenate(parts, axis=1))
    return out


def score_body(
    bias_ref, parts_ref, order_ref, t1_ref, b1_ref, t2_ref, b2_ref, t3_ref, b3_ref, weight_ref, listed_ref, out_ref
):
    b1 = jnp.concatenate([b1_ref[...]] * 16, axis=1)
    b2 = jnp.concatenate([b2_ref[...]] * 2, axis=1)
    b3 = jnp.concatenate([b3_ref[...]] * 2, axis=1)
    weight = jnp.concatenate([weight_ref[...].astype(jnp.float32)] * 2, axis=1)
    lane = lax.broadcasted_iota(jnp.int32, (128, 256), 1) // 128
    even_row = lax.broadcasted_iota(jnp.int32, (128, 256), 0) % 2
    weight = jnp.where(lane == even_row, weight, 0.0).astype(jnp.bfloat16)
    bf16 = jnp.bfloat16
    maps = dot(order_ref[...], parts_ref[...])
    x = [maps[k * 64 : (k + 1) * 64] for k in range(4)]
    x = [(pltpu.roll(v, 64, 1) if k % 2 == 0 else v).astype(bf16) for k, v in enumerate(x)]
    both = jnp.concatenate(
        [jnp.concatenate(x[0:3], axis=1), jnp.concatenate(x[1:4], axis=1)], axis=0
    )
    clip = lax.broadcasted_iota(jnp.int32, both.shape, 1) // 32 % 4
    wide = both.astype(jnp.float32)
    lhs = jnp.concatenate([jnp.where(clip == k, wide, 0.0).astype(bf16) for k in range(4)], axis=0)
    first = dot(lhs, t1_ref[...])
    first = jnp.maximum(first[:, :512], first[:, 512:])
    first = jnp.concatenate(
        [jnp.maximum(first[k * 128 : k * 128 + 64], first[k * 128 + 64 : k * 128 + 128]) for k in range(4)],
        axis=0,
    )
    first = jnp.maximum(first + b1, 0.0)
    even = jnp.concatenate([first[k * 64 : k * 64 + 32] for k in range(4)], axis=0)
    odd = jnp.concatenate([first[k * 64 + 32 : k * 64 + 64] for k in range(4)], axis=0)
    odd_before = rows_beside(odd)[0]
    even_after = rows_beside(even)[1]
    layers = [v.astype(bf16) for v in (odd_before, even, odd, even_after)]
    lhs = jnp.concatenate(windows(layers[0:3], 4) + windows(layers[1:4], 4), axis=0)
    second = dot(lhs, t2_ref[...])
    second = jnp.maximum(second[:, :128], second[:, 128:])
    second = jnp.maximum(second[:512], second[512:])
    second = jnp.maximum(second + b2, 0.0)
    second = jnp.concatenate([second[t * 128 : (t + 1) * 128] for t in range(4)], axis=1)
    before, after = rows_beside(second)
    lhs = jnp.concatenate(windows([v.astype(bf16) for v in (before, second, after)], 4), axis=0)
    third = jnp.maximum(dot(lhs, t3_ref[...]) + b3, 0.0).astype(bf16)
    score = lax.dot_general(
        third, weight, (((1,), (1,)), ((), ())), preferred_element_type=jnp.float32
    )
    score = jnp.maximum(
        jnp.maximum(score[0:128], score[128:256]), jnp.maximum(score[256:384], score[384:512])
    )
    score = jnp.max(score, axis=1, keepdims=True) + jnp.broadcast_to(bias_ref[0], (1, 128))
    score = score.reshape(16, 8, score.shape[1]).sum(axis=1) * 0.125
    listed = listed_ref[...]
    slot_query = lax.broadcasted_iota(jnp.int32, (1, listed.shape[1]), 1) // 2
    total = jnp.zeros(listed.shape, jnp.float32)
    for k in range(4):
        line = jnp.zeros((1, listed.shape[1]), jnp.float32)
        for q in range(4):
            line = jnp.where(slot_query == q, score[k * 4 + q : k * 4 + q + 1, : listed.shape[1]], line)
        total = jnp.where(listed == k, line, total)
    out_ref[...] = total


def slot_scores(parts, listed, spread, first_bias, second_bias, third_bias, score_weight, score_bias):
    operands = [
        score_bias,
        parts,
        jnp.asarray(row_order(), jnp.bfloat16),
        spread[0],
        first_bias[None, :],
        spread[1],
        second_bias[None, :],
        spread[2],
        third_bias[None, :],
        score_weight[None, :],
        listed,
    ]
    outs = [(listed.shape, jnp.float32)]
    return kernel_call(score_body, outs, operands, [], 2 * 10**9, scalars=1)[0]


def on_device(
    queries,
    corpus,
    cand_shard,
    cand_clip,
    cand_count,
    first_kernel,
    first_bias,
    second_kernel,
    second_bias,
    third_kernel,
    third_bias,
    score_weight,
    score_bias,
):
    at = jnp.stack([lax.axis_index(a) for a in ("z", "y", "c", "x")]).astype(jnp.int32)
    clip_dev, frames, regions, width = corpus.shape
    group = cand_shard.shape[0] // NX

    own = corpus.transpose(0, 2, 1, 3).reshape(clip_dev, regions * frames, width)
    four = gather_classes(queries[0, 0])
    ahead = near_shift(four, -1)
    two = near_shift(four, 2)
    behind = near_shift(four, 1)
    first = jnp.concatenate([four, behind], axis=1)
    last = jnp.concatenate([ahead, two], axis=1)
    kernels = (first_kernel, second_kernel, third_kernel)
    listed, *spread = prepare(at, cand_count, cand_shard, cand_clip, *kernels)
    other = lax.ppermute(own, "c", [(0, 1), (1, 0)])
    behind_first = shift(first, 1)
    ahead_first = shift(first, -1)
    two_first = shift(behind_first, 1)
    behind_last = shift(last, 1)
    ahead_last = shift(last, -1)
    two_last = shift(ahead_last, -1)

    near = [first, last, behind_first, behind_last, ahead_first, ahead_last]
    prev = frame_sims(own, other, near)
    two, prev = lax.optimization_barrier(((two_first, two_last), prev))
    table = frame_table(at, own, other, prev, two)

    parts = lax.all_to_all(table, ("c", "x"), 0, 0, tiled=True)
    values = slot_scores(
        parts, listed, spread, first_bias, second_bias, third_bias, score_weight, score_bias
    )
    values = lax.all_to_all(values, ("z", "y"), 0, 0, tiled=True)
    return values.sum(axis=0).reshape(group, -1)


def solution(mesh):
    devices = mesh.devices.reshape(NZ, NY, NC, NX)
    grid = Mesh(devices, ("z", "y", "c", "x"))
    return jax.shard_map(
        on_device,
        mesh=grid,
        in_specs=(P("x", PLANE), P(PLANE)) + (P(),) * 11,
        out_specs=P("x", PLANE),
        check_vma=False,
    )
```

```python
import functools

import jax
import jax.numpy as jnp
import numpy as np
from jax import lax
from jax.experimental import pallas as pl
from jax.experimental.pallas import tpu as pltpu
from jax.sharding import Mesh
from jax.sharding import PartitionSpec as P

NZ, NY, NC, NX = 16, 4, 2, 4
PLANE = ("z", "y", "c")


def device_at(z, y, c):
    return ((z % NZ) * NY + y % NY) * NC + c


def send(values, even, odd):
    pairs = []
    for z in range(NZ):
        for y in range(NY):
            for c, to in ((0, even), (1, odd)):
                pairs.append((device_at(z, y, c), device_at(*to(z, y), c)))
    return lax.ppermute(values, PLANE, pairs)


def shift(values, d):
    return send(values, lambda z, y: (z, y + d), lambda z, y: (z + d, y))


def near_shift(values, d):
    return send(values, lambda z, y: (z + d, y), lambda z, y: (z, y + d))


def gather_classes(block):
    regions, width = block.shape
    flat = block.reshape(regions, width // 128, 128)
    groups = [[j + 4 * k for k in range(4)] for j in range(4)]
    four = lax.all_to_all(
        jnp.broadcast_to(flat, (4,) + flat.shape), "z", 0, 0, axis_index_groups=groups
    )
    return four.reshape(4, regions, width).transpose(1, 0, 2)


def best_means(regions, frames, corpus_ref, clip, rows, count):
    sims = lax.dot_general(
        corpus_ref[clip], rows, (((1,), (1,)), ((), ())), preferred_element_type=jnp.float32
    )
    best = sims[0:frames]
    for j in range(1, regions):
        best = jnp.maximum(best, sims[j * frames : (j + 1) * frames])
    totals = []
    for p in range(rows.shape[0] // (regions * count)):
        total = 0.0
        for i in range(regions):
            at = (p * regions + i) * count
            total = total + best[:, at : at + count]
        totals.append(total * (1.0 / regions))
    return totals


def stacked(refs):
    return jnp.concatenate([ref[...].reshape(-1, ref.shape[-1]) for ref in refs], axis=0)


def sims_body(regions, frames, own_ref, other_ref, *refs):
    out_ref = refs[-1]
    count = refs[0].shape[1]
    rows = stacked(refs[:-1])
    for half, corpus_ref in enumerate((own_ref, other_ref)):
        for clip in range(2):
            at = (half * 2 + clip) * frames
            totals = best_means(regions, frames, corpus_ref, clip, rows, count)
            for p, total in enumerate(totals):
                out_ref[at : at + frames, p * count : (p + 1) * count] = total


def column_places(z, y, c):
    shape = (NZ * NY, NZ * NY)
    col = lax.broadcasted_iota(jnp.int32, shape, 1)
    row = lax.broadcasted_iota(jnp.int32, shape, 0)

    def back(k):
        return jnp.where(k == 2, -1, jnp.where(k == 3, 2, k))

    far, near = back(col // 16), back(col // 4 % 4)
    from_z = (z + NZ - jnp.where(c == 0, near, far)) % 4 + 4 * (col % 4)
    from_y = (y + NY - jnp.where(c == 0, far, near)) % NY
    return jnp.where(from_z * NY + from_y == row, 1.0, 0.0).astype(jnp.bfloat16)


def table_body(regions, frames, at_ref, own_ref, other_ref, prev_ref, *refs):
    out_ref, last_ref = refs[-2:]
    place = column_places(at_ref[0], at_ref[1], at_ref[2])
    sims_body(regions, frames, own_ref, other_ref, *refs[:-2], last_ref)
    prev = prev_ref[...].astype(jnp.bfloat16)
    last = last_ref[...].astype(jnp.bfloat16)
    done = prev.shape[1]
    dims = (((1,), (1,)), ((), ()))
    table = lax.dot_general(
        place[:, :done], prev, dims, preferred_element_type=jnp.float32
    ) + lax.dot_general(place[:, done:], last, dims, preferred_element_type=jnp.float32)
    table = table.astype(jnp.bfloat16)
    out_ref[0 : table.shape[0], :] = table
    out_ref[table.shape[0] :, :] = table


def kernel_call(body, outs, operands, scratch, flops, scalars=0):
    spaces = [pltpu.SMEM] * scalars + [pltpu.VMEM] * (len(operands) - scalars)
    return pl.pallas_call(
        body,
        in_specs=[pl.BlockSpec(memory_space=space) for space in spaces],
        out_specs=[pl.BlockSpec(memory_space=pltpu.VMEM)] * len(outs),
        out_shape=[jax.ShapeDtypeStruct(*out) for out in outs],
        scratch_shapes=scratch,
        compiler_params=pltpu.CompilerParams(vmem_limit_bytes=24 * 2**20),
        cost_estimate=pl.CostEstimate(
            flops=flops,
            bytes_accessed=sum(o.size * o.dtype.itemsize for o in operands),
            transcendentals=0,
        ),
    )(*operands)


def frame_sims(own, other, pieces):
    clips, rows, width = own.shape
    regions, count = pieces[0].shape[:2]
    frames = rows // regions
    total = count * len(pieces)
    body = functools.partial(sims_body, regions, frames)
    flops = 4 * clips * rows * regions * total * width
    outs = [((2 * clips * frames, total), jnp.float32)]
    return kernel_call(body, outs, [own, other, *pieces], [], flops)[0]


def frame_table(at, own, other, prev, pieces):
    clips, rows, width = own.shape
    regions, count = pieces[0].shape[:2]
    frames = rows // regions
    total = count * len(pieces)
    return kernel_call(
        functools.partial(table_body, regions, frames),
        [((NC * NZ * NY, 2 * clips * frames), jnp.bfloat16)],
        [at, own, other, prev, *pieces],
        [pltpu.VMEM((2 * clips * frames, total), jnp.float32)],
        4 * clips * rows * regions * total * width,
        scalars=1,
    )[0]


def row_order():
    group = 4
    order = np.zeros((4, 2, group, 8, NC, NX, group, NY), np.float32)
    for k in range(4):
        for f in range(16):
            frame = 2 * f - 1 + k
            if 0 <= frame < 32:
                for q in range(group):
                    order[k, f % 2, q, f // 2, frame % 2, frame // 8, q, frame % 8 // 2] = 1
    return order.reshape(4 * 64, 128)


def prepare_body(
    at_ref, count_ref, shard_ref, clip_ref, first_ref, second_ref, third_ref, listed_ref, t1_ref, t2_ref, t3_ref
):
    f32, bf16 = jnp.float32, jnp.bfloat16
    group, slots = 4, shard_ref.shape[1]
    chip, core, x = at_ref[0] * NY + at_ref[1], at_ref[2], at_ref[3]
    shards = shard_ref[...]
    names = jnp.where(shards // NC == chip, shards % NC * 2 + clip_ref[...], -1)
    line = lax.broadcasted_iota(jnp.int32, names.shape, 0)
    slot = lax.broadcasted_iota(jnp.int32, (1, slots), 1)
    chips = slots // 4
    to_chip = lax.broadcasted_iota(jnp.int32, (chips, slots), 0)
    of_slot = lax.broadcasted_iota(jnp.int32, (chips, slots), 1)
    pick_slot = lax.broadcasted_iota(jnp.int32, (slots, 2 * group), 0) % 4
    pick_to = lax.broadcasted_iota(jnp.int32, (slots, 2 * group), 1)
    listed = jnp.zeros((chips, 2 * group), f32)
    for q in range(group):
        query = x * group + q
        names_q = jnp.sum(jnp.where(line == query, names, 0), axis=0, keepdims=True)
        names_q = jnp.where(slot < count_ref[query], names_q, -1).astype(f32)
        spread = jnp.where(of_slot // 4 == to_chip, names_q, 0.0).astype(bf16)
        pick = jnp.where((pick_to // 2 == q) & (pick_slot == core * 2 + pick_to % 2), 1.0, 0.0)
        listed = listed + dot(spread, pick.astype(bf16))
    listed_ref[...] = listed.astype(jnp.int32)

    lanes = t1_ref.shape[1]
    row = lax.broadcasted_iota(jnp.int32, (128, lanes), 0) % 32
    lane = lax.broadcasted_iota(jnp.int32, (128, lanes), 1)
    column = (lane // 32) % 16 * 2 + lane // 512
    channel = lax.broadcasted_iota(jnp.int32, (32, lanes), 1) % 32
    each = lax.broadcasted_iota(jnp.int32, (32, lanes), 0)
    taps = dot(first_ref[...], jnp.where(channel == each, 1.0, 0.0).astype(bf16))
    for dy in range(3):
        block = jnp.zeros((128, lanes), f32)
        for dx in range(3):
            tap = taps[dy * 3 + dx : dy * 3 + dx + 1, :]
            block = jnp.where(row == column + (dx - 1), tap, block)
        t1_ref[dy * 128 : (dy + 1) * 128, :] = block.astype(bf16)

    def placed(tap, before, total):
        rows, width = tap.shape
        parts = [jnp.zeros((before, width), f32), tap]
        parts.append(jnp.zeros((total - before - rows, width), f32))
        return jnp.concatenate(parts, axis=0)

    left = lax.broadcasted_iota(jnp.int32, (384, 128), 1) < 64
    for dy in range(3):
        tap = second_ref[dy * 96 : (dy + 1) * 96, :].astype(f32)
        tap = jnp.concatenate([tap, tap], axis=1)
        for odd in range(2):
            one = placed(tap, 96 + 32 * odd, 384)
            two = placed(tap, 160 + 32 * odd, 384)
            block = jnp.where(left, one, two).astype(bf16)
            t2_ref[dy * 384 : (dy + 1) * 384, odd * 128 : (odd + 1) * 128] = block
    for dy in range(3):
        tap = third_ref[dy * 192 : (dy + 1) * 192, :].astype(f32)
        for w in range(2):
            block = placed(tap, 64 + 64 * w, 384).astype(bf16)
            t3_ref[dy * 384 : (dy + 1) * 384, w * 128 : (w + 1) * 128] = block


def prepare(at, cand_count, cand_shard, cand_clip, first_kernel, second_kernel, third_kernel):
    operands = [
        at,
        cand_count,
        cand_shard,
        cand_clip,
        first_kernel.reshape(9, 32),
        second_kernel.reshape(288, 64),
        third_kernel.reshape(576, 128),
    ]
    outs = [
        ((cand_shard.shape[1] // 4, 8), jnp.int32),
        ((384, 1024), jnp.bfloat16),
        ((1152, 256), jnp.bfloat16),
        ((1152, 256), jnp.bfloat16),
    ]
    return kernel_call(prepare_body, outs, operands, [], 10**9, scalars=2)


def dot(a, b):
    return jnp.dot(a, b, preferred_element_type=jnp.float32)


def rows_beside(values):
    rows = values.shape[0]
    at = lax.broadcasted_iota(jnp.int32, values.shape, 0) % 8
    before = jnp.where(at == 0, 0.0, pltpu.roll(values, 1, 0))
    after = jnp.where(at == 7, 0.0, pltpu.roll(values, rows - 1, 0))
    return before, after


def windows(layers, blocks):
    zero = jnp.zeros((layers[0].shape[0], 128), layers[0].dtype)
    out = []
    for t in range(blocks):
        parts = []
        for layer in layers:
            for b in (t - 1, t, t + 1):
                parts.append(layer[:, b * 128 : (b + 1) * 128] if 0 <= b < blocks else zero)
        out.append(jnp.concatenate(parts, axis=1))
    return out


def score_body(
    bias_ref, parts_ref, order_ref, t1_ref, b1_ref, t2_ref, b2_ref, t3_ref, b3_ref, weight_ref, listed_ref, out_ref
):
    b1 = jnp.concatenate([b1_ref[...]] * 16, axis=1)
    b2 = jnp.concatenate([b2_ref[...]] * 2, axis=1)
    b3 = jnp.concatenate([b3_ref[...]] * 2, axis=1)
    weight = jnp.concatenate([weight_ref[...].astype(jnp.float32)] * 2, axis=1)
    lane = lax.broadcasted_iota(jnp.int32, (128, 256), 1) // 128
    even_row = lax.broadcasted_iota(jnp.int32, (128, 256), 0) % 2
    weight = jnp.where(lane == even_row, weight, 0.0).astype(jnp.bfloat16)
    bf16 = jnp.bfloat16
    maps = dot(order_ref[...], parts_ref[...])
    x = [maps[k * 64 : (k + 1) * 64] for k in range(4)]
    x = [(pltpu.roll(v, 64, 1) if k % 2 == 0 else v).astype(bf16) for k, v in enumerate(x)]
    both = jnp.concatenate(
        [jnp.concatenate(x[0:3], axis=1), jnp.concatenate(x[1:4], axis=1)], axis=0
    )
    clip = lax.broadcasted_iota(jnp.int32, both.shape, 1) // 32 % 4
    wide = both.astype(jnp.float32)
    lhs = jnp.concatenate([jnp.where(clip == k, wide, 0.0).astype(bf16) for k in range(4)], axis=0)
    first = dot(lhs, t1_ref[...])
    first = jnp.maximum(first[:, :512], first[:, 512:])
    first = jnp.concatenate(
        [jnp.maximum(first[k * 128 : k * 128 + 64], first[k * 128 + 64 : k * 128 + 128]) for k in range(4)],
        axis=0,
    )
    first = jnp.maximum(first + b1, 0.0)
    even = jnp.concatenate([first[k * 64 : k * 64 + 32] for k in range(4)], axis=0)
    odd = jnp.concatenate([first[k * 64 + 32 : k * 64 + 64] for k in range(4)], axis=0)
    odd_before = rows_beside(odd)[0]
    even_after = rows_beside(even)[1]
    layers = [v.astype(bf16) for v in (odd_before, even, odd, even_after)]
    lhs = jnp.concatenate(windows(layers[0:3], 4) + windows(layers[1:4], 4), axis=0)
    second = dot(lhs, t2_ref[...])
    second = jnp.maximum(second[:, :128], second[:, 128:])
    second = jnp.maximum(second[:512], second[512:])
    second = jnp.maximum(second + b2, 0.0)
    second = jnp.concatenate([second[t * 128 : (t + 1) * 128] for t in range(4)], axis=1)
    before, after = rows_beside(second)
    lhs = jnp.concatenate(windows([v.astype(bf16) for v in (before, second, after)], 4), axis=0)
    third = jnp.maximum(dot(lhs, t3_ref[...]) + b3, 0.0).astype(bf16)
    score = lax.dot_general(
        third, weight, (((1,), (1,)), ((), ())), preferred_element_type=jnp.float32
    )
    score = jnp.maximum(
        jnp.maximum(score[0:128], score[128:256]), jnp.maximum(score[256:384], score[384:512])
    )
    score = jnp.max(score, axis=1, keepdims=True) + jnp.broadcast_to(bias_ref[0], (1, 128))
    score = score.reshape(16, 8, score.shape[1]).sum(axis=1) * 0.125
    listed = listed_ref[...]
    slot_query = lax.broadcasted_iota(jnp.int32, (1, listed.shape[1]), 1) // 2
    total = jnp.zeros(listed.shape, jnp.float32)
    for k in range(4):
        line = jnp.zeros((1, listed.shape[1]), jnp.float32)
        for q in range(4):
            line = jnp.where(slot_query == q, score[k * 4 + q : k * 4 + q + 1, : listed.shape[1]], line)
        total = jnp.where(listed == k, line, total)
    out_ref[...] = total


def slot_scores(parts, listed, spread, first_bias, second_bias, third_bias, score_weight, score_bias):
    operands = [
        score_bias,
        parts,
        jnp.asarray(row_order(), jnp.bfloat16),
        spread[0],
        first_bias[None, :],
        spread[1],
        second_bias[None, :],
        spread[2],
        third_bias[None, :],
        score_weight[None, :],
        listed,
    ]
    outs = [(listed.shape, jnp.float32)]
    return kernel_call(score_body, outs, operands, [], 2 * 10**9, scalars=1)[0]


def on_device(
    queries,
    corpus,
    cand_shard,
    cand_clip,
    cand_count,
    first_kernel,
    first_bias,
    second_kernel,
    second_bias,
    third_kernel,
    third_bias,
    score_weight,
    score_bias,
):
    at = jnp.stack([lax.axis_index(a) for a in ("z", "y", "c", "x")]).astype(jnp.int32)
    clip_dev, frames, regions, width = corpus.shape
    group = cand_shard.shape[0] // NX

    own = corpus.transpose(0, 2, 1, 3).reshape(clip_dev, regions * frames, width)
    four = gather_classes(queries[0, 0])
    ahead = near_shift(four, -1)
    two = near_shift(four, 2)
    behind = near_shift(four, 1)
    first = jnp.concatenate([four, behind], axis=1)
    last = jnp.concatenate([ahead, two], axis=1)
    kernels = (first_kernel, second_kernel, third_kernel)
    listed, *spread = prepare(at, cand_count, cand_shard, cand_clip, *kernels)
    own, first, last = lax.optimization_barrier((own, first, last))
    other = lax.ppermute(own, "c", [(0, 1), (1, 0)])
    behind_first = shift(first, 1)
    ahead_first = shift(first, -1)
    two_first = shift(behind_first, 1)
    behind_last = shift(last, 1)
    ahead_last = shift(last, -1)
    two_last = shift(ahead_last, -1)

    near = [first, last, behind_first, behind_last, ahead_first, ahead_last]
    prev = frame_sims(own, other, near)
    two, prev = lax.optimization_barrier(((two_first, two_last), prev))
    table = frame_table(at, own, other, prev, two)

    parts = lax.all_to_all(table, ("c", "x"), 0, 0, tiled=True)
    values = slot_scores(
        parts, listed, spread, first_bias, second_bias, third_bias, score_weight, score_bias
    )
    values = lax.all_to_all(values, ("z", "y"), 0, 0, tiled=True)
    return values.sum(axis=0).reshape(group, -1)


def solution(mesh):
    devices = mesh.devices.reshape(NZ, NY, NC, NX)
    grid = Mesh(devices, ("z", "y", "c", "x"))
    return jax.shard_map(
        on_device,
        mesh=grid,
        in_specs=(P("x", PLANE), P(PLANE)) + (P(),) * 11,
        out_specs=P("x", PLANE),
        check_vma=False,
    )
```

```python
import functools

import jax
import jax.numpy as jnp
import numpy as np
from jax import lax
from jax.experimental import pallas as pl
from jax.experimental.pallas import tpu as pltpu
from jax.sharding import Mesh
from jax.sharding import PartitionSpec as P

NZ, NY, NC, NX = 16, 4, 2, 4
PLANE = ("z", "y", "c")


def device_at(z, y, c):
    return ((z % NZ) * NY + y % NY) * NC + c


def send(values, even, odd):
    pairs = []
    for z in range(NZ):
        for y in range(NY):
            for c, to in ((0, even), (1, odd)):
                pairs.append((device_at(z, y, c), device_at(*to(z, y), c)))
    return lax.ppermute(values, PLANE, pairs)


def shift(values, d):
    return send(values, lambda z, y: (z, y + d), lambda z, y: (z + d, y))


def near_shift(values, d):
    return send(values, lambda z, y: (z + d, y), lambda z, y: (z, y + d))


def gather_classes(block):
    regions, width = block.shape
    flat = block.reshape(regions, width // 128, 128)
    groups = [[j + 4 * k for k in range(4)] for j in range(4)]
    four = lax.all_to_all(
        jnp.broadcast_to(flat, (4,) + flat.shape), "z", 0, 0, axis_index_groups=groups
    )
    return four.reshape(4, regions, width).transpose(1, 0, 2)


def best_means(regions, frames, corpus_ref, clip, rows, count):
    sims = lax.dot_general(
        corpus_ref[clip], rows, (((1,), (1,)), ((), ())), preferred_element_type=jnp.float32
    )
    best = sims[0:frames]
    for j in range(1, regions):
        best = jnp.maximum(best, sims[j * frames : (j + 1) * frames])
    totals = []
    for p in range(rows.shape[0] // (regions * count)):
        total = 0.0
        for i in range(regions):
            at = (p * regions + i) * count
            total = total + best[:, at : at + count]
        totals.append(total * (1.0 / regions))
    return totals


def stacked(refs):
    return jnp.concatenate([ref[...].reshape(-1, ref.shape[-1]) for ref in refs], axis=0)


def sims_body(regions, frames, own_ref, other_ref, *refs):
    out_ref = refs[-1]
    count = refs[0].shape[1]
    rows = stacked(refs[:-1])
    for half, corpus_ref in enumerate((own_ref, other_ref)):
        for clip in range(2):
            at = (half * 2 + clip) * frames
            totals = best_means(regions, frames, corpus_ref, clip, rows, count)
            for p, total in enumerate(totals):
                out_ref[at : at + frames, p * count : (p + 1) * count] = total


def column_places(z, y, c):
    shape = (NZ * NY, NZ * NY)
    col = lax.broadcasted_iota(jnp.int32, shape, 1)
    row = lax.broadcasted_iota(jnp.int32, shape, 0)

    def back(k):
        return jnp.where(k == 2, -1, jnp.where(k == 3, 2, k))

    far, near = back(col // 16), back(col // 4 % 4)
    from_z = (z + NZ - jnp.where(c == 0, near, far)) % 4 + 4 * (col % 4)
    from_y = (y + NY - jnp.where(c == 0, far, near)) % NY
    return jnp.where(from_z * NY + from_y == row, 1.0, 0.0).astype(jnp.bfloat16)


def table_body(regions, frames, at_ref, own_ref, other_ref, prev_ref, *refs):
    out_ref, last_ref = refs[-2:]
    place = column_places(at_ref[0], at_ref[1], at_ref[2])
    sims_body(regions, frames, own_ref, other_ref, *refs[:-2], last_ref)
    prev = prev_ref[...].astype(jnp.bfloat16)
    last = last_ref[...].astype(jnp.bfloat16)
    done = prev.shape[1]
    dims = (((1,), (1,)), ((), ()))
    table = lax.dot_general(
        place[:, :done], prev, dims, preferred_element_type=jnp.float32
    ) + lax.dot_general(place[:, done:], last, dims, preferred_element_type=jnp.float32)
    table = table.astype(jnp.bfloat16)
    out_ref[0 : table.shape[0], :] = table
    out_ref[table.shape[0] :, :] = table


def kernel_call(body, outs, operands, scratch, flops, scalars=0):
    spaces = [pltpu.SMEM] * scalars + [pltpu.VMEM] * (len(operands) - scalars)
    return pl.pallas_call(
        body,
        in_specs=[pl.BlockSpec(memory_space=space) for space in spaces],
        out_specs=[pl.BlockSpec(memory_space=pltpu.VMEM)] * len(outs),
        out_shape=[jax.ShapeDtypeStruct(*out) for out in outs],
        scratch_shapes=scratch,
        compiler_params=pltpu.CompilerParams(vmem_limit_bytes=24 * 2**20),
        cost_estimate=pl.CostEstimate(
            flops=flops,
            bytes_accessed=sum(o.size * o.dtype.itemsize for o in operands),
            transcendentals=0,
        ),
    )(*operands)


def frame_sims(own, other, pieces):
    clips, rows, width = own.shape
    regions, count = pieces[0].shape[:2]
    frames = rows // regions
    total = count * len(pieces)
    body = functools.partial(sims_body, regions, frames)
    flops = 4 * clips * rows * regions * total * width
    outs = [((2 * clips * frames, total), jnp.float32)]
    return kernel_call(body, outs, [own, other, *pieces], [], flops)[0]


def frame_table(at, own, other, prev, pieces):
    clips, rows, width = own.shape
    regions, count = pieces[0].shape[:2]
    frames = rows // regions
    total = count * len(pieces)
    return kernel_call(
        functools.partial(table_body, regions, frames),
        [((NC * NZ * NY, 2 * clips * frames), jnp.bfloat16)],
        [at, own, other, prev, *pieces],
        [pltpu.VMEM((2 * clips * frames, total), jnp.float32)],
        4 * clips * rows * regions * total * width,
        scalars=1,
    )[0]


def row_order():
    group = 4
    order = np.zeros((4, 2, group, 8, NC, NX, group, NY), np.float32)
    for k in range(4):
        for f in range(16):
            frame = 2 * f - 1 + k
            if 0 <= frame < 32:
                for q in range(group):
                    order[k, f % 2, q, f // 2, frame % 2, frame // 8, q, frame % 8 // 2] = 1
    return order.reshape(4 * 64, 128)


def prepare_body(
    at_ref, count_ref, shard_ref, clip_ref, first_ref, second_ref, third_ref, listed_ref, t1_ref, t2_ref, t3_ref
):
    f32, bf16 = jnp.float32, jnp.bfloat16
    group, slots = 4, shard_ref.shape[1]
    chip, core, x = at_ref[0] * NY + at_ref[1], at_ref[2], at_ref[3]
    shards = shard_ref[...]
    names = jnp.where(shards // NC == chip, shards % NC * 2 + clip_ref[...], -1)
    line = lax.broadcasted_iota(jnp.int32, names.shape, 0)
    slot = lax.broadcasted_iota(jnp.int32, (1, slots), 1)
    chips = slots // 4
    to_chip = lax.broadcasted_iota(jnp.int32, (chips, slots), 0)
    of_slot = lax.broadcasted_iota(jnp.int32, (chips, slots), 1)
    pick_slot = lax.broadcasted_iota(jnp.int32, (slots, 2 * group), 0) % 4
    pick_to = lax.broadcasted_iota(jnp.int32, (slots, 2 * group), 1)
    listed = jnp.zeros((chips, 2 * group), f32)
    for q in range(group):
        query = x * group + q
        names_q = jnp.sum(jnp.where(line == query, names, 0), axis=0, keepdims=True)
        names_q = jnp.where(slot < count_ref[query], names_q, -1).astype(f32)
        spread = jnp.where(of_slot // 4 == to_chip, names_q, 0.0).astype(bf16)
        pick = jnp.where((pick_to // 2 == q) & (pick_slot == core * 2 + pick_to % 2), 1.0, 0.0)
        listed = listed + dot(spread, pick.astype(bf16))
    listed_ref[...] = listed.astype(jnp.int32)

    lanes = t1_ref.shape[1]
    row = lax.broadcasted_iota(jnp.int32, (128, lanes), 0) % 32
    lane = lax.broadcasted_iota(jnp.int32, (128, lanes), 1)
    column = (lane // 32) % 16 * 2 + lane // 512
    channel = lax.broadcasted_iota(jnp.int32, (32, lanes), 1) % 32
    each = lax.broadcasted_iota(jnp.int32, (32, lanes), 0)
    taps = dot(first_ref[...], jnp.where(channel == each, 1.0, 0.0).astype(bf16))
    for dy in range(3):
        block = jnp.zeros((128, lanes), f32)
        for dx in range(3):
            tap = taps[dy * 3 + dx : dy * 3 + dx + 1, :]
            block = jnp.where(row == column + (dx - 1), tap, block)
        t1_ref[dy * 128 : (dy + 1) * 128, :] = block.astype(bf16)

    def placed(tap, before, total):
        rows, width = tap.shape
        parts = [jnp.zeros((before, width), f32), tap]
        parts.append(jnp.zeros((total - before - rows, width), f32))
        return jnp.concatenate(parts, axis=0)

    left = lax.broadcasted_iota(jnp.int32, (384, 128), 1) < 64
    for dy in range(3):
        tap = second_ref[dy * 96 : (dy + 1) * 96, :].astype(f32)
        tap = jnp.concatenate([tap, tap], axis=1)
        for odd in range(2):
            one = placed(tap, 96 + 32 * odd, 384)
            two = placed(tap, 160 + 32 * odd, 384)
            block = jnp.where(left, one, two).astype(bf16)
            t2_ref[dy * 384 : (dy + 1) * 384, odd * 128 : (odd + 1) * 128] = block
    for dy in range(3):
        tap = third_ref[dy * 192 : (dy + 1) * 192, :].astype(f32)
        for w in range(2):
            block = placed(tap, 64 + 64 * w, 384).astype(bf16)
            t3_ref[dy * 384 : (dy + 1) * 384, w * 128 : (w + 1) * 128] = block


def prepare(at, cand_count, cand_shard, cand_clip, first_kernel, second_kernel, third_kernel):
    operands = [
        at,
        cand_count,
        cand_shard,
        cand_clip,
        first_kernel.reshape(9, 32),
        second_kernel.reshape(288, 64),
        third_kernel.reshape(576, 128),
    ]
    outs = [
        ((cand_shard.shape[1] // 4, 8), jnp.int32),
        ((384, 1024), jnp.bfloat16),
        ((1152, 256), jnp.bfloat16),
        ((1152, 256), jnp.bfloat16),
    ]
    return kernel_call(prepare_body, outs, operands, [], 10**9, scalars=2)


def dot(a, b):
    return jnp.dot(a, b, preferred_element_type=jnp.float32)


def rows_beside(values):
    rows = values.shape[0]
    at = lax.broadcasted_iota(jnp.int32, values.shape, 0) % 8
    before = jnp.where(at == 0, 0.0, pltpu.roll(values, 1, 0))
    after = jnp.where(at == 7, 0.0, pltpu.roll(values, rows - 1, 0))
    return before, after


def windows(layers, blocks):
    zero = jnp.zeros((layers[0].shape[0], 128), layers[0].dtype)
    out = []
    for t in range(blocks):
        parts = []
        for layer in layers:
            for b in (t - 1, t, t + 1):
                parts.append(layer[:, b * 128 : (b + 1) * 128] if 0 <= b < blocks else zero)
        out.append(jnp.concatenate(parts, axis=1))
    return out


def score_body(
    bias_ref, parts_ref, order_ref, t1_ref, b1_ref, t2_ref, b2_ref, t3_ref, b3_ref, weight_ref, listed_ref, out_ref
):
    b1 = jnp.concatenate([b1_ref[...]] * 16, axis=1)
    b2 = jnp.concatenate([b2_ref[...]] * 2, axis=1)
    b3 = jnp.concatenate([b3_ref[...]] * 2, axis=1)
    weight = jnp.concatenate([weight_ref[...].astype(jnp.float32)] * 2, axis=1)
    lane = lax.broadcasted_iota(jnp.int32, (128, 256), 1) // 128
    even_row = lax.broadcasted_iota(jnp.int32, (128, 256), 0) % 2
    weight = jnp.where(lane == even_row, weight, 0.0).astype(jnp.bfloat16)
    bf16 = jnp.bfloat16
    maps = dot(order_ref[...], parts_ref[...])
    x = [maps[k * 64 : (k + 1) * 64] for k in range(4)]
    x = [(pltpu.roll(v, 64, 1) if k % 2 == 0 else v).astype(bf16) for k, v in enumerate(x)]
    both = jnp.concatenate(
        [jnp.concatenate(x[0:3], axis=1), jnp.concatenate(x[1:4], axis=1)], axis=0
    )
    clip = lax.broadcasted_iota(jnp.int32, both.shape, 1) // 32 % 4
    wide = both.astype(jnp.float32)
    lhs = jnp.concatenate([jnp.where(clip == k, wide, 0.0).astype(bf16) for k in range(4)], axis=0)
    first = dot(lhs, t1_ref[...])
    first = jnp.maximum(first[:, :512], first[:, 512:])
    first = jnp.concatenate(
        [jnp.maximum(first[k * 128 : k * 128 + 64], first[k * 128 + 64 : k * 128 + 128]) for k in range(4)],
        axis=0,
    )
    first = jnp.maximum(first + b1, 0.0)
    even = jnp.concatenate([first[k * 64 : k * 64 + 32] for k in range(4)], axis=0)
    odd = jnp.concatenate([first[k * 64 + 32 : k * 64 + 64] for k in range(4)], axis=0)
    odd_before = rows_beside(odd)[0]
    even_after = rows_beside(even)[1]
    layers = [v.astype(bf16) for v in (odd_before, even, odd, even_after)]
    lhs = jnp.concatenate(windows(layers[0:3], 4) + windows(layers[1:4], 4), axis=0)
    second = dot(lhs, t2_ref[...])
    second = jnp.maximum(second[:, :128], second[:, 128:])
    second = jnp.maximum(second[:512], second[512:])
    second = jnp.maximum(second + b2, 0.0)
    second = jnp.concatenate([second[t * 128 : (t + 1) * 128] for t in range(4)], axis=1)
    before, after = rows_beside(second)
    lhs = jnp.concatenate(windows([v.astype(bf16) for v in (before, second, after)], 4), axis=0)
    third = jnp.maximum(dot(lhs, t3_ref[...]) + b3, 0.0).astype(bf16)
    score = lax.dot_general(
        third, weight, (((1,), (1,)), ((), ())), preferred_element_type=jnp.float32
    )
    score = jnp.maximum(
        jnp.maximum(score[0:128], score[128:256]), jnp.maximum(score[256:384], score[384:512])
    )
    score = jnp.max(score, axis=1, keepdims=True) + jnp.broadcast_to(bias_ref[0], (1, 128))
    score = score.reshape(16, 8, score.shape[1]).sum(axis=1) * 0.125
    listed = listed_ref[...]
    slot_query = lax.broadcasted_iota(jnp.int32, (1, listed.shape[1]), 1) // 2
    total = jnp.zeros(listed.shape, jnp.float32)
    for k in range(4):
        line = jnp.zeros((1, listed.shape[1]), jnp.float32)
        for q in range(4):
            line = jnp.where(slot_query == q, score[k * 4 + q : k * 4 + q + 1, : listed.shape[1]], line)
        total = jnp.where(listed == k, line, total)
    out_ref[...] = total


def slot_scores(parts, listed, spread, first_bias, second_bias, third_bias, score_weight, score_bias):
    operands = [
        score_bias,
        parts,
        jnp.asarray(row_order(), jnp.bfloat16),
        spread[0],
        first_bias[None, :],
        spread[1],
        second_bias[None, :],
        spread[2],
        third_bias[None, :],
        score_weight[None, :],
        listed,
    ]
    outs = [(listed.shape, jnp.float32)]
    return kernel_call(score_body, outs, operands, [], 2 * 10**9, scalars=1)[0]


def on_device(
    queries,
    corpus,
    cand_shard,
    cand_clip,
    cand_count,
    first_kernel,
    first_bias,
    second_kernel,
    second_bias,
    third_kernel,
    third_bias,
    score_weight,
    score_bias,
):
    at = jnp.stack([lax.axis_index(a) for a in ("z", "y", "c", "x")]).astype(jnp.int32)
    clip_dev, frames, regions, width = corpus.shape
    group = cand_shard.shape[0] // NX

    own = corpus.transpose(0, 2, 1, 3).reshape(clip_dev, regions * frames, width)
    four = gather_classes(queries[0, 0])
    ahead = near_shift(four, -1)
    two = near_shift(four, 2)
    behind = near_shift(four, 1)
    kernels = (first_kernel, second_kernel, third_kernel)
    kernels, behind = lax.optimization_barrier((kernels, behind))
    listed, *spread = prepare(at, cand_count, cand_shard, cand_clip, *kernels)
    first = jnp.concatenate([four, behind], axis=1)
    last = jnp.concatenate([ahead, two], axis=1)
    own, listed, first, last = lax.optimization_barrier((own, listed, first, last))
    other = lax.ppermute(own, "c", [(0, 1), (1, 0)])
    behind_first = shift(first, 1)
    ahead_first = shift(first, -1)
    two_first = shift(behind_first, 1)
    behind_last = shift(last, 1)
    ahead_last = shift(last, -1)
    two_last = shift(ahead_last, -1)

    near = [first, last, behind_first, behind_last, ahead_first, ahead_last]
    prev = frame_sims(own, other, near)
    two, prev = lax.optimization_barrier(((two_first, two_last), prev))
    table = frame_table(at, own, other, prev, two)

    parts = lax.all_to_all(table, ("c", "x"), 0, 0, tiled=True)
    values = slot_scores(
        parts, listed, spread, first_bias, second_bias, third_bias, score_weight, score_bias
    )
    values = lax.all_to_all(values, ("z", "y"), 0, 0, tiled=True)
    return values.sum(axis=0).reshape(group, -1)


def solution(mesh):
    devices = mesh.devices.reshape(NZ, NY, NC, NX)
    grid = Mesh(devices, ("z", "y", "c", "x"))
    return jax.shard_map(
        on_device,
        mesh=grid,
        in_specs=(P("x", PLANE), P(PLANE)) + (P(),) * 11,
        out_specs=P("x", PLANE),
        check_vma=False,
    )
```

```python
import functools

import jax
import jax.numpy as jnp
import numpy as np
from jax import lax
from jax.experimental import pallas as pl
from jax.experimental.pallas import tpu as pltpu
from jax.sharding import Mesh
from jax.sharding import PartitionSpec as P

NZ, NY, NC, NX = 16, 4, 2, 4
PLANE = ("z", "y", "c")
CLASS_STEPS = (6, -6, 2, -2)


def device_at(z, y, c):
    return ((z % NZ) * NY + y % NY) * NC + c


def send(values, even, odd):
    pairs = []
    for z in range(NZ):
        for y in range(NY):
            for c, to in ((0, even), (1, odd)):
                pairs.append((device_at(z, y, c), device_at(*to(z, y), c)))
    return lax.ppermute(values, PLANE, pairs)


def shift(values, d):
    return send(values, lambda z, y: (z, y + d), lambda z, y: (z + d, y))


def near_shift(values, d):
    return send(values, lambda z, y: (z + d, y), lambda z, y: (z, y + d))


def gather_classes(block):
    regions, width = block.shape
    flat = block.reshape(regions, width // 128, 128)
    four = [send(flat, lambda z, y: (z + d, y), lambda z, y: (z + d, y)) for d in CLASS_STEPS]
    return jnp.stack([v.reshape(regions, width) for v in four], axis=1)


def best_means(regions, frames, corpus_ref, clip, rows, count):
    sims = lax.dot_general(
        corpus_ref[clip], rows, (((1,), (1,)), ((), ())), preferred_element_type=jnp.float32
    )
    best = sims[0:frames]
    for j in range(1, regions):
        best = jnp.maximum(best, sims[j * frames : (j + 1) * frames])
    totals = []
    for p in range(rows.shape[0] // (regions * count)):
        total = 0.0
        for i in range(regions):
            at = (p * regions + i) * count
            total = total + best[:, at : at + count]
        totals.append(total * (1.0 / regions))
    return totals


def stacked(refs):
    return jnp.concatenate([ref[...].reshape(-1, ref.shape[-1]) for ref in refs], axis=0)


def sims_body(regions, frames, own_ref, other_ref, *refs):
    out_ref = refs[-1]
    count = refs[0].shape[1]
    rows = stacked(refs[:-1])
    for half, corpus_ref in enumerate((own_ref, other_ref)):
        for clip in range(2):
            at = (half * 2 + clip) * frames
            totals = best_means(regions, frames, corpus_ref, clip, rows, count)
            for p, total in enumerate(totals):
                out_ref[at : at + frames, p * count : (p + 1) * count] = total


def column_places(z, y, c):
    shape = (NZ * NY, NZ * NY)
    col = lax.broadcasted_iota(jnp.int32, shape, 1)
    row = lax.broadcasted_iota(jnp.int32, shape, 0)

    def back(k):
        return jnp.where(k == 2, -1, jnp.where(k == 3, 2, k))

    far, step = back(col // 16), col // 4 % 4
    near = jnp.where(step == 1, 2, jnp.where(step == 2, 1, jnp.where(step == 3, -1, 0)))
    far_z = jnp.where((far == 2) & (step >= 2), -2, far)
    kind = col % 4
    first = jnp.where(kind < 2, 6, 2) * (1 - kind % 2 * 2)
    from_z = (z + NZ - jnp.where(c == 0, near, far_z) - first) % NZ
    from_y = (y + NY - jnp.where(c == 0, far, near)) % NY
    return jnp.where(from_z * NY + from_y == row, 1.0, 0.0).astype(jnp.bfloat16)


def table_body(regions, frames, at_ref, own_ref, other_ref, prev_ref, *refs):
    out_ref, last_ref = refs[-2:]
    place = column_places(at_ref[0], at_ref[1], at_ref[2])
    sims_body(regions, frames, own_ref, other_ref, *refs[:-2], last_ref)
    prev = prev_ref[...].astype(jnp.bfloat16)
    last = last_ref[...].astype(jnp.bfloat16)
    done = prev.shape[1]
    dims = (((1,), (1,)), ((), ()))
    table = lax.dot_general(
        place[:, :done], prev, dims, preferred_element_type=jnp.float32
    ) + lax.dot_general(place[:, done:], last, dims, preferred_element_type=jnp.float32)
    table = table.astype(jnp.bfloat16)
    out_ref[0 : table.shape[0], :] = table
    out_ref[table.shape[0] :, :] = table


def kernel_call(body, outs, operands, scratch, flops, scalars=0):
    spaces = [pltpu.SMEM] * scalars + [pltpu.VMEM] * (len(operands) - scalars)
    return pl.pallas_call(
        body,
        in_specs=[pl.BlockSpec(memory_space=space) for space in spaces],
        out_specs=[pl.BlockSpec(memory_space=pltpu.VMEM)] * len(outs),
        out_shape=[jax.ShapeDtypeStruct(*out) for out in outs],
        scratch_shapes=scratch,
        compiler_params=pltpu.CompilerParams(vmem_limit_bytes=24 * 2**20),
        cost_estimate=pl.CostEstimate(
            flops=flops,
            bytes_accessed=sum(o.size * o.dtype.itemsize for o in operands),
            transcendentals=0,
        ),
    )(*operands)


def frame_sims(own, other, pieces):
    clips, rows, width = own.shape
    regions, count = pieces[0].shape[:2]
    frames = rows // regions
    total = count * len(pieces)
    body = functools.partial(sims_body, regions, frames)
    flops = 4 * clips * rows * regions * total * width
    outs = [((2 * clips * frames, total), jnp.float32)]
    return kernel_call(body, outs, [own, other, *pieces], [], flops)[0]


def frame_table(at, own, other, prev, pieces):
    clips, rows, width = own.shape
    regions, count = pieces[0].shape[:2]
    frames = rows // regions
    total = count * len(pieces)
    return kernel_call(
        functools.partial(table_body, regions, frames),
        [((NC * NZ * NY, 2 * clips * frames), jnp.bfloat16)],
        [at, own, other, prev, *pieces],
        [pltpu.VMEM((2 * clips * frames, total), jnp.float32)],
        4 * clips * rows * regions * total * width,
        scalars=1,
    )[0]


def row_order():
    group = 4
    order = np.zeros((4, 2, group, 8, NC, NX, group, NY), np.float32)
    for k in range(4):
        for f in range(16):
            frame = 2 * f - 1 + k
            if 0 <= frame < 32:
                for q in range(group):
                    order[k, f % 2, q, f // 2, frame % 2, frame // 8, q, frame % 8 // 2] = 1
    return order.reshape(4 * 64, 128)


def prepare_body(
    at_ref, count_ref, shard_ref, clip_ref, first_ref, second_ref, third_ref, listed_ref, t1_ref, t2_ref, t3_ref
):
    f32, bf16 = jnp.float32, jnp.bfloat16
    group, slots = 4, shard_ref.shape[1]
    chip, core, x = at_ref[0] * NY + at_ref[1], at_ref[2], at_ref[3]
    shards = shard_ref[...]
    names = jnp.where(shards // NC == chip, shards % NC * 2 + clip_ref[...], -1)
    line = lax.broadcasted_iota(jnp.int32, names.shape, 0)
    slot = lax.broadcasted_iota(jnp.int32, (1, slots), 1)
    chips = slots // 4
    to_chip = lax.broadcasted_iota(jnp.int32, (chips, slots), 0)
    of_slot = lax.broadcasted_iota(jnp.int32, (chips, slots), 1)
    pick_slot = lax.broadcasted_iota(jnp.int32, (slots, 2 * group), 0) % 4
    pick_to = lax.broadcasted_iota(jnp.int32, (slots, 2 * group), 1)
    listed = jnp.zeros((chips, 2 * group), f32)
    for q in range(group):
        query = x * group + q
        names_q = jnp.sum(jnp.where(line == query, names, 0), axis=0, keepdims=True)
        names_q = jnp.where(slot < count_ref[query], names_q, -1).astype(f32)
        spread = jnp.where(of_slot // 4 == to_chip, names_q, 0.0).astype(bf16)
        pick = jnp.where((pick_to // 2 == q) & (pick_slot == core * 2 + pick_to % 2), 1.0, 0.0)
        listed = listed + dot(spread, pick.astype(bf16))
    listed_ref[...] = listed.astype(jnp.int32)

    lanes = t1_ref.shape[1]
    row = lax.broadcasted_iota(jnp.int32, (128, lanes), 0) % 32
    lane = lax.broadcasted_iota(jnp.int32, (128, lanes), 1)
    column = (lane // 32) % 16 * 2 + lane // 512
    channel = lax.broadcasted_iota(jnp.int32, (32, lanes), 1) % 32
    each = lax.broadcasted_iota(jnp.int32, (32, lanes), 0)
    taps = dot(first_ref[...], jnp.where(channel == each, 1.0, 0.0).astype(bf16))
    for dy in range(3):
        block = jnp.zeros((128, lanes), f32)
        for dx in range(3):
            tap = taps[dy * 3 + dx : dy * 3 + dx + 1, :]
            block = jnp.where(row == column + (dx - 1), tap, block)
        t1_ref[dy * 128 : (dy + 1) * 128, :] = block.astype(bf16)

    def placed(tap, before, total):
        rows, width = tap.shape
        parts = [jnp.zeros((before, width), f32), tap]
        parts.append(jnp.zeros((total - before - rows, width), f32))
        return jnp.concatenate(parts, axis=0)

    left = lax.broadcasted_iota(jnp.int32, (384, 128), 1) < 64
    for dy in range(3):
        tap = second_ref[dy * 96 : (dy + 1) * 96, :].astype(f32)
        tap = jnp.concatenate([tap, tap], axis=1)
        for odd in range(2):
            one = placed(tap, 96 + 32 * odd, 384)
            two = placed(tap, 160 + 32 * odd, 384)
            block = jnp.where(left, one, two).astype(bf16)
            t2_ref[dy * 384 : (dy + 1) * 384, odd * 128 : (odd + 1) * 128] = block
    for dy in range(3):
        tap = third_ref[dy * 192 : (dy + 1) * 192, :].astype(f32)
        for w in range(2):
            block = placed(tap, 64 + 64 * w, 384).astype(bf16)
            t3_ref[dy * 384 : (dy + 1) * 384, w * 128 : (w + 1) * 128] = block


def prepare(at, cand_count, cand_shard, cand_clip, first_kernel, second_kernel, third_kernel):
    operands = [
        at,
        cand_count,
        cand_shard,
        cand_clip,
        first_kernel.reshape(9, 32),
        second_kernel.reshape(288, 64),
        third_kernel.reshape(576, 128),
    ]
    outs = [
        ((cand_shard.shape[1] // 4, 8), jnp.int32),
        ((384, 1024), jnp.bfloat16),
        ((1152, 256), jnp.bfloat16),
        ((1152, 256), jnp.bfloat16),
    ]
    return kernel_call(prepare_body, outs, operands, [], 10**9, scalars=2)


def dot(a, b):
    return jnp.dot(a, b, preferred_element_type=jnp.float32)


def rows_beside(values):
    rows = values.shape[0]
    at = lax.broadcasted_iota(jnp.int32, values.shape, 0) % 8
    before = jnp.where(at == 0, 0.0, pltpu.roll(values, 1, 0))
    after = jnp.where(at == 7, 0.0, pltpu.roll(values, rows - 1, 0))
    return before, after


def windows(layers, blocks):
    zero = jnp.zeros((layers[0].shape[0], 128), layers[0].dtype)
    out = []
    for t in range(blocks):
        parts = []
        for layer in layers:
            for b in (t - 1, t, t + 1):
                parts.append(layer[:, b * 128 : (b + 1) * 128] if 0 <= b < blocks else zero)
        out.append(jnp.concatenate(parts, axis=1))
    return out


def score_body(
    bias_ref, parts_ref, order_ref, t1_ref, b1_ref, t2_ref, b2_ref, t3_ref, b3_ref, weight_ref, listed_ref, out_ref
):
    b1 = jnp.concatenate([b1_ref[...]] * 16, axis=1)
    b2 = jnp.concatenate([b2_ref[...]] * 2, axis=1)
    b3 = jnp.concatenate([b3_ref[...]] * 2, axis=1)
    weight = jnp.concatenate([weight_ref[...].astype(jnp.float32)] * 2, axis=1)
    lane = lax.broadcasted_iota(jnp.int32, (128, 256), 1) // 128
    even_row = lax.broadcasted_iota(jnp.int32, (128, 256), 0) % 2
    weight = jnp.where(lane == even_row, weight, 0.0).astype(jnp.bfloat16)
    bf16 = jnp.bfloat16
    maps = dot(order_ref[...], parts_ref[...])
    x = [maps[k * 64 : (k + 1) * 64] for k in range(4)]
    x = [(pltpu.roll(v, 64, 1) if k % 2 == 0 else v).astype(bf16) for k, v in enumerate(x)]
    both = jnp.concatenate(
        [jnp.concatenate(x[0:3], axis=1), jnp.concatenate(x[1:4], axis=1)], axis=0
    )
    clip = lax.broadcasted_iota(jnp.int32, both.shape, 1) // 32 % 4
    wide = both.astype(jnp.float32)
    lhs = jnp.concatenate([jnp.where(clip == k, wide, 0.0).astype(bf16) for k in range(4)], axis=0)
    first = dot(lhs, t1_ref[...])
    first = jnp.maximum(first[:, :512], first[:, 512:])
    first = jnp.concatenate(
        [jnp.maximum(first[k * 128 : k * 128 + 64], first[k * 128 + 64 : k * 128 + 128]) for k in range(4)],
        axis=0,
    )
    first = jnp.maximum(first + b1, 0.0)
    even = jnp.concatenate([first[k * 64 : k * 64 + 32] for k in range(4)], axis=0)
    odd = jnp.concatenate([first[k * 64 + 32 : k * 64 + 64] for k in range(4)], axis=0)
    odd_before = rows_beside(odd)[0]
    even_after = rows_beside(even)[1]
    layers = [v.astype(bf16) for v in (odd_before, even, odd, even_after)]
    lhs = jnp.concatenate(windows(layers[0:3], 4) + windows(layers[1:4], 4), axis=0)
    second = dot(lhs, t2_ref[...])
    second = jnp.maximum(second[:, :128], second[:, 128:])
    second = jnp.maximum(second[:512], second[512:])
    second = jnp.maximum(second + b2, 0.0)
    second = jnp.concatenate([second[t * 128 : (t + 1) * 128] for t in range(4)], axis=1)
    before, after = rows_beside(second)
    lhs = jnp.concatenate(windows([v.astype(bf16) for v in (before, second, after)], 4), axis=0)
    third = jnp.maximum(dot(lhs, t3_ref[...]) + b3, 0.0).astype(bf16)
    score = lax.dot_general(
        third, weight, (((1,), (1,)), ((), ())), preferred_element_type=jnp.float32
    )
    score = jnp.maximum(
        jnp.maximum(score[0:128], score[128:256]), jnp.maximum(score[256:384], score[384:512])
    )
    score = jnp.max(score, axis=1, keepdims=True) + jnp.broadcast_to(bias_ref[0], (1, 128))
    score = score.reshape(16, 8, score.shape[1]).sum(axis=1) * 0.125
    listed = listed_ref[...]
    slot_query = lax.broadcasted_iota(jnp.int32, (1, listed.shape[1]), 1) // 2
    total = jnp.zeros(listed.shape, jnp.float32)
    for k in range(4):
        line = jnp.zeros((1, listed.shape[1]), jnp.float32)
        for q in range(4):
            line = jnp.where(slot_query == q, score[k * 4 + q : k * 4 + q + 1, : listed.shape[1]], line)
        total = jnp.where(listed == k, line, total)
    out_ref[...] = total


def slot_scores(parts, listed, spread, first_bias, second_bias, third_bias, score_weight, score_bias):
    operands = [
        score_bias,
        parts,
        jnp.asarray(row_order(), jnp.bfloat16),
        spread[0],
        first_bias[None, :],
        spread[1],
        second_bias[None, :],
        spread[2],
        third_bias[None, :],
        score_weight[None, :],
        listed,
    ]
    outs = [(listed.shape, jnp.float32)]
    return kernel_call(score_body, outs, operands, [], 2 * 10**9, scalars=1)[0]


def on_device(
    queries,
    corpus,
    cand_shard,
    cand_clip,
    cand_count,
    first_kernel,
    first_bias,
    second_kernel,
    second_bias,
    third_kernel,
    third_bias,
    score_weight,
    score_bias,
):
    at = jnp.stack([lax.axis_index(a) for a in ("z", "y", "c", "x")]).astype(jnp.int32)
    clip_dev, frames, regions, width = corpus.shape
    group = cand_shard.shape[0] // NX

    own = corpus.transpose(0, 2, 1, 3).reshape(clip_dev, regions * frames, width)
    four = gather_classes(queries[0, 0])
    ahead = near_shift(four, -1)
    two = near_shift(four, 2)
    behind = near_shift(four, 1)
    kernels = (first_kernel, second_kernel, third_kernel)
    kernels, two = lax.optimization_barrier((kernels, two))
    listed, *spread = prepare(at, cand_count, cand_shard, cand_clip, *kernels)
    first = jnp.concatenate([four, two], axis=1)
    last = jnp.concatenate([behind, ahead], axis=1)
    own, listed, first, last = lax.optimization_barrier((own, listed, first, last))
    other = lax.ppermute(own, "c", [(0, 1), (1, 0)])
    behind_first = shift(first, 1)
    ahead_first = shift(first, -1)
    two_first = shift(behind_first, 1)
    behind_last = shift(last, 1)
    ahead_last = shift(last, -1)
    two_last = shift(ahead_last, -1)

    near = [first, last, behind_first, behind_last, ahead_first, ahead_last]
    prev = frame_sims(own, other, near)
    two, prev = lax.optimization_barrier(((two_first, two_last), prev))
    table = frame_table(at, own, other, prev, two)

    parts = lax.all_to_all(table, ("c", "x"), 0, 0, tiled=True)
    values = slot_scores(
        parts, listed, spread, first_bias, second_bias, third_bias, score_weight, score_bias
    )
    values = lax.all_to_all(values, ("z", "y"), 0, 0, tiled=True)
    return values.sum(axis=0).reshape(group, -1)


def solution(mesh):
    devices = mesh.devices.reshape(NZ, NY, NC, NX)
    grid = Mesh(devices, ("z", "y", "c", "x"))
    return jax.shard_map(
        on_device,
        mesh=grid,
        in_specs=(P("x", PLANE), P(PLANE)) + (P(),) * 11,
        out_specs=P("x", PLANE),
        check_vma=False,
    )
```

```python
import functools

import jax
import jax.numpy as jnp
import numpy as np
from jax import lax
from jax.experimental import pallas as pl
from jax.experimental.pallas import tpu as pltpu
from jax.sharding import Mesh
from jax.sharding import PartitionSpec as P

NZ, NY, NC, NX = 16, 4, 2, 4
PLANE = ("z", "y", "c")
CLASS_STEPS = (6, 2)


def device_at(z, y, c):
    return ((z % NZ) * NY + y % NY) * NC + c


def send(values, even, odd):
    pairs = []
    for z in range(NZ):
        for y in range(NY):
            for c, to in ((0, even), (1, odd)):
                pairs.append((device_at(z, y, c), device_at(*to(z, y), c)))
    return lax.ppermute(values, PLANE, pairs)


def shift(values, d):
    return send(values, lambda z, y: (z, y + d), lambda z, y: (z + d, y))


def near_shift(values, d):
    return send(values, lambda z, y: (z + d, y), lambda z, y: (z, y + d))


def gather_classes(block):
    regions, width = block.shape
    flat = block.reshape(regions, width // 128, 128)
    other = lax.ppermute(flat, "c", [(0, 1), (1, 0)])
    both = jnp.stack([flat, other])
    four = [send(both, lambda z, y: (z + d, y), lambda z, y: (z - d, y)) for d in CLASS_STEPS]
    return jnp.concatenate(four, axis=0).reshape(4, regions, width).transpose(1, 0, 2)


def best_means(regions, frames, corpus_ref, clip, rows, count):
    sims = lax.dot_general(
        corpus_ref[clip], rows, (((1,), (1,)), ((), ())), preferred_element_type=jnp.float32
    )
    best = sims[0:frames]
    for j in range(1, regions):
        best = jnp.maximum(best, sims[j * frames : (j + 1) * frames])
    totals = []
    for p in range(rows.shape[0] // (regions * count)):
        total = 0.0
        for i in range(regions):
            at = (p * regions + i) * count
            total = total + best[:, at : at + count]
        totals.append(total * (1.0 / regions))
    return totals


def stacked(refs):
    return jnp.concatenate([ref[...].reshape(-1, ref.shape[-1]) for ref in refs], axis=0)


def sims_body(regions, frames, own_ref, other_ref, *refs):
    out_ref = refs[-1]
    count = refs[0].shape[1]
    rows = stacked(refs[:-1])
    for half, corpus_ref in enumerate((own_ref, other_ref)):
        for clip in range(2):
            at = (half * 2 + clip) * frames
            totals = best_means(regions, frames, corpus_ref, clip, rows, count)
            for p, total in enumerate(totals):
                out_ref[at : at + frames, p * count : (p + 1) * count] = total


def column_places(z, y, c):
    shape = (2 * NZ * NY, NZ * NY)
    col = lax.broadcasted_iota(jnp.int32, shape, 1)
    row = lax.broadcasted_iota(jnp.int32, shape, 0)
    far, step = col // 16, col // 4 % 4
    far = jnp.where(far == 2, -1, jnp.where(far == 3, 2, far))
    near = jnp.where(step == 1, 2, jnp.where(step == 2, 1, jnp.where(step == 3, -1, 0)))
    first = jnp.where(col % 4 < 2, 6, 2)
    from_z = jnp.where(c == 0, z - near - first, z - far + first)
    from_y = jnp.where(c == 0, y - far, y - near)
    parity = (c + col % 2) % 2
    place = ((from_z + NZ) % NZ * NY + (from_y + NY) % NY) * 2 + parity
    return jnp.where(place == row, 1.0, 0.0).astype(jnp.bfloat16)


def table_body(regions, frames, at_ref, own_ref, other_ref, prev_ref, *refs):
    out_ref, last_ref = refs[-2:]
    place = column_places(at_ref[0], at_ref[1], at_ref[2])
    sims_body(regions, frames, own_ref, other_ref, *refs[:-2], last_ref)
    prev = prev_ref[...].astype(jnp.bfloat16)
    last = last_ref[...].astype(jnp.bfloat16)
    done = prev.shape[1]
    dims = (((1,), (1,)), ((), ()))
    table = lax.dot_general(
        place[:, :done], prev, dims, preferred_element_type=jnp.float32
    ) + lax.dot_general(place[:, done:], last, dims, preferred_element_type=jnp.float32)
    table = table.astype(jnp.bfloat16)
    out_ref[0 : table.shape[0], :] = table
    out_ref[table.shape[0] :, :] = table


def kernel_call(body, outs, operands, scratch, flops, scalars=0):
    spaces = [pltpu.SMEM] * scalars + [pltpu.VMEM] * (len(operands) - scalars)
    return pl.pallas_call(
        body,
        in_specs=[pl.BlockSpec(memory_space=space) for space in spaces],
        out_specs=[pl.BlockSpec(memory_space=pltpu.VMEM)] * len(outs),
        out_shape=[jax.ShapeDtypeStruct(*out) for out in outs],
        scratch_shapes=scratch,
        compiler_params=pltpu.CompilerParams(vmem_limit_bytes=24 * 2**20),
        cost_estimate=pl.CostEstimate(
            flops=flops,
            bytes_accessed=sum(o.size * o.dtype.itemsize for o in operands),
            transcendentals=0,
        ),
    )(*operands)


def frame_sims(own, other, pieces):
    clips, rows, width = own.shape
    regions, count = pieces[0].shape[:2]
    frames = rows // regions
    total = count * len(pieces)
    body = functools.partial(sims_body, regions, frames)
    flops = 4 * clips * rows * regions * total * width
    outs = [((2 * clips * frames, total), jnp.float32)]
    return kernel_call(body, outs, [own, other, *pieces], [], flops)[0]


def frame_table(at, own, other, prev, pieces):
    clips, rows, width = own.shape
    regions, count = pieces[0].shape[:2]
    frames = rows // regions
    total = count * len(pieces)
    return kernel_call(
        functools.partial(table_body, regions, frames),
        [((2 * NC * NZ * NY, 2 * clips * frames), jnp.bfloat16)],
        [at, own, other, prev, *pieces],
        [pltpu.VMEM((2 * clips * frames, total), jnp.float32)],
        4 * clips * rows * regions * total * width,
        scalars=1,
    )[0]


def row_order():
    group = 4
    order = np.zeros((4, 2, group, 8, NX, group, NY, 2), np.float32)
    for k in range(4):
        for f in range(16):
            frame = 2 * f - 1 + k
            if 0 <= frame < 32:
                for q in range(group):
                    order[k, f % 2, q, f // 2, frame // 8, q, frame % 8 // 2, frame % 2] = 1
    return order.reshape(4 * 64, 128)


def prepare_body(
    at_ref, count_ref, shard_ref, clip_ref, first_ref, second_ref, third_ref, listed_ref, t1_ref, t2_ref, t3_ref
):
    f32, bf16 = jnp.float32, jnp.bfloat16
    group, slots = 4, shard_ref.shape[1]
    chip, core, x = at_ref[0] * NY + at_ref[1], at_ref[2], at_ref[3]
    shards = shard_ref[...]
    names = jnp.where(shards // NC == chip, shards % NC * 2 + clip_ref[...], -1)
    line = lax.broadcasted_iota(jnp.int32, names.shape, 0)
    slot = lax.broadcasted_iota(jnp.int32, (1, slots), 1)
    chips = slots // 4
    to_chip = lax.broadcasted_iota(jnp.int32, (chips, slots), 0)
    of_slot = lax.broadcasted_iota(jnp.int32, (chips, slots), 1)
    pick_slot = lax.broadcasted_iota(jnp.int32, (slots, 2 * group), 0) % 4
    pick_to = lax.broadcasted_iota(jnp.int32, (slots, 2 * group), 1)
    listed = jnp.zeros((chips, 2 * group), f32)
    for q in range(group):
        query = x * group + q
        names_q = jnp.sum(jnp.where(line == query, names, 0), axis=0, keepdims=True)
        names_q = jnp.where(slot < count_ref[query], names_q, -1).astype(f32)
        spread = jnp.where(of_slot // 4 == to_chip, names_q, 0.0).astype(bf16)
        pick = jnp.where((pick_to % group == q) & (pick_slot == core * 2 + pick_to // group), 1.0, 0.0)
        listed = listed + dot(spread, pick.astype(bf16))
    listed_ref[...] = listed.astype(jnp.int32)

    lanes = t1_ref.shape[1]
    row = lax.broadcasted_iota(jnp.int32, (128, lanes), 0) % 32
    lane = lax.broadcasted_iota(jnp.int32, (128, lanes), 1)
    column = (lane // 32) % 16 * 2 + lane // 512
    channel = lax.broadcasted_iota(jnp.int32, (32, lanes), 1) % 32
    each = lax.broadcasted_iota(jnp.int32, (32, lanes), 0)
    taps = dot(first_ref[...], jnp.where(channel == each, 1.0, 0.0).astype(bf16))
    for dy in range(3):
        block = jnp.zeros((128, lanes), f32)
        for dx in range(3):
            tap = taps[dy * 3 + dx : dy * 3 + dx + 1, :]
            block = jnp.where(row == column + (dx - 1), tap, block)
        t1_ref[dy * 128 : (dy + 1) * 128, :] = block.astype(bf16)

    def placed(tap, before, total):
        rows, width = tap.shape
        parts = [jnp.zeros((before, width), f32), tap]
        parts.append(jnp.zeros((total - before - rows, width), f32))
        return jnp.concatenate(parts, axis=0)

    left = lax.broadcasted_iota(jnp.int32, (384, 128), 1) < 64
    for dy in range(3):
        tap = second_ref[dy * 96 : (dy + 1) * 96, :].astype(f32)
        tap = jnp.concatenate([tap, tap], axis=1)
        for odd in range(2):
            one = placed(tap, 96 + 32 * odd, 384)
            two = placed(tap, 160 + 32 * odd, 384)
            block = jnp.where(left, one, two).astype(bf16)
            t2_ref[dy * 384 : (dy + 1) * 384, odd * 128 : (odd + 1) * 128] = block
    for dy in range(3):
        tap = third_ref[dy * 192 : (dy + 1) * 192, :].astype(f32)
        for w in range(2):
            block = placed(tap, 64 + 64 * w, 384).astype(bf16)
            t3_ref[dy * 384 : (dy + 1) * 384, w * 128 : (w + 1) * 128] = block


def prepare(at, cand_count, cand_shard, cand_clip, first_kernel, second_kernel, third_kernel):
    operands = [
        at,
        cand_count,
        cand_shard,
        cand_clip,
        first_kernel.reshape(9, 32),
        second_kernel.reshape(288, 64),
        third_kernel.reshape(576, 128),
    ]
    outs = [
        ((cand_shard.shape[1] // 4, 8), jnp.int32),
        ((384, 1024), jnp.bfloat16),
        ((1152, 256), jnp.bfloat16),
        ((1152, 256), jnp.bfloat16),
    ]
    return kernel_call(prepare_body, outs, operands, [], 10**9, scalars=2)


def dot(a, b):
    return jnp.dot(a, b, preferred_element_type=jnp.float32)


def rows_beside(values):
    rows = values.shape[0]
    at = lax.broadcasted_iota(jnp.int32, values.shape, 0) % 8
    before = jnp.where(at == 0, 0.0, pltpu.roll(values, 1, 0))
    after = jnp.where(at == 7, 0.0, pltpu.roll(values, rows - 1, 0))
    return before, after


def windows(layers, blocks):
    zero = jnp.zeros((layers[0].shape[0], 128), layers[0].dtype)
    out = []
    for t in range(blocks):
        parts = []
        for layer in layers:
            for b in (t - 1, t, t + 1):
                parts.append(layer[:, b * 128 : (b + 1) * 128] if 0 <= b < blocks else zero)
        out.append(jnp.concatenate(parts, axis=1))
    return out


def score_body(
    bias_ref, parts_ref, order_ref, t1_ref, b1_ref, t2_ref, b2_ref, t3_ref, b3_ref, weight_ref, listed_ref, out_ref
):
    b1 = jnp.concatenate([b1_ref[...]] * 16, axis=1)
    b2 = jnp.concatenate([b2_ref[...]] * 2, axis=1)
    b3 = jnp.concatenate([b3_ref[...]] * 2, axis=1)
    weight = jnp.concatenate([weight_ref[...].astype(jnp.float32)] * 2, axis=1)
    lane = lax.broadcasted_iota(jnp.int32, (128, 256), 1) // 128
    even_row = lax.broadcasted_iota(jnp.int32, (128, 256), 0) % 2
    weight = jnp.where(lane == even_row, weight, 0.0).astype(jnp.bfloat16)
    bf16 = jnp.bfloat16
    parts = parts_ref[...].astype(jnp.float32)
    half = parts.shape[0] // 2
    parts = (parts[:half] + pltpu.roll(parts[half:], 64, 1)).astype(bf16)
    maps = dot(order_ref[...], parts)
    x = [maps[k * 64 : (k + 1) * 64].astype(bf16) for k in range(4)]
    both = jnp.concatenate(
        [jnp.concatenate(x[0:3], axis=1), jnp.concatenate(x[1:4], axis=1)], axis=0
    )
    clip = lax.broadcasted_iota(jnp.int32, both.shape, 1) // 32 % 4
    wide = both.astype(jnp.float32)
    lhs = jnp.concatenate([jnp.where(clip == k, wide, 0.0).astype(bf16) for k in range(4)], axis=0)
    first = dot(lhs, t1_ref[...])
    first = jnp.maximum(first[:, :512], first[:, 512:])
    first = jnp.concatenate(
        [jnp.maximum(first[k * 128 : k * 128 + 64], first[k * 128 + 64 : k * 128 + 128]) for k in range(4)],
        axis=0,
    )
    first = jnp.maximum(first + b1, 0.0)
    even = jnp.concatenate([first[k * 64 : k * 64 + 32] for k in range(4)], axis=0)
    odd = jnp.concatenate([first[k * 64 + 32 : k * 64 + 64] for k in range(4)], axis=0)
    odd_before = rows_beside(odd)[0]
    even_after = rows_beside(even)[1]
    layers = [v.astype(bf16) for v in (odd_before, even, odd, even_after)]
    lhs = jnp.concatenate(windows(layers[0:3], 4) + windows(layers[1:4], 4), axis=0)
    second = dot(lhs, t2_ref[...])
    second = jnp.maximum(second[:, :128], second[:, 128:])
    second = jnp.maximum(second[:512], second[512:])
    second = jnp.maximum(second + b2, 0.0)
    second = jnp.concatenate([second[t * 128 : (t + 1) * 128] for t in range(4)], axis=1)
    before, after = rows_beside(second)
    lhs = jnp.concatenate(windows([v.astype(bf16) for v in (before, second, after)], 4), axis=0)
    third = jnp.maximum(dot(lhs, t3_ref[...]) + b3, 0.0).astype(bf16)
    score = lax.dot_general(
        third, weight, (((1,), (1,)), ((), ())), preferred_element_type=jnp.float32
    )
    score = jnp.maximum(
        jnp.maximum(score[0:128], score[128:256]), jnp.maximum(score[256:384], score[384:512])
    )
    score = jnp.max(score, axis=1, keepdims=True) + jnp.broadcast_to(bias_ref[0], (1, 128))
    score = score.reshape(16, 8, score.shape[1]).sum(axis=1) * 0.125
    listed = listed_ref[...]
    slot_query = lax.broadcasted_iota(jnp.int32, (1, listed.shape[1]), 1) % 4
    total = jnp.zeros(listed.shape, jnp.float32)
    for k in range(4):
        line = jnp.zeros((1, listed.shape[1]), jnp.float32)
        for q in range(4):
            line = jnp.where(slot_query == q, score[k * 4 + q : k * 4 + q + 1, : listed.shape[1]], line)
        total = jnp.where(listed == k, line, total)
    out_ref[...] = total


def slot_scores(parts, listed, spread, first_bias, second_bias, third_bias, score_weight, score_bias):
    operands = [
        score_bias,
        parts,
        jnp.asarray(row_order(), jnp.bfloat16),
        spread[0],
        first_bias[None, :],
        spread[1],
        second_bias[None, :],
        spread[2],
        third_bias[None, :],
        score_weight[None, :],
        listed,
    ]
    outs = [(listed.shape, jnp.float32)]
    return kernel_call(score_body, outs, operands, [], 2 * 10**9, scalars=1)[0]


def on_device(
    queries,
    corpus,
    cand_shard,
    cand_clip,
    cand_count,
    first_kernel,
    first_bias,
    second_kernel,
    second_bias,
    third_kernel,
    third_bias,
    score_weight,
    score_bias,
):
    at = jnp.stack([lax.axis_index(a) for a in ("z", "y", "c", "x")]).astype(jnp.int32)
    clip_dev, frames, regions, width = corpus.shape
    group = cand_shard.shape[0] // NX

    own = corpus.transpose(0, 2, 1, 3).reshape(clip_dev, regions * frames, width)
    four = gather_classes(queries[0, 0])
    ahead = near_shift(four, -1)
    two = near_shift(four, 2)
    behind = near_shift(four, 1)
    kernels = (first_kernel, second_kernel, third_kernel)
    kernels, two = lax.optimization_barrier((kernels, two))
    listed, *spread = prepare(at, cand_count, cand_shard, cand_clip, *kernels)
    first = jnp.concatenate([four, two], axis=1)
    last = jnp.concatenate([behind, ahead], axis=1)
    own, listed, first, last = lax.optimization_barrier((own, listed, first, last))
    other = lax.ppermute(own, "c", [(0, 1), (1, 0)])
    behind_first = shift(first, 1)
    ahead_first = shift(first, -1)
    two_first = shift(behind_first, 1)
    behind_last = shift(last, 1)
    ahead_last = shift(last, -1)
    two_last = shift(behind_last, 1)

    near = [first, last, behind_first, behind_last, ahead_first, ahead_last]
    prev = frame_sims(own, other, near)
    two, prev = lax.optimization_barrier(((two_first, two_last), prev))
    table = frame_table(at, own, other, prev, two)

    parts = lax.all_to_all(table, ("c", "x"), 0, 0, tiled=True)
    values = slot_scores(
        parts, listed, spread, first_bias, second_bias, third_bias, score_weight, score_bias
    )
    values = lax.all_to_all(values, ("z", "y"), 0, 0, tiled=True)
    return values.sum(axis=0).reshape(-1, group).T


def solution(mesh):
    devices = mesh.devices.reshape(NZ, NY, NC, NX)
    grid = Mesh(devices, ("z", "y", "c", "x"))
    return jax.shard_map(
        on_device,
        mesh=grid,
        in_specs=(P("x", PLANE), P(PLANE)) + (P(),) * 11,
        out_specs=P("x", PLANE),
        check_vma=False,
    )
```

```python
import functools

import jax
import jax.numpy as jnp
import numpy as np
from jax import lax
from jax.experimental import pallas as pl
from jax.experimental.pallas import tpu as pltpu
from jax.sharding import Mesh
from jax.sharding import PartitionSpec as P

NZ, NY, NC, NX = 16, 4, 2, 4
PLANE = ("z", "y", "c")
CLASS_STEPS = (6, 2)


def device_at(z, y, c):
    return ((z % NZ) * NY + y % NY) * NC + c


def send(values, even, odd):
    pairs = []
    for z in range(NZ):
        for y in range(NY):
            for c, to in ((0, even), (1, odd)):
                pairs.append((device_at(z, y, c), device_at(*to(z, y), c)))
    return lax.ppermute(values, PLANE, pairs)


def shift(values, d):
    return send(values, lambda z, y: (z, y + d), lambda z, y: (z + d, y))


def near_shift(values, d):
    return send(values, lambda z, y: (z + d, y), lambda z, y: (z, y + d))


def gather_classes(block):
    other = lax.ppermute(block, "c", [(0, 1), (1, 0)])
    both = jnp.stack([block, other], axis=1)
    four = [send(both, lambda z, y: (z + d, y), lambda z, y: (z - d, y)) for d in CLASS_STEPS]
    return jnp.concatenate(four, axis=1)


def best_means(regions, frames, corpus_ref, clip, rows, count):
    sims = lax.dot_general(
        corpus_ref[clip], rows, (((1,), (1,)), ((), ())), preferred_element_type=jnp.float32
    )
    best = sims[0:frames]
    for j in range(1, regions):
        best = jnp.maximum(best, sims[j * frames : (j + 1) * frames])
    totals = []
    for p in range(rows.shape[0] // (regions * count)):
        total = 0.0
        for i in range(regions):
            at = (p * regions + i) * count
            total = total + best[:, at : at + count]
        totals.append(total * (1.0 / regions))
    return totals


def stacked(refs):
    return jnp.concatenate([ref[...].reshape(-1, ref.shape[-1]) for ref in refs], axis=0)


def sims_body(regions, frames, own_ref, other_ref, *refs):
    out_ref = refs[-1]
    count = refs[0].shape[1]
    rows = stacked(refs[:-1])
    for half, corpus_ref in enumerate((own_ref, other_ref)):
        for clip in range(2):
            at = (half * 2 + clip) * frames
            totals = best_means(regions, frames, corpus_ref, clip, rows, count)
            for p, total in enumerate(totals):
                out_ref[at : at + frames, p * count : (p + 1) * count] = total


def column_places(z, y, c):
    shape = (2 * NZ * NY, NZ * NY)
    col = lax.broadcasted_iota(jnp.int32, shape, 1)
    row = lax.broadcasted_iota(jnp.int32, shape, 0)
    far, step = col // 16, col // 4 % 4
    far = jnp.where(far == 2, -1, jnp.where(far == 3, 2, far))
    near = jnp.where(step == 1, 2, jnp.where(step == 2, 1, jnp.where(step == 3, -1, 0)))
    first = jnp.where(col % 4 < 2, 6, 2)
    from_z = jnp.where(c == 0, z - near - first, z - far + first)
    from_y = jnp.where(c == 0, y - far, y - near)
    parity = (c + col % 2) % 2
    place = ((from_z + NZ) % NZ * NY + (from_y + NY) % NY) * 2 + parity
    return jnp.where(place == row, 1.0, 0.0).astype(jnp.bfloat16)


def table_body(regions, frames, own_ref, other_ref, prev_ref, place_ref, *refs):
    out_ref, last_ref = refs[-2:]
    place = place_ref[...]
    sims_body(regions, frames, own_ref, other_ref, *refs[:-2], last_ref)
    prev = prev_ref[...].astype(jnp.bfloat16)
    last = last_ref[...].astype(jnp.bfloat16)
    done = prev.shape[1]
    dims = (((1,), (1,)), ((), ()))
    table = lax.dot_general(
        place[:, :done], prev, dims, preferred_element_type=jnp.float32
    ) + lax.dot_general(place[:, done:], last, dims, preferred_element_type=jnp.float32)
    table = table.astype(jnp.bfloat16)
    out_ref[0 : table.shape[0], :] = table
    out_ref[table.shape[0] :, :] = table


def kernel_call(body, outs, operands, scratch, flops, scalars=0):
    spaces = [pltpu.SMEM] * scalars + [pltpu.VMEM] * (len(operands) - scalars)
    return pl.pallas_call(
        body,
        in_specs=[pl.BlockSpec(memory_space=space) for space in spaces],
        out_specs=[pl.BlockSpec(memory_space=pltpu.VMEM)] * len(outs),
        out_shape=[jax.ShapeDtypeStruct(*out) for out in outs],
        scratch_shapes=scratch,
        compiler_params=pltpu.CompilerParams(vmem_limit_bytes=24 * 2**20),
        cost_estimate=pl.CostEstimate(
            flops=flops,
            bytes_accessed=sum(o.size * o.dtype.itemsize for o in operands),
            transcendentals=0,
        ),
    )(*operands)


def frame_sims(own, other, pieces):
    clips, rows, width = own.shape
    regions, count = pieces[0].shape[:2]
    frames = rows // regions
    total = count * len(pieces)
    body = functools.partial(sims_body, regions, frames)
    flops = 4 * clips * rows * regions * total * width
    outs = [((2 * clips * frames, total), jnp.float32)]
    return kernel_call(body, outs, [own, other, *pieces], [], flops)[0]


def frame_table(own, other, prev, place, pieces):
    clips, rows, width = own.shape
    regions, count = pieces[0].shape[:2]
    frames = rows // regions
    total = count * len(pieces)
    return kernel_call(
        functools.partial(table_body, regions, frames),
        [((2 * NC * NZ * NY, 2 * clips * frames), jnp.bfloat16)],
        [own, other, prev, place, *pieces],
        [pltpu.VMEM((2 * clips * frames, total), jnp.float32)],
        4 * clips * rows * regions * total * width,
    )[0]


def row_order():
    group = 4
    order = np.zeros((4, 2, group, 8, NX, group, NY, 2), np.float32)
    for k in range(4):
        for f in range(16):
            frame = 2 * f - 1 + k
            if 0 <= frame < 32:
                for q in range(group):
                    order[k, f % 2, q, f // 2, frame // 8, q, frame % 8 // 2, frame % 2] = 1
    return order.reshape(4 * 64, 128)


def prepare_body(
    at_ref, count_ref, shard_ref, clip_ref, first_ref, second_ref, third_ref, listed_ref, place_ref, t1_ref, t2_ref, t3_ref
):
    f32, bf16 = jnp.float32, jnp.bfloat16
    group, slots = 4, shard_ref.shape[1]
    chip, core, x = at_ref[0] * NY + at_ref[1], at_ref[2], at_ref[3]
    shards = shard_ref[...]
    names = jnp.where(shards // NC == chip, shards % NC * 2 + clip_ref[...], -1)
    line = lax.broadcasted_iota(jnp.int32, names.shape, 0)
    slot = lax.broadcasted_iota(jnp.int32, (1, slots), 1)
    chips = slots // 4
    to_chip = lax.broadcasted_iota(jnp.int32, (chips, slots), 0)
    of_slot = lax.broadcasted_iota(jnp.int32, (chips, slots), 1)
    pick_slot = lax.broadcasted_iota(jnp.int32, (slots, 2 * group), 0) % 4
    pick_to = lax.broadcasted_iota(jnp.int32, (slots, 2 * group), 1)
    listed = jnp.zeros((chips, 2 * group), f32)
    for q in range(group):
        query = x * group + q
        names_q = jnp.sum(jnp.where(line == query, names, 0), axis=0, keepdims=True)
        names_q = jnp.where(slot < count_ref[query], names_q, -1).astype(f32)
        spread = jnp.where(of_slot // 4 == to_chip, names_q, 0.0).astype(bf16)
        pick = jnp.where((pick_to % group == q) & (pick_slot == core * 2 + pick_to // group), 1.0, 0.0)
        listed = listed + dot(spread, pick.astype(bf16))
    listed_ref[...] = listed.astype(jnp.int32)
    place_ref[...] = column_places(at_ref[0], at_ref[1], core)

    lanes = t1_ref.shape[1]
    row = lax.broadcasted_iota(jnp.int32, (128, lanes), 0) % 32
    lane = lax.broadcasted_iota(jnp.int32, (128, lanes), 1)
    column = (lane // 32) % 16 * 2 + lane // 512
    channel = lax.broadcasted_iota(jnp.int32, (32, lanes), 1) % 32
    each = lax.broadcasted_iota(jnp.int32, (32, lanes), 0)
    taps = dot(first_ref[...], jnp.where(channel == each, 1.0, 0.0).astype(bf16))
    for dy in range(3):
        block = jnp.zeros((128, lanes), f32)
        for dx in range(3):
            tap = taps[dy * 3 + dx : dy * 3 + dx + 1, :]
            block = jnp.where(row == column + (dx - 1), tap, block)
        t1_ref[dy * 128 : (dy + 1) * 128, :] = block.astype(bf16)

    def placed(tap, before, total):
        rows, width = tap.shape
        parts = [jnp.zeros((before, width), f32), tap]
        parts.append(jnp.zeros((total - before - rows, width), f32))
        return jnp.concatenate(parts, axis=0)

    left = lax.broadcasted_iota(jnp.int32, (384, 128), 1) < 64
    for dy in range(3):
        tap = second_ref[dy * 96 : (dy + 1) * 96, :].astype(f32)
        tap = jnp.concatenate([tap, tap], axis=1)
        for odd in range(2):
            one = placed(tap, 96 + 32 * odd, 384)
            two = placed(tap, 160 + 32 * odd, 384)
            block = jnp.where(left, one, two).astype(bf16)
            t2_ref[dy * 384 : (dy + 1) * 384, odd * 128 : (odd + 1) * 128] = block
    for dy in range(3):
        tap = third_ref[dy * 192 : (dy + 1) * 192, :].astype(f32)
        for w in range(2):
            block = placed(tap, 64 + 64 * w, 384).astype(bf16)
            t3_ref[dy * 384 : (dy + 1) * 384, w * 128 : (w + 1) * 128] = block


def prepare(at, cand_count, cand_shard, cand_clip, first_kernel, second_kernel, third_kernel):
    operands = [
        at,
        cand_count,
        cand_shard,
        cand_clip,
        first_kernel.reshape(9, 32),
        second_kernel.reshape(288, 64),
        third_kernel.reshape(576, 128),
    ]
    outs = [
        ((cand_shard.shape[1] // 4, 8), jnp.int32),
        ((2 * NZ * NY, NZ * NY), jnp.bfloat16),
        ((384, 1024), jnp.bfloat16),
        ((1152, 256), jnp.bfloat16),
        ((1152, 256), jnp.bfloat16),
    ]
    return kernel_call(prepare_body, outs, operands, [], 10**9, scalars=2)


def dot(a, b):
    return jnp.dot(a, b, preferred_element_type=jnp.float32)


def rows_beside(values):
    rows = values.shape[0]
    at = lax.broadcasted_iota(jnp.int32, values.shape, 0) % 8
    before = jnp.where(at == 0, 0.0, pltpu.roll(values, 1, 0))
    after = jnp.where(at == 7, 0.0, pltpu.roll(values, rows - 1, 0))
    return before, after


def windows(layers, blocks):
    zero = jnp.zeros((layers[0].shape[0], 128), layers[0].dtype)
    out = []
    for t in range(blocks):
        parts = []
        for layer in layers:
            for b in (t - 1, t, t + 1):
                parts.append(layer[:, b * 128 : (b + 1) * 128] if 0 <= b < blocks else zero)
        out.append(jnp.concatenate(parts, axis=1))
    return out


def score_body(
    bias_ref, parts_ref, order_ref, t1_ref, b1_ref, t2_ref, b2_ref, t3_ref, b3_ref, weight_ref, listed_ref, out_ref
):
    b1 = jnp.concatenate([b1_ref[...]] * 16, axis=1)
    b2 = jnp.concatenate([b2_ref[...]] * 2, axis=1)
    b3 = jnp.concatenate([b3_ref[...]] * 2, axis=1)
    weight = jnp.concatenate([weight_ref[...].astype(jnp.float32)] * 2, axis=1)
    lane = lax.broadcasted_iota(jnp.int32, (128, 256), 1) // 128
    even_row = lax.broadcasted_iota(jnp.int32, (128, 256), 0) % 2
    weight = jnp.where(lane == even_row, weight, 0.0).astype(jnp.bfloat16)
    bf16 = jnp.bfloat16
    parts = parts_ref[...].astype(jnp.float32)
    half = parts.shape[0] // 2
    parts = (parts[:half] + pltpu.roll(parts[half:], 64, 1)).astype(bf16)
    maps = dot(order_ref[...], parts)
    x = [maps[k * 64 : (k + 1) * 64].astype(bf16) for k in range(4)]
    both = jnp.concatenate(
        [jnp.concatenate(x[0:3], axis=1), jnp.concatenate(x[1:4], axis=1)], axis=0
    )
    clip = lax.broadcasted_iota(jnp.int32, both.shape, 1) // 32 % 4
    wide = both.astype(jnp.float32)
    lhs = jnp.concatenate([jnp.where(clip == k, wide, 0.0).astype(bf16) for k in range(4)], axis=0)
    first = dot(lhs, t1_ref[...])
    first = jnp.maximum(first[:, :512], first[:, 512:])
    first = jnp.concatenate(
        [jnp.maximum(first[k * 128 : k * 128 + 64], first[k * 128 + 64 : k * 128 + 128]) for k in range(4)],
        axis=0,
    )
    first = jnp.maximum(first + b1, 0.0)
    even = jnp.concatenate([first[k * 64 : k * 64 + 32] for k in range(4)], axis=0)
    odd = jnp.concatenate([first[k * 64 + 32 : k * 64 + 64] for k in range(4)], axis=0)
    odd_before = rows_beside(odd)[0]
    even_after = rows_beside(even)[1]
    layers = [v.astype(bf16) for v in (odd_before, even, odd, even_after)]
    lhs = jnp.concatenate(windows(layers[0:3], 4) + windows(layers[1:4], 4), axis=0)
    second = dot(lhs, t2_ref[...])
    second = jnp.maximum(second[:, :128], second[:, 128:])
    second = jnp.maximum(second[:512], second[512:])
    second = jnp.maximum(second + b2, 0.0)
    second = jnp.concatenate([second[t * 128 : (t + 1) * 128] for t in range(4)], axis=1)
    before, after = rows_beside(second)
    lhs = jnp.concatenate(windows([v.astype(bf16) for v in (before, second, after)], 4), axis=0)
    third = jnp.maximum(dot(lhs, t3_ref[...]) + b3, 0.0).astype(bf16)
    score = lax.dot_general(
        third, weight, (((1,), (1,)), ((), ())), preferred_element_type=jnp.float32
    )
    score = jnp.maximum(
        jnp.maximum(score[0:128], score[128:256]), jnp.maximum(score[256:384], score[384:512])
    )
    score = jnp.max(score, axis=1, keepdims=True) + jnp.broadcast_to(bias_ref[0], (1, 128))
    score = score.reshape(16, 8, score.shape[1]).sum(axis=1) * 0.125
    listed = listed_ref[...]
    slot_query = lax.broadcasted_iota(jnp.int32, (1, listed.shape[1]), 1) % 4
    total = jnp.zeros(listed.shape, jnp.float32)
    for k in range(4):
        line = jnp.zeros((1, listed.shape[1]), jnp.float32)
        for q in range(4):
            line = jnp.where(slot_query == q, score[k * 4 + q : k * 4 + q + 1, : listed.shape[1]], line)
        total = jnp.where(listed == k, line, total)
    out_ref[...] = total


def slot_scores(parts, listed, spread, first_bias, second_bias, third_bias, score_weight, score_bias):
    operands = [
        score_bias,
        parts,
        jnp.asarray(row_order(), jnp.bfloat16),
        spread[0],
        first_bias[None, :],
        spread[1],
        second_bias[None, :],
        spread[2],
        third_bias[None, :],
        score_weight[None, :],
        listed,
    ]
    outs = [(listed.shape, jnp.float32)]
    return kernel_call(score_body, outs, operands, [], 2 * 10**9, scalars=1)[0]


def on_device(
    queries,
    corpus,
    cand_shard,
    cand_clip,
    cand_count,
    first_kernel,
    first_bias,
    second_kernel,
    second_bias,
    third_kernel,
    third_bias,
    score_weight,
    score_bias,
):
    at = jnp.stack([lax.axis_index(a) for a in ("z", "y", "c", "x")]).astype(jnp.int32)
    clip_dev, frames, regions, width = corpus.shape
    group = cand_shard.shape[0] // NX

    own = corpus.transpose(0, 2, 1, 3).reshape(clip_dev, regions * frames, width)
    four = gather_classes(queries[0, 0])
    ahead = near_shift(four, -1)
    two = near_shift(four, 2)
    behind = near_shift(four, 1)
    kernels = (first_kernel, second_kernel, third_kernel)
    kernels, two = lax.optimization_barrier((kernels, two))
    listed, place, *spread = prepare(at, cand_count, cand_shard, cand_clip, *kernels)
    first = jnp.concatenate([four, two], axis=1)
    last = jnp.concatenate([behind, ahead], axis=1)
    own, listed, first, last = lax.optimization_barrier((own, listed, first, last))
    other = lax.ppermute(own, "c", [(0, 1), (1, 0)])
    behind_first = shift(first, 1)
    ahead_first = shift(first, -1)
    two_first = shift(behind_first, 1)
    behind_last = shift(last, 1)
    ahead_last = shift(last, -1)
    two_last = shift(behind_last, 1)

    near = [first, last, behind_first, behind_last, ahead_first, ahead_last]
    prev = frame_sims(own, other, near)
    two, prev = lax.optimization_barrier(((two_first, two_last), prev))
    table = frame_table(own, other, prev, place, two)

    parts = lax.all_to_all(table, ("c", "x"), 0, 0, tiled=True)
    values = slot_scores(
        parts, listed, spread, first_bias, second_bias, third_bias, score_weight, score_bias
    )
    values = lax.all_to_all(values, ("z", "y"), 0, 0, tiled=True)
    return values.sum(axis=0).reshape(-1, group).T


def solution(mesh):
    devices = mesh.devices.reshape(NZ, NY, NC, NX)
    grid = Mesh(devices, ("z", "y", "c", "x"))
    return jax.shard_map(
        on_device,
        mesh=grid,
        in_specs=(P("x", PLANE), P(PLANE)) + (P(),) * 11,
        out_specs=P("x", PLANE),
        check_vma=False,
    )
```

```python
import functools

import jax
import jax.numpy as jnp
import numpy as np
from jax import lax
from jax.experimental import pallas as pl
from jax.experimental.pallas import tpu as pltpu
from jax.sharding import Mesh
from jax.sharding import PartitionSpec as P

NZ, NY, NC, NX = 16, 4, 2, 4
PLANE = ("z", "y", "c")
CLASS_STEPS = (6, 2)


def device_at(z, y, c):
    return ((z % NZ) * NY + y % NY) * NC + c


def send(values, even, odd):
    pairs = []
    for z in range(NZ):
        for y in range(NY):
            for c, to in ((0, even), (1, odd)):
                pairs.append((device_at(z, y, c), device_at(*to(z, y), c)))
    return lax.ppermute(values, PLANE, pairs)


def shift(values, d):
    return send(values, lambda z, y: (z, y + d), lambda z, y: (z + d, y))


def near_shift(values, d):
    return send(values, lambda z, y: (z + d, y), lambda z, y: (z, y + d))


def gather_classes(block):
    other = lax.ppermute(block, "c", [(0, 1), (1, 0)])
    both = jnp.stack([block, other], axis=1)
    four = [send(both, lambda z, y: (z + d, y), lambda z, y: (z - d, y)) for d in CLASS_STEPS]
    return four


def best_means(regions, frames, corpus_ref, clip, rows, count):
    sims = lax.dot_general(
        corpus_ref[clip], rows, (((1,), (1,)), ((), ())), preferred_element_type=jnp.float32
    )
    best = sims[0:frames]
    for j in range(1, regions):
        best = jnp.maximum(best, sims[j * frames : (j + 1) * frames])
    totals = []
    for p in range(rows.shape[0] // (regions * count)):
        total = 0.0
        for i in range(regions):
            at = (p * regions + i) * count
            total = total + best[:, at : at + count]
        totals.append(total * (1.0 / regions))
    return totals


def stacked(refs):
    return jnp.concatenate([ref[...].reshape(-1, ref.shape[-1]) for ref in refs], axis=0)


def sims_body(regions, frames, own_ref, other_ref, *refs):
    out_ref = refs[-1]
    count = refs[0].shape[1]
    rows = stacked(refs[:-1])
    for half, corpus_ref in enumerate((own_ref, other_ref)):
        for clip in range(2):
            at = (half * 2 + clip) * frames
            totals = best_means(regions, frames, corpus_ref, clip, rows, count)
            for p, total in enumerate(totals):
                out_ref[at : at + frames, p * count : (p + 1) * count] = total


def column_places(z, y, c):
    shape = (2 * NZ * NY, NZ * NY)
    col = lax.broadcasted_iota(jnp.int32, shape, 1)
    row = lax.broadcasted_iota(jnp.int32, shape, 0)
    far, step = col // 16, col // 4 % 4
    far = jnp.where(far == 2, -1, jnp.where(far == 3, 2, far))
    near = jnp.where(step == 1, 2, jnp.where(step == 2, 1, jnp.where(step == 3, -1, 0)))
    first = jnp.where(col % 4 < 2, 6, 2)
    from_z = jnp.where(c == 0, z - near - first, z - far + first)
    from_y = jnp.where(c == 0, y - far, y - near)
    parity = (c + col % 2) % 2
    place = ((from_z + NZ) % NZ * NY + (from_y + NY) % NY) * 2 + parity
    return jnp.where(place == row, 1.0, 0.0).astype(jnp.bfloat16)


def table_body(regions, frames, own_ref, other_ref, prev_ref, place_ref, *refs):
    out_ref, last_ref = refs[-2:]
    place = place_ref[...]
    sims_body(regions, frames, own_ref, other_ref, *refs[:-2], last_ref)
    prev = prev_ref[...].astype(jnp.bfloat16)
    last = last_ref[...].astype(jnp.bfloat16)
    done = prev.shape[1]
    dims = (((1,), (1,)), ((), ()))
    table = lax.dot_general(
        place[:, :done], prev, dims, preferred_element_type=jnp.float32
    ) + lax.dot_general(place[:, done:], last, dims, preferred_element_type=jnp.float32)
    table = table.astype(jnp.bfloat16)
    out_ref[0 : table.shape[0], :] = table
    out_ref[table.shape[0] :, :] = table


def kernel_call(body, outs, operands, scratch, flops, scalars=0):
    spaces = [pltpu.SMEM] * scalars + [pltpu.VMEM] * (len(operands) - scalars)
    return pl.pallas_call(
        body,
        in_specs=[pl.BlockSpec(memory_space=space) for space in spaces],
        out_specs=[pl.BlockSpec(memory_space=pltpu.VMEM)] * len(outs),
        out_shape=[jax.ShapeDtypeStruct(*out) for out in outs],
        scratch_shapes=scratch,
        compiler_params=pltpu.CompilerParams(vmem_limit_bytes=24 * 2**20),
        cost_estimate=pl.CostEstimate(
            flops=flops,
            bytes_accessed=sum(o.size * o.dtype.itemsize for o in operands),
            transcendentals=0,
        ),
    )(*operands)


def frame_sims(own, other, pieces):
    clips, rows, width = own.shape
    regions, count = pieces[0].shape[:2]
    frames = rows // regions
    total = count * len(pieces)
    body = functools.partial(sims_body, regions, frames)
    flops = 4 * clips * rows * regions * total * width
    outs = [((2 * clips * frames, total), jnp.float32)]
    return kernel_call(body, outs, [own, other, *pieces], [], flops)[0]


def frame_table(own, other, prev, place, pieces):
    clips, rows, width = own.shape
    regions, count = pieces[0].shape[:2]
    frames = rows // regions
    total = count * len(pieces)
    return kernel_call(
        functools.partial(table_body, regions, frames),
        [((2 * NC * NZ * NY, 2 * clips * frames), jnp.bfloat16)],
        [own, other, prev, place, *pieces],
        [pltpu.VMEM((2 * clips * frames, total), jnp.float32)],
        4 * clips * rows * regions * total * width,
    )[0]


def row_order():
    group = 4
    order = np.zeros((4, 2, group, 8, NX, group, NY, 2), np.float32)
    for k in range(4):
        for f in range(16):
            frame = 2 * f - 1 + k
            if 0 <= frame < 32:
                for q in range(group):
                    order[k, f % 2, q, f // 2, frame // 8, q, frame % 8 // 2, frame % 2] = 1
    return order.reshape(4 * 64, 128)


def prepare_body(
    at_ref, count_ref, shard_ref, clip_ref, first_ref, second_ref, third_ref, listed_ref, place_ref, t1_ref, t2_ref, t3_ref
):
    f32, bf16 = jnp.float32, jnp.bfloat16
    group, slots = 4, shard_ref.shape[1]
    chip, core, x = at_ref[0] * NY + at_ref[1], at_ref[2], at_ref[3]
    shards = shard_ref[...]
    names = jnp.where(shards // NC == chip, shards % NC * 2 + clip_ref[...], -1)
    line = lax.broadcasted_iota(jnp.int32, names.shape, 0)
    slot = lax.broadcasted_iota(jnp.int32, (1, slots), 1)
    chips = slots // 4
    to_chip = lax.broadcasted_iota(jnp.int32, (chips, slots), 0)
    of_slot = lax.broadcasted_iota(jnp.int32, (chips, slots), 1)
    pick_slot = lax.broadcasted_iota(jnp.int32, (slots, 2 * group), 0) % 4
    pick_to = lax.broadcasted_iota(jnp.int32, (slots, 2 * group), 1)
    listed = jnp.zeros((chips, 2 * group), f32)
    for q in range(group):
        query = x * group + q
        names_q = jnp.sum(jnp.where(line == query, names, 0), axis=0, keepdims=True)
        names_q = jnp.where(slot < count_ref[query], names_q, -1).astype(f32)
        spread = jnp.where(of_slot // 4 == to_chip, names_q, 0.0).astype(bf16)
        pick = jnp.where((pick_to % group == q) & (pick_slot == core * 2 + pick_to // group), 1.0, 0.0)
        listed = listed + dot(spread, pick.astype(bf16))
    listed_ref[...] = listed.astype(jnp.int32)
    place_ref[...] = column_places(at_ref[0], at_ref[1], core)

    lanes = t1_ref.shape[1]
    row = lax.broadcasted_iota(jnp.int32, (128, lanes), 0) % 32
    lane = lax.broadcasted_iota(jnp.int32, (128, lanes), 1)
    column = (lane // 32) % 16 * 2 + lane // 512
    channel = lax.broadcasted_iota(jnp.int32, (32, lanes), 1) % 32
    each = lax.broadcasted_iota(jnp.int32, (32, lanes), 0)
    taps = dot(first_ref[...], jnp.where(channel == each, 1.0, 0.0).astype(bf16))
    for dy in range(3):
        block = jnp.zeros((128, lanes), f32)
        for dx in range(3):
            tap = taps[dy * 3 + dx : dy * 3 + dx + 1, :]
            block = jnp.where(row == column + (dx - 1), tap, block)
        t1_ref[dy * 128 : (dy + 1) * 128, :] = block.astype(bf16)

    def placed(tap, before, total):
        rows, width = tap.shape
        parts = [jnp.zeros((before, width), f32), tap]
        parts.append(jnp.zeros((total - before - rows, width), f32))
        return jnp.concatenate(parts, axis=0)

    left = lax.broadcasted_iota(jnp.int32, (384, 128), 1) < 64
    for dy in range(3):
        tap = second_ref[dy * 96 : (dy + 1) * 96, :].astype(f32)
        tap = jnp.concatenate([tap, tap], axis=1)
        for odd in range(2):
            one = placed(tap, 96 + 32 * odd, 384)
            two = placed(tap, 160 + 32 * odd, 384)
            block = jnp.where(left, one, two).astype(bf16)
            t2_ref[dy * 384 : (dy + 1) * 384, odd * 128 : (odd + 1) * 128] = block
    for dy in range(3):
        tap = third_ref[dy * 192 : (dy + 1) * 192, :].astype(f32)
        for w in range(2):
            block = placed(tap, 64 + 64 * w, 384).astype(bf16)
            t3_ref[dy * 384 : (dy + 1) * 384, w * 128 : (w + 1) * 128] = block


def prepare(at, cand_count, cand_shard, cand_clip, first_kernel, second_kernel, third_kernel):
    operands = [
        at,
        cand_count,
        cand_shard,
        cand_clip,
        first_kernel.reshape(9, 32),
        second_kernel.reshape(288, 64),
        third_kernel.reshape(576, 128),
    ]
    outs = [
        ((cand_shard.shape[1] // 4, 8), jnp.int32),
        ((2 * NZ * NY, NZ * NY), jnp.bfloat16),
        ((384, 1024), jnp.bfloat16),
        ((1152, 256), jnp.bfloat16),
        ((1152, 256), jnp.bfloat16),
    ]
    return kernel_call(prepare_body, outs, operands, [], 10**9, scalars=2)


def dot(a, b):
    return jnp.dot(a, b, preferred_element_type=jnp.float32)


def rows_beside(values):
    rows = values.shape[0]
    at = lax.broadcasted_iota(jnp.int32, values.shape, 0) % 8
    before = jnp.where(at == 0, 0.0, pltpu.roll(values, 1, 0))
    after = jnp.where(at == 7, 0.0, pltpu.roll(values, rows - 1, 0))
    return before, after


def windows(layers, blocks):
    zero = jnp.zeros((layers[0].shape[0], 128), layers[0].dtype)
    out = []
    for t in range(blocks):
        parts = []
        for layer in layers:
            for b in (t - 1, t, t + 1):
                parts.append(layer[:, b * 128 : (b + 1) * 128] if 0 <= b < blocks else zero)
        out.append(jnp.concatenate(parts, axis=1))
    return out


def score_body(
    bias_ref, parts_ref, order_ref, t1_ref, b1_ref, t2_ref, b2_ref, t3_ref, b3_ref, weight_ref, listed_ref, out_ref
):
    b1 = jnp.concatenate([b1_ref[...]] * 16, axis=1)
    b2 = jnp.concatenate([b2_ref[...]] * 2, axis=1)
    b3 = jnp.concatenate([b3_ref[...]] * 2, axis=1)
    weight = jnp.concatenate([weight_ref[...].astype(jnp.float32)] * 2, axis=1)
    lane = lax.broadcasted_iota(jnp.int32, (128, 256), 1) // 128
    even_row = lax.broadcasted_iota(jnp.int32, (128, 256), 0) % 2
    weight = jnp.where(lane == even_row, weight, 0.0).astype(jnp.bfloat16)
    bf16 = jnp.bfloat16
    parts = parts_ref[...].astype(jnp.float32)
    half = parts.shape[0] // 2
    parts = (parts[:half] + pltpu.roll(parts[half:], 64, 1)).astype(bf16)
    maps = dot(order_ref[...], parts)
    x = [maps[k * 64 : (k + 1) * 64].astype(bf16) for k in range(4)]
    both = jnp.concatenate(
        [jnp.concatenate(x[0:3], axis=1), jnp.concatenate(x[1:4], axis=1)], axis=0
    )
    clip = lax.broadcasted_iota(jnp.int32, both.shape, 1) // 32 % 4
    wide = both.astype(jnp.float32)
    lhs = jnp.concatenate([jnp.where(clip == k, wide, 0.0).astype(bf16) for k in range(4)], axis=0)
    first = dot(lhs, t1_ref[...])
    first = jnp.maximum(first[:, :512], first[:, 512:])
    first = jnp.concatenate(
        [jnp.maximum(first[k * 128 : k * 128 + 64], first[k * 128 + 64 : k * 128 + 128]) for k in range(4)],
        axis=0,
    )
    first = jnp.maximum(first + b1, 0.0)
    even = jnp.concatenate([first[k * 64 : k * 64 + 32] for k in range(4)], axis=0)
    odd = jnp.concatenate([first[k * 64 + 32 : k * 64 + 64] for k in range(4)], axis=0)
    odd_before = rows_beside(odd)[0]
    even_after = rows_beside(even)[1]
    layers = [v.astype(bf16) for v in (odd_before, even, odd, even_after)]
    lhs = jnp.concatenate(windows(layers[0:3], 4) + windows(layers[1:4], 4), axis=0)
    second = dot(lhs, t2_ref[...])
    second = jnp.maximum(second[:, :128], second[:, 128:])
    second = jnp.maximum(second[:512], second[512:])
    second = jnp.maximum(second + b2, 0.0)
    second = jnp.concatenate([second[t * 128 : (t + 1) * 128] for t in range(4)], axis=1)
    before, after = rows_beside(second)
    lhs = jnp.concatenate(windows([v.astype(bf16) for v in (before, second, after)], 4), axis=0)
    third = jnp.maximum(dot(lhs, t3_ref[...]) + b3, 0.0).astype(bf16)
    score = lax.dot_general(
        third, weight, (((1,), (1,)), ((), ())), preferred_element_type=jnp.float32
    )
    score = jnp.maximum(
        jnp.maximum(score[0:128], score[128:256]), jnp.maximum(score[256:384], score[384:512])
    )
    score = jnp.max(score, axis=1, keepdims=True) + jnp.broadcast_to(bias_ref[0], (1, 128))
    score = score.reshape(16, 8, score.shape[1]).sum(axis=1) * 0.125
    listed = listed_ref[...]
    slot_query = lax.broadcasted_iota(jnp.int32, (1, listed.shape[1]), 1) % 4
    total = jnp.zeros(listed.shape, jnp.float32)
    for k in range(4):
        line = jnp.zeros((1, listed.shape[1]), jnp.float32)
        for q in range(4):
            line = jnp.where(slot_query == q, score[k * 4 + q : k * 4 + q + 1, : listed.shape[1]], line)
        total = jnp.where(listed == k, line, total)
    out_ref[...] = total


def slot_scores(parts, listed, spread, first_bias, second_bias, third_bias, score_weight, score_bias):
    operands = [
        score_bias,
        parts,
        jnp.asarray(row_order(), jnp.bfloat16),
        spread[0],
        first_bias[None, :],
        spread[1],
        second_bias[None, :],
        spread[2],
        third_bias[None, :],
        score_weight[None, :],
        listed,
    ]
    outs = [(listed.shape, jnp.float32)]
    return kernel_call(score_body, outs, operands, [], 2 * 10**9, scalars=1)[0]


def on_device(
    queries,
    corpus,
    cand_shard,
    cand_clip,
    cand_count,
    first_kernel,
    first_bias,
    second_kernel,
    second_bias,
    third_kernel,
    third_bias,
    score_weight,
    score_bias,
):
    at = jnp.stack([lax.axis_index(a) for a in ("z", "y", "c", "x")]).astype(jnp.int32)
    clip_dev, frames, regions, width = corpus.shape
    group = cand_shard.shape[0] // NX

    own = corpus.transpose(0, 2, 1, 3).reshape(clip_dev, regions * frames, width)
    head, tail = gather_classes(queries[0, 0])
    kernels = (first_kernel, second_kernel, third_kernel)
    kernels, head = lax.optimization_barrier((kernels, head))
    listed, place, *spread = prepare(at, cand_count, cand_shard, cand_clip, *kernels)
    own, listed, tail = lax.optimization_barrier((own, listed, tail))
    other = lax.ppermute(own, "c", [(0, 1), (1, 0)])
    four = jnp.concatenate([head, tail], axis=1)
    ahead = near_shift(four, -1)
    two = near_shift(four, 2)
    behind = near_shift(four, 1)
    first = jnp.concatenate([four, two], axis=1)
    last = jnp.concatenate([behind, ahead], axis=1)
    behind_first = shift(first, 1)
    ahead_first = shift(first, -1)
    two_first = shift(behind_first, 1)
    behind_last = shift(last, 1)
    ahead_last = shift(last, -1)
    two_last = shift(behind_last, 1)

    near = [first, last, behind_first, behind_last, ahead_first, ahead_last]
    prev = frame_sims(own, other, near)
    two, prev = lax.optimization_barrier(((two_first, two_last), prev))
    table = frame_table(own, other, prev, place, two)

    parts = lax.all_to_all(table, ("c", "x"), 0, 0, tiled=True)
    values = slot_scores(
        parts, listed, spread, first_bias, second_bias, third_bias, score_weight, score_bias
    )
    values = lax.all_to_all(values, ("z", "y"), 0, 0, tiled=True)
    return values.sum(axis=0).reshape(-1, group).T


def solution(mesh):
    devices = mesh.devices.reshape(NZ, NY, NC, NX)
    grid = Mesh(devices, ("z", "y", "c", "x"))
    return jax.shard_map(
        on_device,
        mesh=grid,
        in_specs=(P("x", PLANE), P(PLANE)) + (P(),) * 11,
        out_specs=P("x", PLANE),
        check_vma=False,
    )
```

```python
import functools

import jax
import jax.numpy as jnp
import numpy as np
from jax import lax
from jax.experimental import pallas as pl
from jax.experimental.pallas import tpu as pltpu
from jax.sharding import Mesh
from jax.sharding import PartitionSpec as P

NZ, NY, NC, NX = 16, 4, 2, 4
PLANE = ("z", "y", "c")
CLASS_STEPS = (6, 2)


def device_at(z, y, c):
    return ((z % NZ) * NY + y % NY) * NC + c


def send(values, even, odd):
    pairs = []
    for z in range(NZ):
        for y in range(NY):
            for c, to in ((0, even), (1, odd)):
                pairs.append((device_at(z, y, c), device_at(*to(z, y), c)))
    return lax.ppermute(values, PLANE, pairs)


def shift(values, d):
    return send(values, lambda z, y: (z, y + d), lambda z, y: (z + d, y))


def near_shift(values, d):
    return send(values, lambda z, y: (z + d, y), lambda z, y: (z, y + d))


def gather_classes(block):
    other = lax.ppermute(block, "c", [(0, 1), (1, 0)])
    both = jnp.stack([block, other], axis=1)
    four = [send(both, lambda z, y: (z + d, y), lambda z, y: (z - d, y)) for d in CLASS_STEPS]
    return jnp.concatenate(four, axis=1)


def best_means(regions, frames, corpus_ref, clip, rows, count):
    sims = lax.dot_general(
        corpus_ref[clip], rows, (((1,), (1,)), ((), ())), preferred_element_type=jnp.float32
    )
    best = sims[0:frames]
    for j in range(1, regions):
        best = jnp.maximum(best, sims[j * frames : (j + 1) * frames])
    totals = []
    for p in range(rows.shape[0] // (regions * count)):
        total = 0.0
        for i in range(regions):
            at = (p * regions + i) * count
            total = total + best[:, at : at + count]
        totals.append(total * (1.0 / regions))
    return totals


def stacked(refs):
    return jnp.concatenate([ref[...].reshape(-1, ref.shape[-1]) for ref in refs], axis=0)


def sims_body(regions, frames, own_ref, other_ref, *refs):
    out_ref = refs[-1]
    count = refs[0].shape[1]
    rows = stacked(refs[:-1])
    for half, corpus_ref in enumerate((own_ref, other_ref)):
        for clip in range(2):
            at = (half * 2 + clip) * frames
            totals = best_means(regions, frames, corpus_ref, clip, rows, count)
            for p, total in enumerate(totals):
                out_ref[at : at + frames, p * count : (p + 1) * count] = total


def column_places(z, y, c):
    shape = (2 * NZ * NY, NZ * NY)
    col = lax.broadcasted_iota(jnp.int32, shape, 1)
    row = lax.broadcasted_iota(jnp.int32, shape, 0)
    far, step = col // 16, col // 4 % 4
    far = jnp.where(far == 2, -1, jnp.where(far == 3, 2, far))
    near = jnp.where(step == 1, 2, jnp.where(step == 2, 1, jnp.where(step == 3, -1, 0)))
    first = jnp.where(col % 4 < 2, 6, 2)
    from_z = jnp.where(c == 0, z - near - first, z - far + first)
    from_y = jnp.where(c == 0, y - far, y - near)
    parity = (c + col % 2) % 2
    place = ((from_z + NZ) % NZ * NY + (from_y + NY) % NY) * 2 + parity
    return jnp.where(place == row, 1.0, 0.0).astype(jnp.bfloat16)


def table_body(regions, frames, own_ref, other_ref, prev_ref, place_ref, *refs):
    out_ref, last_ref = refs[-2:]
    place = place_ref[...]
    sims_body(regions, frames, own_ref, other_ref, *refs[:-2], last_ref)
    prev = prev_ref[...].astype(jnp.bfloat16)
    last = last_ref[...].astype(jnp.bfloat16)
    done = prev.shape[1]
    dims = (((1,), (1,)), ((), ()))
    table = lax.dot_general(
        place[:, :done], prev, dims, preferred_element_type=jnp.float32
    ) + lax.dot_general(place[:, done:], last, dims, preferred_element_type=jnp.float32)
    table = table.astype(jnp.bfloat16)
    out_ref[0 : table.shape[0], :] = table
    out_ref[table.shape[0] :, :] = table


def kernel_call(body, outs, operands, scratch, flops, scalars=0):
    spaces = [pltpu.SMEM] * scalars + [pltpu.VMEM] * (len(operands) - scalars)
    return pl.pallas_call(
        body,
        in_specs=[pl.BlockSpec(memory_space=space) for space in spaces],
        out_specs=[pl.BlockSpec(memory_space=pltpu.VMEM)] * len(outs),
        out_shape=[jax.ShapeDtypeStruct(*out) for out in outs],
        scratch_shapes=scratch,
        compiler_params=pltpu.CompilerParams(vmem_limit_bytes=24 * 2**20),
        cost_estimate=pl.CostEstimate(
            flops=flops,
            bytes_accessed=sum(o.size * o.dtype.itemsize for o in operands),
            transcendentals=0,
        ),
    )(*operands)


def frame_sims(own, other, pieces):
    clips, rows, width = own.shape
    regions, count = pieces[0].shape[:2]
    frames = rows // regions
    total = count * len(pieces)
    body = functools.partial(sims_body, regions, frames)
    flops = 4 * clips * rows * regions * total * width
    outs = [((2 * clips * frames, total), jnp.float32)]
    return kernel_call(body, outs, [own, other, *pieces], [], flops)[0]


def frame_table(own, other, prev, place, pieces):
    clips, rows, width = own.shape
    regions, count = pieces[0].shape[:2]
    frames = rows // regions
    total = count * len(pieces)
    return kernel_call(
        functools.partial(table_body, regions, frames),
        [((2 * NC * NZ * NY, 2 * clips * frames), jnp.bfloat16)],
        [own, other, prev, place, *pieces],
        [pltpu.VMEM((2 * clips * frames, total), jnp.float32)],
        4 * clips * rows * regions * total * width,
    )[0]


def row_order():
    group = 4
    order = np.zeros((4, 2, group, 8, NX, group, NY, 2), np.float32)
    for k in range(4):
        for f in range(16):
            frame = 2 * f - 1 + k
            if 0 <= frame < 32:
                for q in range(group):
                    order[k, f % 2, q, f // 2, frame // 8, q, frame % 8 // 2, frame % 2] = 1
    return order.reshape(4 * 64, 128)


def prepare_body(
    at_ref, count_ref, shard_ref, clip_ref, first_ref, second_ref, third_ref, listed_ref, place_ref, t1_ref, t2_ref, t3_ref
):
    f32, bf16 = jnp.float32, jnp.bfloat16
    group, slots = 4, shard_ref.shape[1]
    chip, core, x = at_ref[0] * NY + at_ref[1], at_ref[2], at_ref[3]
    shards = shard_ref[...]
    names = jnp.where(shards // NC == chip, shards % NC * 2 + clip_ref[...], -1)
    line = lax.broadcasted_iota(jnp.int32, names.shape, 0)
    slot = lax.broadcasted_iota(jnp.int32, (1, slots), 1)
    chips = slots // 4
    to_chip = lax.broadcasted_iota(jnp.int32, (chips, slots), 0)
    of_slot = lax.broadcasted_iota(jnp.int32, (chips, slots), 1)
    pick_slot = lax.broadcasted_iota(jnp.int32, (slots, 2 * group), 0) % 4
    pick_to = lax.broadcasted_iota(jnp.int32, (slots, 2 * group), 1)
    listed = jnp.zeros((chips, 2 * group), f32)
    for q in range(group):
        query = x * group + q
        names_q = jnp.sum(jnp.where(line == query, names, 0), axis=0, keepdims=True)
        names_q = jnp.where(slot < count_ref[query], names_q, -1).astype(f32)
        spread = jnp.where(of_slot // 4 == to_chip, names_q, 0.0).astype(bf16)
        pick = jnp.where((pick_to % group == q) & (pick_slot == core * 2 + pick_to // group), 1.0, 0.0)
        listed = listed + dot(spread, pick.astype(bf16))
    listed_ref[...] = listed.astype(jnp.int32)
    place_ref[...] = column_places(at_ref[0], at_ref[1], core)

    lanes = t1_ref.shape[1]
    row = lax.broadcasted_iota(jnp.int32, (128, lanes), 0) % 32
    lane = lax.broadcasted_iota(jnp.int32, (128, lanes), 1)
    column = (lane // 32) % 16 * 2 + lane // 512
    channel = lax.broadcasted_iota(jnp.int32, (32, lanes), 1) % 32
    each = lax.broadcasted_iota(jnp.int32, (32, lanes), 0)
    taps = dot(first_ref[...], jnp.where(channel == each, 1.0, 0.0).astype(bf16))
    for dy in range(3):
        block = jnp.zeros((128, lanes), f32)
        for dx in range(3):
            tap = taps[dy * 3 + dx : dy * 3 + dx + 1, :]
            block = jnp.where(row == column + (dx - 1), tap, block)
        t1_ref[dy * 128 : (dy + 1) * 128, :] = block.astype(bf16)

    def placed(tap, before, total):
        rows, width = tap.shape
        parts = [jnp.zeros((before, width), f32), tap]
        parts.append(jnp.zeros((total - before - rows, width), f32))
        return jnp.concatenate(parts, axis=0)

    left = lax.broadcasted_iota(jnp.int32, (384, 128), 1) < 64
    for dy in range(3):
        tap = second_ref[dy * 96 : (dy + 1) * 96, :].astype(f32)
        tap = jnp.concatenate([tap, tap], axis=1)
        for odd in range(2):
            one = placed(tap, 96 + 32 * odd, 384)
            two = placed(tap, 160 + 32 * odd, 384)
            block = jnp.where(left, one, two).astype(bf16)
            t2_ref[dy * 384 : (dy + 1) * 384, odd * 128 : (odd + 1) * 128] = block
    for dy in range(3):
        tap = third_ref[dy * 192 : (dy + 1) * 192, :].astype(f32)
        for w in range(2):
            block = placed(tap, 64 + 64 * w, 384).astype(bf16)
            t3_ref[dy * 384 : (dy + 1) * 384, w * 128 : (w + 1) * 128] = block


def prepare(at, cand_count, cand_shard, cand_clip, first_kernel, second_kernel, third_kernel):
    operands = [
        at,
        cand_count,
        cand_shard,
        cand_clip,
        first_kernel.reshape(9, 32),
        second_kernel.reshape(288, 64),
        third_kernel.reshape(576, 128),
    ]
    outs = [
        ((cand_shard.shape[1] // 4, 8), jnp.int32),
        ((2 * NZ * NY, NZ * NY), jnp.bfloat16),
        ((384, 1024), jnp.bfloat16),
        ((1152, 256), jnp.bfloat16),
        ((1152, 256), jnp.bfloat16),
    ]
    return kernel_call(prepare_body, outs, operands, [], 10**9, scalars=2)


def dot(a, b):
    return jnp.dot(a, b, preferred_element_type=jnp.float32)


def rows_beside(values):
    rows = values.shape[0]
    at = lax.broadcasted_iota(jnp.int32, values.shape, 0) % 8
    before = jnp.where(at == 0, 0.0, pltpu.roll(values, 1, 0))
    after = jnp.where(at == 7, 0.0, pltpu.roll(values, rows - 1, 0))
    return before, after


def windows(layers, blocks):
    zero = jnp.zeros((layers[0].shape[0], 128), layers[0].dtype)
    out = []
    for t in range(blocks):
        parts = []
        for layer in layers:
            for b in (t - 1, t, t + 1):
                parts.append(layer[:, b * 128 : (b + 1) * 128] if 0 <= b < blocks else zero)
        out.append(jnp.concatenate(parts, axis=1))
    return out


def score_body(
    bias_ref, parts_ref, order_ref, t1_ref, b1_ref, t2_ref, b2_ref, t3_ref, b3_ref, weight_ref, listed_ref, out_ref
):
    b1 = jnp.concatenate([b1_ref[...]] * 16, axis=1)
    b2 = jnp.concatenate([b2_ref[...]] * 2, axis=1)
    b3 = jnp.concatenate([b3_ref[...]] * 2, axis=1)
    weight = jnp.concatenate([weight_ref[...].astype(jnp.float32)] * 2, axis=1)
    lane = lax.broadcasted_iota(jnp.int32, (128, 256), 1) // 128
    even_row = lax.broadcasted_iota(jnp.int32, (128, 256), 0) % 2
    weight = jnp.where(lane == even_row, weight, 0.0).astype(jnp.bfloat16)
    bf16 = jnp.bfloat16
    parts = parts_ref[...].astype(jnp.float32)
    half = parts.shape[0] // 2
    parts = (parts[:half] + pltpu.roll(parts[half:], 64, 1)).astype(bf16)
    maps = dot(order_ref[...], parts)
    x = [maps[k * 64 : (k + 1) * 64].astype(bf16) for k in range(4)]
    both = jnp.concatenate(
        [jnp.concatenate(x[0:3], axis=1), jnp.concatenate(x[1:4], axis=1)], axis=0
    )
    clip = lax.broadcasted_iota(jnp.int32, both.shape, 1) // 32 % 4
    wide = both.astype(jnp.float32)
    lhs = jnp.concatenate([jnp.where(clip == k, wide, 0.0).astype(bf16) for k in range(4)], axis=0)
    first = dot(lhs, t1_ref[...])
    first = jnp.maximum(first[:, :512], first[:, 512:])
    first = jnp.concatenate(
        [jnp.maximum(first[k * 128 : k * 128 + 64], first[k * 128 + 64 : k * 128 + 128]) for k in range(4)],
        axis=0,
    )
    first = jnp.maximum(first + b1, 0.0)
    even = jnp.concatenate([first[k * 64 : k * 64 + 32] for k in range(4)], axis=0)
    odd = jnp.concatenate([first[k * 64 + 32 : k * 64 + 64] for k in range(4)], axis=0)
    odd_before = rows_beside(odd)[0]
    even_after = rows_beside(even)[1]
    layers = [v.astype(bf16) for v in (odd_before, even, odd, even_after)]
    lhs = jnp.concatenate(windows(layers[0:3], 4) + windows(layers[1:4], 4), axis=0)
    second = dot(lhs, t2_ref[...])
    second = jnp.maximum(second[:, :128], second[:, 128:])
    second = jnp.maximum(second[:512], second[512:])
    second = jnp.maximum(second + b2, 0.0)
    second = jnp.concatenate([second[t * 128 : (t + 1) * 128] for t in range(4)], axis=1)
    before, after = rows_beside(second)
    lhs = jnp.concatenate(windows([v.astype(bf16) for v in (before, second, after)], 4), axis=0)
    third = jnp.maximum(dot(lhs, t3_ref[...]) + b3, 0.0).astype(bf16)
    score = lax.dot_general(
        third, weight, (((1,), (1,)), ((), ())), preferred_element_type=jnp.float32
    )
    score = jnp.maximum(
        jnp.maximum(score[0:128], score[128:256]), jnp.maximum(score[256:384], score[384:512])
    )
    score = jnp.max(score, axis=1, keepdims=True) + jnp.broadcast_to(bias_ref[0], (1, 128))
    score = score.reshape(16, 8, score.shape[1]).sum(axis=1) * 0.125
    listed = listed_ref[...]
    slot_query = lax.broadcasted_iota(jnp.int32, (1, listed.shape[1]), 1) % 4
    total = jnp.zeros(listed.shape, jnp.float32)
    for k in range(4):
        line = jnp.zeros((1, listed.shape[1]), jnp.float32)
        for q in range(4):
            line = jnp.where(slot_query == q, score[k * 4 + q : k * 4 + q + 1, : listed.shape[1]], line)
        total = jnp.where(listed == k, line, total)
    out_ref[:, 0, :] = total[:, :4]
    out_ref[:, 1, :] = total[:, 4:]


def slot_scores(parts, listed, spread, first_bias, second_bias, third_bias, score_weight, score_bias):
    operands = [
        score_bias,
        parts,
        jnp.asarray(row_order(), jnp.bfloat16),
        spread[0],
        first_bias[None, :],
        spread[1],
        second_bias[None, :],
        spread[2],
        third_bias[None, :],
        score_weight[None, :],
        listed,
    ]
    outs = [((listed.shape[0], 2, listed.shape[1] // 2), jnp.float32)]
    return kernel_call(score_body, outs, operands, [], 2 * 10**9, scalars=1)[0]


def on_device(
    queries,
    corpus,
    cand_shard,
    cand_clip,
    cand_count,
    first_kernel,
    first_bias,
    second_kernel,
    second_bias,
    third_kernel,
    third_bias,
    score_weight,
    score_bias,
):
    at = jnp.stack([lax.axis_index(a) for a in ("z", "y", "c", "x")]).astype(jnp.int32)
    clip_dev, frames, regions, width = corpus.shape
    group = cand_shard.shape[0] // NX

    own = corpus.transpose(0, 2, 1, 3).reshape(clip_dev, regions * frames, width)
    four = gather_classes(queries[0, 0])
    ahead = near_shift(four, -1)
    two = near_shift(four, 2)
    behind = near_shift(four, 1)
    kernels = (first_kernel, second_kernel, third_kernel)
    kernels, two = lax.optimization_barrier((kernels, two))
    listed, place, *spread = prepare(at, cand_count, cand_shard, cand_clip, *kernels)
    first = jnp.concatenate([four, two], axis=1)
    last = jnp.concatenate([behind, ahead], axis=1)
    own, listed, first, last = lax.optimization_barrier((own, listed, first, last))
    other = lax.ppermute(own, "c", [(0, 1), (1, 0)])
    behind_first = shift(first, 1)
    ahead_first = shift(first, -1)
    two_first = shift(behind_first, 1)
    behind_last = shift(last, 1)
    ahead_last = shift(last, -1)
    two_last = shift(behind_last, 1)

    near = [first, last, behind_first, behind_last, ahead_first, ahead_last]
    prev = frame_sims(own, other, near)
    two, prev = lax.optimization_barrier(((two_first, two_last), prev))
    table = frame_table(own, other, prev, place, two)

    parts = lax.all_to_all(table, ("c", "x"), 0, 0, tiled=True)
    values = slot_scores(
        parts, listed, spread, first_bias, second_bias, third_bias, score_weight, score_bias
    )
    values = lax.all_to_all(values, ("z", "y"), 0, 0, tiled=True)
    return values.sum(axis=0).T


def solution(mesh):
    devices = mesh.devices.reshape(NZ, NY, NC, NX)
    grid = Mesh(devices, ("z", "y", "c", "x"))
    return jax.shard_map(
        on_device,
        mesh=grid,
        in_specs=(P("x", PLANE), P(PLANE)) + (P(),) * 11,
        out_specs=P("x", PLANE),
        check_vma=False,
    )
```
